128 devices in a mesh: pipe: 4 (over x_hi, core), expert: 32 (over x_lo, y, z).
Axes of the slice: x: 4 (x_hi: 2, x_lo: 2; x = x_hi * 2 + x_lo), y: 4, z: 4, core: 2. Of those that a mesh axis runs over, the one named last changes fastest.
Arguments:
- tokens: bfloat16 [4096, 7168], P('expert'), may hold values from -6 to 6
- cotangent: bfloat16 [4096, 7168], P('expert'), may hold values from -6 to 6
- norm_gain: float32 [7168], replicated, may hold values from 0.1 to 1.9
- expert_ids: int32 [4096, 2], P('expert'), may hold values from 0 to 31, all different within a row; in each aligned block of 128 rows (0 to 127, 128 to 255, ...) at most 12 rows name the same one
- gate_weights: float32 [4096, 2], P('expert'), may hold values from 0.1 to 1
- w_gate: bfloat16 [32, 7168, 2048], P('expert', None, 'pipe'), may hold values from -0.0625 to 0.0625
- w_up: bfloat16 [32, 7168, 2048], P('expert', None, 'pipe'), may hold values from -0.0625 to 0.0625
- w_down: bfloat16 [32, 2048, 7168], P('expert', 'pipe'), may hold values from -0.125 to 0.125
Outputs:
- input_grad: bfloat16 [4096, 7168], P('expert', 'pipe')
The draws below stay inside these ranges and needn't reach their ends.
Inputs may be any that keep to these rules, and one draw needn't show every extreme that they name: `expert_ids`: each row names 2 different experts. Among the rows of one device no expert is named by more than 12 rows, and in some devices' rows one expert is named by exactly 12.
All inputs are finite; a program needn't handle non-finite values.
Results may differ from the reference program's by a relative error of at most 0.0054.
Values may be sent and summed in bfloat16 or wider, within the bound.
No kernel may reach another device: no remote copies, remote signals or barrier semaphores. Data moves between devices by JAX's collectives and lax.ppermute only.
A program may use at most 128 MiB of HBM per device.

```python
import math
import jax
import jax.numpy as jnp
import numpy as np
from jax import lax

D = 7168
FF = 2048
TOP = 2
TOK_DEV = 128
EXPERTS = 32
CAP = 12
TOKENS = 4096
N_EXPERT = 32


def with_spikes(entries, own_key, source, target, parts, factor):
    def block_of(axis_at):
        return (jnp.arange(entries.shape[axis_at]) // (entries.shape[axis_at] // parts)).reshape((-1,) + (1,) * (entries.ndim - 1 - axis_at))

    one_side = jax.random.permutation(own_key, parts)[block_of(target)]
    second = (block_of(target) + parts // 2) % parts
    return jnp.where((block_of(source) == one_side) | (block_of(source) == second), factor * entries, entries)


def shard_levels(stream_key, dims, pieces, smallest, largest):
    def one(dim, parts):
        heights = jax.random.uniform(jax.random.fold_in(jax.random.fold_in(stream_key, 6), dim), (parts,), jnp.float32, smallest / len(pieces), largest / len(pieces))
        return jnp.repeat(jnp.exp(heights), dims[dim] // parts).reshape((-1,) + (1,) * (len(dims) - dim - 1))

    loudness = one(*pieces[0])
    for cut in pieces[1:]:
        loudness = loudness * one(*cut)
    return loudness


def routed_block(rng, own, number, rows, amount, top, reach, lean):
    order = jax.random.permutation(rng, amount)
    crowded, common = shares(amount, rows * top, reach, lean, True), shares(amount, rows * top, reach, lean, False)
    places = jnp.arange(amount)

    def named(tallies, offset_by):
        used = int((tallies > 0).sum())
        fixed = max(1, used // 4)
        moved = fixed + (places - fixed + offset_by * (used - fixed)) % max(1, amount - fixed)
        return jnp.zeros((amount,), jnp.int32).at[order[jnp.where(places < fixed, places, moved)]].set(jnp.asarray(tallies, jnp.int32))

    tallies = jnp.where(number % 4 == 0, named(crowded, number // 4), named(common, number - number // 4 - 1))
    mixed = jax.random.permutation(jax.random.fold_in(own, 3), amount)
    source_of, receiver = mixed[0:amount // 2 * 2:2], mixed[1:amount // 2 * 2:2]
    margin = jnp.minimum(tallies[source_of] - 1, reach - tallies[receiver]) // 2
    margin = jnp.where((source_of == order[0]) | (receiver == order[0]) | (tallies[receiver] == 0), 0, jnp.maximum(margin, 0))
    moved = jax.random.randint(jax.random.fold_in(own, 4), (amount // 2,), 0, 1 << 20) % (margin + 1)
    tallies = tallies.at[source_of].add(-moved).at[receiver].add(moved)
    members = jnp.searchsorted(jnp.cumsum(tallies), jnp.arange(rows * top), side="right").astype(jnp.int32)
    grid = members.reshape(top, rows).T
    grid = grid[jax.random.permutation(jax.random.fold_in(own, 1), rows)]
    offset_by = jax.random.randint(jax.random.fold_in(own, 2), (rows, 1), 0, top)
    return jnp.take_along_axis(grid, (jnp.arange(top)[None, :] + offset_by) % top, axis=1)


def shares(number_of, total, bound, skew, full):
    weights = [(1 << 20) // math.isqrt(rank ** skew) + 1 for rank in range(1, number_of + 1)]
    largest = bound if full else min(bound, max(-(-total // number_of), total * weights[0] // sum(weights)))
    least = 1 if total - largest >= number_of - 1 else 0
    given, surplus = [largest] + [least] * (number_of - 1), total - largest - least * (number_of - 1)
    while surplus > 0:
        movable = [i for i in range(1, number_of) if given[i] < largest] or [i for i in range(1, number_of) if given[i] < bound]
        pool, left = sum([weights[i] for i in movable]), surplus
        for i in movable:
            more = min(bound - given[i], max(1, left * weights[i] // pool), surplus)
            given[i] = given[i] + more
            surplus = surplus - more
    return np.array(given)


def gaussian(rng, shape, spread, reach, pieces=(), held_as=jnp.bfloat16):
    level = shard_levels(rng, shape, pieces, -0.22, 0.18) if pieces else 1.0
    values = jax.random.normal(rng, shape, jnp.float32) * spread * level
    return jnp.minimum(jnp.maximum(values, -reach), reach).astype(held_as)


def bell_draw_with(stream_key, dims, deviation, bound, pieces, heavy, kind=jnp.bfloat16):
    values = deviation * jax.random.normal(stream_key, dims, jnp.float32)
    if pieces:
        values = values * shard_levels(stream_key, dims, pieces, -0.22, 0.18)
    return jnp.clip(with_spikes(values, jax.random.fold_in(stream_key, 3), *heavy), -bound, bound).astype(kind)


def setup_inputs(seed: int = 0) -> dict:
    key_of = jax.random.split(jax.random.key(seed), 9)
    tokens = bell_draw_with(key_of[0], (TOKENS, D), 1.0, 6.0, ((0, 32),), (0, 1, 32, 2.75))
    cotangent = gaussian(key_of[1], (TOKENS, D), 1.0, 6.0, ((0, 32),))
    norm_gain = jnp.clip(1.0 + 0.18 * jax.random.normal(key_of[2], (D,), jnp.float32), 0.1, 1.9)
    expert_ids_keys = jax.random.split(jax.random.fold_in(key_of[3], 1), TOKENS // TOK_DEV)
    expert_ids_turns = jax.random.permutation(jax.random.fold_in(key_of[3], 3), TOKENS // TOK_DEV)
    expert_ids = jax.vmap(lambda own, number: routed_block(jax.random.fold_in(key_of[3], 2), own, number, TOK_DEV, N_EXPERT, TOP, CAP, 2))(expert_ids_keys, expert_ids_turns).reshape((TOKENS, TOP))
    gate_weights = jnp.clip(jnp.exp(math.log(1.0) - 2.3025851 * jax.random.uniform(key_of[4], (TOKENS, TOP), jnp.float32) ** shard_levels(key_of[4], (TOKENS, TOP), ((0, 32),), -0.2, 0.2)), 0.1, 1.0)
    w_gate = gaussian(key_of[5], (EXPERTS, D, FF), D ** -0.5, 0.0625, ((0, 32), (2, 4)))
    w_up = gaussian(key_of[6], (EXPERTS, D, FF), D ** -0.5, 0.0625, ((0, 32), (2, 4)))
    w_down = gaussian(key_of[7], (EXPERTS, FF, D), FF ** -0.5, 0.125, ((0, 32), (1, 4)))
    return {"tokens": tokens, "cotangent": cotangent, "norm_gain": norm_gain, "expert_ids": expert_ids, "gate_weights": gate_weights, "w_gate": w_gate, "w_up": w_up, "w_down": w_down}


EPSILON = 1e-06

def slot_layout(block_ids, experts, capacity):
    pairs = block_ids.reshape(-1).astype(jnp.int32)
    count = pairs.shape[0]
    onehot = (pairs[:, None] == jnp.arange(experts, dtype=jnp.int32)[None, :]).astype(jnp.int32)
    earlier = jnp.cumsum(onehot, axis=0) - onehot
    rank_in = lax.optimization_barrier(jnp.sum(earlier * onehot, axis=1))
    slot_of = (pairs * capacity + rank_in).astype(jnp.int32)
    matches = (slot_of[None, :] == jnp.arange(experts * capacity, dtype=jnp.int32)[:, None]).astype(jnp.int32)
    source_pair = lax.optimization_barrier(jnp.sum(matches * jnp.arange(count, dtype=jnp.int32)[None, :], axis=1)).astype(jnp.int32)
    filled = lax.optimization_barrier(jnp.sum(matches, axis=1))
    return (slot_of, source_pair, filled)

def expert_backward(normed_rows, routed_rows, gate_mat, up_mat, down_mat):
    pre_gate = jnp.dot(normed_rows, gate_mat, preferred_element_type=jnp.float32)
    pre_up = jnp.dot(normed_rows, up_mat, preferred_element_type=jnp.float32)
    contract = (((1,), (1,)), ((), ()))
    hidden_grad = lax.dot_general(routed_rows, down_mat, contract, preferred_element_type=jnp.float32)
    sigma = jax.nn.sigmoid(pre_gate)
    grad_gate = (hidden_grad * pre_up * sigma * (1.0 + pre_gate * (1.0 - sigma))).astype(jnp.bfloat16)
    grad_up = (hidden_grad * pre_gate * sigma).astype(jnp.bfloat16)
    back = lax.dot_general(grad_gate, gate_mat, contract, preferred_element_type=jnp.float32)
    return back + lax.dot_general(grad_up, up_mat, contract, preferred_element_type=jnp.float32)

def reference(tokens, cotangent, norm_gain, expert_ids, gate_weights, w_gate, w_up, w_down):
    width = tokens.shape[1]
    values = tokens.astype(jnp.float32)
    inverse = lax.rsqrt(lax.optimization_barrier(jnp.mean(values * values, axis=1, keepdims=True)) + EPSILON)
    gain = norm_gain.astype(jnp.float32)
    normed = (values * inverse * gain).astype(jnp.bfloat16)
    routed = (gate_weights.astype(jnp.float32)[:, :, None] * cotangent.astype(jnp.float32)[:, None, :]).astype(jnp.bfloat16)
    routed = routed.reshape(TOKENS * TOP, width)
    blocks = expert_ids.reshape(N_EXPERT, TOK_DEV, TOP)
    slot_of, source_pair, filled = jax.vmap(lambda block: slot_layout(block, EXPERTS, CAP))(blocks)
    offsets = (jnp.arange(N_EXPERT, dtype=jnp.int32) * (TOK_DEV * TOP))[:, None]
    global_pair = (source_pair + offsets).reshape(N_EXPERT, EXPERTS, CAP).transpose(1, 0, 2).reshape(EXPERTS, N_EXPERT * CAP)
    live = filled.reshape(N_EXPERT, EXPERTS, CAP).transpose(1, 0, 2).reshape(EXPERTS, N_EXPERT * CAP)

    def one_expert(index):
        pair_rows = global_pair[index]
        mask = live[index].astype(jnp.bfloat16)[:, None]
        normed_rows = jnp.take(normed, pair_rows // TOP, axis=0) * mask
        routed_rows = jnp.take(routed, pair_rows, axis=0) * mask
        return expert_backward(normed_rows, routed_rows, w_gate[index], w_up[index], w_down[index])
    returned = lax.map(one_expert, jnp.arange(EXPERTS, dtype=jnp.int32))
    per_source = returned.reshape(EXPERTS, N_EXPERT, CAP, width).transpose(1, 0, 2, 3).reshape(N_EXPERT, EXPERTS * CAP, width)
    pair_grads = jax.vmap(lambda rows, slots: jnp.take(rows, slots, axis=0))(per_source, slot_of)
    normed_grad = pair_grads.reshape(TOKENS, TOP, width).sum(axis=1)
    row_product = lax.optimization_barrier(jnp.sum(normed_grad * gain * values, axis=1, keepdims=True))
    cubed = inverse * inverse * inverse
    input_grad = (cotangent.astype(jnp.float32) + inverse * gain * normed_grad - values * cubed * row_product / width).astype(jnp.bfloat16)
    return input_grad
```

```python
import functools

import jax
import jax.numpy as jnp
from jax import lax
from jax.experimental import pallas as pl
from jax.experimental.pallas import tpu as pltpu
from jax.sharding import PartitionSpec as P

EPSILON = 1e-06
BF16 = jnp.bfloat16
F32 = jnp.float32
VMEM_LIMIT = 48 * 1024 * 1024
FILL = 512
DEPTH = 1792
BACK = 896
LANES = 128
LAST = (((1,), (1,)), ((), ()))
CORE_SWAP = [(0, 1), (1, 0), (2, 3), (3, 2)]


def params():
    return pltpu.CompilerParams(vmem_limit_bytes=VMEM_LIMIT)


def whole(shape):
    return pl.BlockSpec(shape, lambda *_: (0,) * len(shape))


def grid_of(grid, in_specs, out_specs, scratch=()):
    return pltpu.PrefetchScalarGridSpec(
        num_scalar_prefetch=1, grid=grid, in_specs=in_specs, out_specs=out_specs, scratch_shapes=scratch
    )


def same_plane(group):
    return [[x * group + k for k in range(group)] for x in range(lax.axis_size("expert") // group)]


def ring_permute(array, steps):
    plane = lax.axis_size("expert") // 2
    moves = []
    for x in range(4):
        for core in range(2):
            to = (x + steps[core]) % 4
            for k in range(plane):
                source = (2 * (x // 2) + core) * 2 * plane + (x % 2) * plane + k
                target = (2 * (to // 2) + core) * 2 * plane + (to % 2) * plane + k
                moves.append((source, target))
    return lax.ppermute(array, ("pipe", "expert"), moves)


def core_swap(array):
    return lax.ppermute(array, "pipe", CORE_SWAP)


def plane_exchange(rows):
    plane = lax.axis_size("expert") // 2
    shaped = rows.reshape(plane, rows.shape[0] // plane, rows.shape[1])
    out = lax.all_to_all(
        shaped, "expert", split_axis=0, concat_axis=0, tiled=True, axis_index_groups=same_plane(plane)
    )
    return out.reshape(rows.shape)


def message_kernel(capacity, other, first, place, *refs):
    tokens, cotangent, gain, ids, weights = refs[:5]
    if first:
        all_tokens, rows, inverse, select = refs[5:]
    else:
        inverse, rows, select = refs[5:]
    top, count = ids.shape

    @pl.when(pl.program_id(0) == 0)
    def _():
        height = select.shape[0]
        plane = height // (2 * capacity)
        expert_of = lax.broadcasted_iota(jnp.int32, (2 * plane, count), 0)
        earlier_of = lax.broadcasted_iota(jnp.int32, (count, count), 0)
        later_of = lax.broadcasted_iota(jnp.int32, (count, count), 1)
        before = (earlier_of < later_of).astype(F32).astype(BF16)
        row = lax.broadcasted_iota(jnp.int32, (height, count), 0)
        taken = jnp.zeros((2 * plane, 1), F32)
        normed_part = jnp.zeros(row.shape, F32)
        base = plane * (1 - place[1] if other else place[1])
        for k in range(top):
            expert = ids[k : k + 1, :]
            named = (expert_of == expert).astype(F32)
            earlier = jnp.dot(named.astype(BF16), before, preferred_element_type=F32) + taken
            rank = jnp.sum(earlier * named, axis=0, keepdims=True).astype(jnp.int32)
            taken = taken + jnp.sum(named, axis=1, keepdims=True)
            local = expert - base
            at = jnp.where((local >= 0) & (local < plane), local * (2 * capacity) + rank, -2 * capacity)
            normed_part = normed_part + (row == at).astype(F32)
            select[:, (k + 1) * count : (k + 2) * count] = (row == at + capacity).astype(F32).astype(BF16)
        select[:, :count] = normed_part.astype(BF16)
        if first:
            values = all_tokens[...].astype(F32)
            inverse[...] = lax.rsqrt(jnp.mean(values * values, axis=1, keepdims=True) + EPSILON)

    normed = (tokens[...].astype(F32) * inverse[...] * gain[...]).astype(BF16)
    values = cotangent[...].astype(F32)
    parts = [normed] + [(weights[:, k : k + 1] * values).astype(BF16) for k in range(top)]
    rows[...] = jnp.dot(select[...], jnp.concatenate(parts, axis=0), preferred_element_type=F32).astype(BF16)


def make_message(place, tokens, cotangent, gain, ids, weights, inverse, capacity, plane, other):
    count, width = tokens.shape
    half = width // 2
    height = plane * 2 * capacity
    steps = half // FILL
    first = inverse is None
    column = lambda i, place: (0, place[0] * steps + i)
    split = [pl.BlockSpec((count, FILL), column), pl.BlockSpec((count, FILL), column), pl.BlockSpec((1, FILL), column)]
    last = (count, width) if first else (count, 1)
    message = jax.ShapeDtypeStruct((height, half), BF16)
    message_spec = pl.BlockSpec((height, FILL), lambda i, place: (0, i))
    out = pl.pallas_call(
        functools.partial(message_kernel, capacity, other, first),
        out_shape=(message, jax.ShapeDtypeStruct((count, 1), F32)) if first else message,
        grid_spec=grid_of(
            (steps,),
            split + [whole(ids.shape), whole(weights.shape), whole(last)],
            (message_spec, whole((count, 1))) if first else message_spec,
            [pltpu.VMEM((height, 3 * count), BF16)],
        ),
        compiler_params=params(),
        name="message",
    )(place, tokens, cotangent, gain, ids, weights, tokens if first else inverse)
    return out


def gather_kernel(capacity, place, ids, out):
    count, top = ids.shape
    rows = out.shape[1]
    plane = rows // (2 * capacity)
    expert_of = lax.broadcasted_iota(jnp.int32, (count, 2 * plane), 1)
    later_of = lax.broadcasted_iota(jnp.int32, (count, count), 0)
    earlier_of = lax.broadcasted_iota(jnp.int32, (count, count), 1)
    before = (earlier_of < later_of).astype(F32).astype(BF16)
    row = lax.broadcasted_iota(jnp.int32, (count, rows), 1)
    taken = jnp.zeros((1, 2 * plane), F32)
    first = jnp.zeros(row.shape, F32)
    second = jnp.zeros(row.shape, F32)
    for k in range(top):
        expert = ids[:, k : k + 1]
        named = (expert_of == expert).astype(F32)
        earlier = jnp.dot(before, named.astype(BF16), preferred_element_type=F32) + taken
        rank = jnp.sum(earlier * named, axis=1, keepdims=True).astype(jnp.int32)
        taken = taken + jnp.sum(named, axis=0, keepdims=True)
        local = expert - place[1] * plane
        at = jnp.where((local >= 0) & (local < plane), local * (2 * capacity) + rank, -2 * capacity)
        first = first + (row == at).astype(F32)
        second = second + (row == at + capacity).astype(F32)
    out[:count, :] = first.astype(BF16)
    out[count:, :] = second.astype(BF16)


def gather_matrix(place, ids, capacity, plane):
    count = ids.shape[0]
    rows = plane * 2 * capacity
    return pl.pallas_call(
        functools.partial(gather_kernel, capacity),
        out_shape=jax.ShapeDtypeStruct((2 * count, rows), BF16),
        grid_spec=grid_of((1,), [whole(ids.shape)], whole((2 * count, rows))),
        compiler_params=params(),
        name="gather_matrix",
    )(place, ids)


def tiles(x, group):
    return x.reshape(x.shape[0] // (8 * group), group, 8, x.shape[1])


def upper(shape):
    return lax.broadcasted_iota(jnp.int32, shape, 1) < 4


def compact(x):
    rows, columns = x.shape
    a, b = tiles(x, 6), tiles(pltpu.roll(x, 4, 0), 6)
    shape = (rows // 48, 8, columns)
    parts = [a[:, 0], jnp.where(upper(shape), a[:, 1], b[:, 3]), b[:, 4]]
    return jnp.concatenate([p[:, None] for p in parts], axis=1).reshape(rows // 2, columns)


def interleave(x, y):
    rows, columns = x.shape
    x0, x1, x2 = tiles(x, 3), tiles(pltpu.roll(x, 4, 0), 3), tiles(pltpu.roll(x, rows - 4, 0), 3)
    y0, y1 = tiles(y, 3), tiles(pltpu.roll(y, 4, 0), 3)
    shape = (rows // 24, 8, columns)
    parts = [
        x0[:, 0],
        jnp.where(upper(shape), x0[:, 1], y1[:, 0]),
        y1[:, 1],
        x1[:, 2],
        jnp.where(upper(shape), x2[:, 2], y0[:, 1]),
        y0[:, 2],
    ]
    return jnp.concatenate([p[:, None] for p in parts], axis=1).reshape(2 * rows, columns)


def project_kernel(capacity, blocks, first, last, place, *refs):
    own, other, gate, up, down = refs[:5]
    rest = list(refs[5:])
    previous = [] if first else [rest.pop(0) for _ in range(3)]
    outs = [rest.pop(0) for _ in range(3)]
    accs = rest if last else outs
    step = pl.program_id(0)

    @pl.when(step == 0)
    def _():
        for number, acc in enumerate(accs):
            acc[...] = jnp.zeros_like(acc) if first else previous[number][...]

    def add(rows):
        x = rows[...]
        accs[0][...] += jnp.dot(x, gate[...], preferred_element_type=F32)
        accs[1][...] += jnp.dot(x, up[...], preferred_element_type=F32)
        accs[2][...] += lax.dot_general(x, down[...], LAST, preferred_element_type=F32)

    @pl.when(step < blocks)
    def _():
        add(own)

    @pl.when(step >= blocks)
    def _():
        add(other)

    if last:

        @pl.when(step == 2 * blocks - 1)
        def _():
            rows = accs[2].shape[0]
            pre_gate = compact(accs[0][...])
            pre_up = compact(accs[1][...])
            hidden = compact(pltpu.roll(accs[2][...], rows - capacity, 0))
            sigma = jax.nn.sigmoid(pre_gate)
            grad_gate = hidden * pre_up * sigma * (1.0 + pre_gate * (1.0 - sigma))
            grad_up = hidden * pre_gate * sigma
            outs[0][...] = grad_gate.astype(BF16)
            outs[1][...] = grad_up.astype(BF16)
            product = jnp.sum(grad_gate * pre_gate + grad_up * pre_up, axis=1, keepdims=True)
            outs[2][...] = jnp.broadcast_to(product, outs[2].shape)


def project(place, own, other, weights, at, previous, last, capacity):
    gate, up, down = weights
    rows, columns = own.shape
    width, hidden = gate.shape
    blocks = columns // DEPTH if columns % DEPTH == 0 else columns // 256
    depth = columns // blocks
    per_half = width // 2 // depth
    start = at // depth

    def at_block(i, place):
        side = jnp.where(i < blocks, place[0], 1 - place[0])
        return side * per_half + start + lax.rem(i, blocks)

    acc = jax.ShapeDtypeStruct((rows, hidden), F32)
    grad = jax.ShapeDtypeStruct((rows // 2, hidden), BF16)
    product = jax.ShapeDtypeStruct((rows // 2, LANES), F32)
    outs = (grad, grad, product) if last else (acc,) * 3
    return pl.pallas_call(
        functools.partial(project_kernel, capacity, blocks, not previous, last),
        out_shape=outs,
        grid_spec=grid_of(
            (2 * blocks,),
            [
                pl.BlockSpec((rows, depth), lambda i, place: (0, jnp.minimum(i, blocks - 1))),
                pl.BlockSpec((rows, depth), lambda i, place: (0, jnp.maximum(i - blocks, 0))),
                pl.BlockSpec((depth, hidden), lambda i, place: (at_block(i, place), 0)),
                pl.BlockSpec((depth, hidden), lambda i, place: (at_block(i, place), 0)),
                pl.BlockSpec((hidden, depth), lambda i, place: (0, at_block(i, place))),
            ]
            + [whole((rows, hidden))] * len(previous),
            tuple(whole(o.shape) for o in outs),
            [pltpu.VMEM((rows, hidden), F32)] * 3 if last else [],
        ),
        compiler_params=params(),
        name="project",
    )(place, own, other, gate, up, down, *previous)


def back_kernel(place, *refs):
    grad_gate, grad_up, product, gate_0, gate_1, up_0, up_1 = refs[:7]
    out = refs[-1]
    other = refs[7] if len(refs) == 9 else None
    columns = out.shape[1] - LANES

    def one(gate, up):
        total = lax.dot_general(grad_gate[...], gate[...], LAST, preferred_element_type=F32)
        return total + lax.dot_general(grad_up[...], up[...], LAST, preferred_element_type=F32)

    def put(rows, at):
        if other is not None:
            rows = rows + other[:, at].astype(F32)
        out[:, at] = rows.astype(BF16)

    step = pl.program_id(0)
    put(interleave(one(gate_0, up_0), one(gate_1, up_1)), pl.ds(pl.multiple_of(step * BACK, LANES), BACK))

    @pl.when(step == 0)
    def _():
        put(interleave(product[...], product[...]), pl.ds(columns, LANES))


def back(place, grads, weights, other):
    gate, up, _ = weights
    rows, hidden = grads[0].shape
    columns = gate.shape[0] // 4
    steps = columns // BACK

    def quarter(high):
        def index(i, place):
            side = 1 - place[0] if other is None else place[0]
            return ((2 * high + side) * steps + i, 0)

        return pl.BlockSpec((BACK, hidden), index)

    shape = (2 * rows, columns + LANES)
    extra = [] if other is None else [other]
    return pl.pallas_call(
        back_kernel,
        out_shape=jax.ShapeDtypeStruct(shape, BF16),
        grid_spec=grid_of(
            (steps,),
            [whole(g.shape) for g in grads]
            + [quarter(0), quarter(1), quarter(0), quarter(1)]
            + [whole(shape)] * len(extra),
            whole(shape),
        ),
        compiler_params=params(),
        name="back",
    )(place, *grads, gate, gate, up, up, *extra)


def combine_kernel(place, gather, rows, first, second):
    count = first.shape[0]
    total = jnp.dot(gather[...], rows[...], preferred_element_type=F32)
    low, high = total[:count], total[count:]
    flip = place[2] == 1
    first[...] = jnp.where(flip, high, low).astype(first.dtype)
    second[...] = jnp.where(flip, low, high).astype(second.dtype)


def combine(place, gather, rows, first_type):
    count = gather.shape[0] // 2
    columns = rows.shape[1]
    part = columns // 3
    block = pl.BlockSpec((count, part), lambda i, place: (0, i))
    return pl.pallas_call(
        combine_kernel,
        out_shape=(
            jax.ShapeDtypeStruct((count, columns), first_type),
            jax.ShapeDtypeStruct((count, columns), BF16),
        ),
        grid_spec=grid_of(
            (3,),
            [whole(gather.shape), pl.BlockSpec((rows.shape[0], part), lambda i, place: (0, i))],
            (block, block),
        ),
        compiler_params=params(),
        name="combine",
    )(place, gather, rows)


def body(tokens, cotangent, norm_gain, expert_ids, gate_weights, w_gate, w_up, w_down):
    experts = lax.axis_size("expert")
    plane = experts // 2
    token_count, width = tokens.shape
    top_count = expert_ids.shape[1]
    capacity = token_count * top_count * 3 // (2 * experts)
    columns = width // lax.axis_size("pipe")
    pipe = lax.axis_index("pipe")
    core, high = lax.rem(pipe, 2), pipe // 2
    low = lax.axis_index("expert") // plane
    after = lax.rem(2 * high + low + 1, 4) // 2
    place = jnp.stack([core, low, high]).astype(jnp.int32)
    place_after = jnp.stack([core, low, after]).astype(jnp.int32)
    weights = (w_gate[0], w_up[0], w_down[0])

    gain = norm_gain.reshape(1, width)
    make = functools.partial(
        make_message, place, tokens, cotangent, gain, expert_ids.T, gate_weights, capacity=capacity, plane=plane
    )
    other, inverse = make(inverse=None, other=True)
    own = make(inverse=inverse, other=False)
    other_ids = lax.ppermute(expert_ids, "expert", [(k, (k + plane) % experts) for k in range(experts)])
    gathers = [gather_matrix(place, ids, capacity, plane) for ids in (expert_ids, other_ids)]

    other = ring_permute(other, (1, 3))
    own = plane_exchange(own)
    other = plane_exchange(other)

    grads = project(place, own, core_swap(own), weights, 0, (), True, capacity)
    theirs = core_swap(back(place, grads, weights, None))
    mine = back(place, grads, weights, theirs)

    mine, other = lax.optimization_barrier((mine, other))
    own_back = plane_exchange(mine)
    grads = project(place, other, core_swap(other), weights, 0, (), True, capacity)
    theirs = core_swap(back(place, grads, weights, None))
    mine = back(place, grads, weights, theirs)
    other_back = plane_exchange(mine)

    kept, sent = combine(place, gathers[0], own_back, F32)
    from_far = ring_permute(sent, (2, 2))
    forth, back_ = combine(place_after, gathers[1], other_back, BF16)
    from_before = ring_permute(forth, (1, 1))
    from_after = ring_permute(back_, (3, 3))

    def own_columns(array):
        return lax.dynamic_slice_in_dim(array, pipe * columns, columns, array.ndim - 1)

    total = kept + from_far.astype(F32) + from_before.astype(F32) + from_after.astype(F32)
    normed_grad, product = total[:, :columns], total[:, columns : columns + 1]
    value_part = own_columns(tokens).astype(F32)
    cotangent_part = own_columns(cotangent).astype(F32)
    return (
        cotangent_part
        + inverse * own_columns(norm_gain) * normed_grad
        - value_part * (inverse * inverse * product / width)
    ).astype(BF16)


def solution(mesh):
    in_specs = (
        P("expert", None),
        P("expert", None),
        P(),
        P("expert", None),
        P("expert", None),
        P("expert", None, "pipe"),
        P("expert", None, "pipe"),
        P("expert", "pipe", None),
    )
    out_specs = P("expert", "pipe")
    return jax.shard_map(body, mesh=mesh, in_specs=in_specs, out_specs=out_specs, check_vma=False)
```

```python
import functools

import jax
import jax.numpy as jnp
from jax import lax
from jax.experimental import pallas as pl
from jax.experimental.pallas import tpu as pltpu
from jax.sharding import PartitionSpec as P

EPSILON = 1e-06
BF16 = jnp.bfloat16
F32 = jnp.float32
MIB = 1024 * 1024
FILL = 1792
DEPTH = 1792
AHEAD = 1
BACK = 896
LANES = 128
LAST = (((1,), (1,)), ((), ()))
CORE_SWAP = [(0, 1), (1, 0), (2, 3), (3, 2)]


def params(mebibytes):
    return pltpu.CompilerParams(vmem_limit_bytes=mebibytes * MIB)


def in_hbm(array):
    return pltpu.with_memory_space_constraint(array, pltpu.HBM)


def whole(shape):
    return pl.BlockSpec(shape, lambda *_: (0,) * len(shape))


def grid_of(grid, in_specs, out_specs, scratch=()):
    return pltpu.PrefetchScalarGridSpec(
        num_scalar_prefetch=1, grid=grid, in_specs=in_specs, out_specs=out_specs, scratch_shapes=scratch
    )


def same_plane(group):
    return [[x * group + k for k in range(group)] for x in range(lax.axis_size("expert") // group)]


def ring_permute(array, steps):
    plane = lax.axis_size("expert") // 2
    moves = []
    for x in range(4):
        for core in range(2):
            to = (x + steps[core]) % 4
            for k in range(plane):
                source = (2 * (x // 2) + core) * 2 * plane + (x % 2) * plane + k
                target = (2 * (to // 2) + core) * 2 * plane + (to % 2) * plane + k
                moves.append((source, target))
    return lax.ppermute(array, ("pipe", "expert"), moves)


def core_swap(array):
    return lax.ppermute(array, "pipe", CORE_SWAP)


def plane_exchange(rows):
    plane = lax.axis_size("expert") // 2
    shaped = rows.reshape(plane, rows.shape[0] // plane, rows.shape[1])
    out = lax.all_to_all(
        shaped, "expert", split_axis=0, concat_axis=0, tiled=True, axis_index_groups=same_plane(plane)
    )
    return out.reshape(rows.shape)


def message_kernel(capacity, other, first, place, *refs):
    tokens, cotangent, gain, ids, weights = refs[:5]
    if first:
        all_tokens, rows, inverse, select = refs[5:]
    else:
        inverse, rows, select = refs[5:]
    top, count = ids.shape

    @pl.when(pl.program_id(0) == 0)
    def _():
        height = select.shape[0]
        plane = height // (2 * capacity)
        expert_of = lax.broadcasted_iota(jnp.int32, (2 * plane, count), 0)
        earlier_of = lax.broadcasted_iota(jnp.int32, (count, count), 0)
        later_of = lax.broadcasted_iota(jnp.int32, (count, count), 1)
        before = (earlier_of < later_of).astype(F32).astype(BF16)
        row = lax.broadcasted_iota(jnp.int32, (height, count), 0)
        taken = jnp.zeros((2 * plane, 1), F32)
        normed_part = jnp.zeros(row.shape, F32)
        base = plane * (1 - place[1] if other else place[1])
        for k in range(top):
            expert = ids[k : k + 1, :]
            named = (expert_of == expert).astype(F32)
            earlier = jnp.dot(named.astype(BF16), before, preferred_element_type=F32) + taken
            rank = jnp.sum(earlier * named, axis=0, keepdims=True).astype(jnp.int32)
            taken = taken + jnp.sum(named, axis=1, keepdims=True)
            local = expert - base
            at = jnp.where((local >= 0) & (local < plane), local * (2 * capacity) + rank, -2 * capacity)
            normed_part = normed_part + (row == at).astype(F32)
            select[:, (k + 1) * count : (k + 2) * count] = (row == at + capacity).astype(F32).astype(BF16)
        select[:, :count] = normed_part.astype(BF16)
        if first:
            values = all_tokens[...].astype(F32)
            inverse[...] = lax.rsqrt(jnp.mean(values * values, axis=1, keepdims=True) + EPSILON)

    normed = (tokens[...].astype(F32) * inverse[...] * gain[...]).astype(BF16)
    values = cotangent[...].astype(F32)
    parts = [normed] + [(weights[:, k : k + 1] * values).astype(BF16) for k in range(top)]
    rows[...] = jnp.dot(select[...], jnp.concatenate(parts, axis=0), preferred_element_type=F32).astype(BF16)


def make_message(place, tokens, cotangent, gain, ids, weights, inverse, capacity, plane, other):
    count, width = tokens.shape
    half = width // 2
    height = plane * 2 * capacity
    steps = half // FILL
    first = inverse is None
    column = lambda i, place: (0, place[0] * steps + i)
    split = [pl.BlockSpec((count, FILL), column), pl.BlockSpec((count, FILL), column), pl.BlockSpec((1, FILL), column)]
    last = (count, width) if first else (count, 1)
    message = jax.ShapeDtypeStruct((height, half), BF16)
    message_spec = pl.BlockSpec((height, FILL), lambda i, place: (0, i))
    out = pl.pallas_call(
        functools.partial(message_kernel, capacity, other, first),
        out_shape=(message, jax.ShapeDtypeStruct((count, 1), F32)) if first else message,
        grid_spec=grid_of(
            (steps,),
            split + [whole(ids.shape), whole(weights.shape), whole(last)],
            (message_spec, whole((count, 1))) if first else message_spec,
            [pltpu.VMEM((height, 3 * count), BF16)],
        ),
        compiler_params=params(24),
        name="message",
    )(place, tokens, cotangent, gain, ids, weights, tokens if first else inverse)
    return out


def gather_kernel(capacity, place, ids, out):
    count, top = ids.shape
    rows = out.shape[1]
    plane = rows // (2 * capacity)
    expert_of = lax.broadcasted_iota(jnp.int32, (count, 2 * plane), 1)
    later_of = lax.broadcasted_iota(jnp.int32, (count, count), 0)
    earlier_of = lax.broadcasted_iota(jnp.int32, (count, count), 1)
    before = (earlier_of < later_of).astype(F32).astype(BF16)
    row = lax.broadcasted_iota(jnp.int32, (count, rows), 1)
    taken = jnp.zeros((1, 2 * plane), F32)
    first = jnp.zeros(row.shape, F32)
    second = jnp.zeros(row.shape, F32)
    for k in range(top):
        expert = ids[:, k : k + 1]
        named = (expert_of == expert).astype(F32)
        earlier = jnp.dot(before, named.astype(BF16), preferred_element_type=F32) + taken
        rank = jnp.sum(earlier * named, axis=1, keepdims=True).astype(jnp.int32)
        taken = taken + jnp.sum(named, axis=0, keepdims=True)
        local = expert - place[1] * plane
        at = jnp.where((local >= 0) & (local < plane), local * (2 * capacity) + rank, -2 * capacity)
        first = first + (row == at).astype(F32)
        second = second + (row == at + capacity).astype(F32)
    out[:count, :] = first.astype(BF16)
    out[count:, :] = second.astype(BF16)


def gather_matrix(place, ids, capacity, plane):
    count = ids.shape[0]
    rows = plane * 2 * capacity
    return pl.pallas_call(
        functools.partial(gather_kernel, capacity),
        out_shape=jax.ShapeDtypeStruct((2 * count, rows), BF16),
        grid_spec=grid_of((1,), [whole(ids.shape)], whole((2 * count, rows))),
        compiler_params=params(8),
        name="gather_matrix",
    )(place, ids)


def tiles(x, group):
    return x.reshape(x.shape[0] // (8 * group), group, 8, x.shape[1])


def upper(shape):
    return lax.broadcasted_iota(jnp.int32, shape, 1) < 4


def split_rows(x):
    rows, columns = x.shape
    x = x.astype(F32)
    a, b = tiles(x, 6), tiles(pltpu.roll(x, 4, 0), 6)
    top = upper((rows // 48, 8, columns))
    first = [a[:, 0], jnp.where(top, a[:, 1], b[:, 3]), b[:, 4]]
    second = [b[:, 2], jnp.where(top, b[:, 3], a[:, 4]), a[:, 5]]
    return [
        jnp.concatenate([p[:, None] for p in parts], axis=1).reshape(rows // 2, columns).astype(BF16)
        for parts in (first, second)
    ]


def interleave(x, y):
    rows, columns = x.shape
    x0, x1, x2 = tiles(x, 3), tiles(pltpu.roll(x, 4, 0), 3), tiles(pltpu.roll(x, rows - 4, 0), 3)
    y0, y1 = tiles(y, 3), tiles(pltpu.roll(y, 4, 0), 3)
    shape = (rows // 24, 8, columns)
    parts = [
        x0[:, 0],
        jnp.where(upper(shape), x0[:, 1], y1[:, 0]),
        y1[:, 1],
        x1[:, 2],
        jnp.where(upper(shape), x2[:, 2], y0[:, 1]),
        y0[:, 2],
    ]
    return jnp.concatenate([p[:, None] for p in parts], axis=1).reshape(2 * rows, columns)


def start_all(copies):
    for copy in copies:
        copy.start()


def wait_all(copies):
    for copy in copies:
        copy.wait()


def chunk_copies(side, half, rows, gate, up, down, rows_in, gate_in, up_in, down_in, gate_at, sems):
    copies = []
    for i in range(half // DEPTH):
        local = pl.ds(i * DEPTH, DEPTH)
        at = pl.ds(pl.multiple_of(side * half + i * DEPTH, DEPTH), DEPTH)
        to = pl.ds(pl.multiple_of(gate_at + i * DEPTH, DEPTH), DEPTH)
        copies.append(
            [
                pltpu.make_async_copy(rows.at[:, local], rows_in.at[:, local], sems.at[i, 0]),
                pltpu.make_async_copy(gate.at[at, :], gate_in.at[to, :], sems.at[i, 1]),
                pltpu.make_async_copy(up.at[at, :], up_in.at[to, :], sems.at[i, 2]),
                pltpu.make_async_copy(down.at[:, at], down_in.at[:, local], sems.at[i, 3]),
            ]
        )
    return copies


def project_half(copies, rows_in, gate_in, up_in, down_in, gate_at, accs, first, ahead):
    for i, copy in enumerate(copies):
        if i + AHEAD < len(copies):
            start_all(copies[i + AHEAD])
        elif ahead:
            start_all(ahead.pop(0))
        wait_all(copy)
        local = pl.ds(i * DEPTH, DEPTH)
        to = pl.ds(pl.multiple_of(gate_at + i * DEPTH, DEPTH), DEPTH)
        normed, routed = split_rows(rows_in[:, local])
        adds = (
            jnp.dot(normed, gate_in[to, :], preferred_element_type=F32),
            jnp.dot(normed, up_in[to, :], preferred_element_type=F32),
            lax.dot_general(routed, down_in[:, local], LAST, preferred_element_type=F32),
        )
        for acc, add in zip(accs, adds):
            acc[...] = add if first and i == 0 else acc[...] + add


def project_kernel(place, rows, gate, up, down, acc_gate, acc_up, acc_hidden, rows_in, gate_in, up_in, down_in, sems):
    half = rows.shape[1]
    copies = chunk_copies(place[0], half, rows, gate, up, down, rows_in, gate_in, up_in, down_in, 0, sems)
    for i in range(AHEAD):
        start_all(copies[i])
    project_half(copies, rows_in, gate_in, up_in, down_in, 0, (acc_gate, acc_up, acc_hidden), True, [])


def project(place, rows, weights):
    gate, up, down = weights
    height, half = rows.shape
    hidden = gate.shape[1]
    any_space = pl.BlockSpec(memory_space=pl.ANY)
    acc = jax.ShapeDtypeStruct((height // 2, hidden), F32)
    return pl.pallas_call(
        project_kernel,
        out_shape=(acc,) * 3,
        grid_spec=grid_of(
            (1,),
            [any_space] * 4,
            (whole(acc.shape),) * 3,
            [
                pltpu.VMEM((height, half), BF16),
                pltpu.VMEM((half, hidden), BF16),
                pltpu.VMEM((half, hidden), BF16),
                pltpu.VMEM((hidden, half), BF16),
                pltpu.SemaphoreType.DMA((half // DEPTH, 4)),
            ],
        ),
        compiler_params=params(20),
        name="project",
    )(place, rows, gate, up, down)


def expert_kernel(place, rows, gate, up, down, in_gate, in_up, in_hidden, theirs, mine, rows_in, gate_in, up_in, down_in, acc_gate, acc_up, acc_hidden, out, sems, more_sems, out_sems):
    half = rows.shape[1]
    core = place[0]
    side = 1 - core
    copies = chunk_copies(
        side, half, rows, gate, up, down, rows_in, gate_in, up_in, down_in, side * half, sems
    )
    rest = []
    for i in range(half // DEPTH):
        at = pl.ds(pl.multiple_of(core * half + i * DEPTH, DEPTH), DEPTH)
        rest.append(
            [
                pltpu.make_async_copy(gate.at[at, :], gate_in.at[at, :], more_sems.at[i, 0]),
                pltpu.make_async_copy(up.at[at, :], up_in.at[at, :], more_sems.at[i, 1]),
            ]
        )
    for i in range(AHEAD):
        start_all(copies[i])
    accs = (acc_gate, acc_up, acc_hidden)
    for acc, value in zip(accs, (in_gate, in_up, in_hidden)):
        acc[...] = value[...]
    ahead = list(rest)
    project_half(copies, rows_in, gate_in, up_in, down_in, side * half, accs, False, ahead)
    for copy in ahead:
        start_all(copy)

    pre_gate, pre_up, hidden = acc_gate[...], acc_up[...], acc_hidden[...]
    sigma = jax.nn.sigmoid(pre_gate)
    grad_gate = hidden * pre_up * sigma * (1.0 + pre_gate * (1.0 - sigma))
    grad_up = hidden * pre_gate * sigma
    product = jnp.sum(grad_gate * pre_gate + grad_up * pre_up, axis=1, keepdims=True)
    product = jnp.broadcast_to(product, (product.shape[0], LANES))
    product = interleave(product, product).astype(BF16)
    grad_gate, grad_up = grad_gate.astype(BF16), grad_up.astype(BF16)
    for copy in rest:
        wait_all(copy)

    columns = out.shape[2] - LANES

    def one(start):
        at = pl.ds(pl.multiple_of(start, LANES), BACK)
        total = lax.dot_general(grad_gate, gate_in[at, :], LAST, preferred_element_type=F32)
        return total + lax.dot_general(grad_up, up_in[at, :], LAST, preferred_element_type=F32)

    sent = []
    for slot, (to, whose) in enumerate(((theirs, side), (mine, core))):
        for at in range(0, columns, BACK):
            low, high = one(whose * columns + at), one((2 + whose) * columns + at)
            out[slot, :, at : at + BACK] = interleave(low, high).astype(BF16)
        out[slot, :, columns:] = product
        copy = pltpu.make_async_copy(out.at[slot], to, out_sems.at[slot])
        copy.start()
        sent.append(copy)
    wait_all(sent)


def expert(place, rows, weights, accs):
    gate, up, down = weights
    height, half = rows.shape
    width, hidden = gate.shape
    columns = width // 4
    any_space = pl.BlockSpec(memory_space=pl.ANY)
    message = jax.ShapeDtypeStruct((height, columns + LANES), BF16)
    acc = accs[0].shape
    return pl.pallas_call(
        expert_kernel,
        out_shape=(message, message),
        grid_spec=grid_of(
            (1,),
            [any_space] * 4 + [whole(acc)] * 3,
            (any_space, any_space),
            [
                pltpu.VMEM((height, half), BF16),
                pltpu.VMEM((width, hidden), BF16),
                pltpu.VMEM((width, hidden), BF16),
                pltpu.VMEM((hidden, half), BF16),
                pltpu.VMEM(acc, F32),
                pltpu.VMEM(acc, F32),
                pltpu.VMEM(acc, F32),
                pltpu.VMEM((2,) + message.shape, BF16),
                pltpu.SemaphoreType.DMA((half // DEPTH, 4)),
                pltpu.SemaphoreType.DMA((half // DEPTH, 2)),
                pltpu.SemaphoreType.DMA((2,)),
            ],
        ),
        compiler_params=params(32),
        name="expert",
    )(place, rows, gate, up, down, *accs)


def combine_kernel(place, gather, rows, first, second):
    count = first.shape[0]
    total = jnp.dot(gather[...], rows[...], preferred_element_type=F32)
    low, high = total[:count], total[count:]
    flip = place[2] == 1
    first[...] = jnp.where(flip, high, low).astype(first.dtype)
    second[...] = jnp.where(flip, low, high).astype(second.dtype)


def combine(place, gather, rows, first_type):
    count = gather.shape[0] // 2
    columns = rows.shape[1]
    part = columns // 3
    block = pl.BlockSpec((count, part), lambda i, place: (0, i))
    return pl.pallas_call(
        combine_kernel,
        out_shape=(
            jax.ShapeDtypeStruct((count, columns), first_type),
            jax.ShapeDtypeStruct((count, columns), BF16),
        ),
        grid_spec=grid_of(
            (3,),
            [whole(gather.shape), pl.BlockSpec((rows.shape[0], part), lambda i, place: (0, i))],
            (block, block),
        ),
        compiler_params=params(12),
        name="combine",
    )(place, gather, rows)


def body(tokens, cotangent, norm_gain, expert_ids, gate_weights, w_gate, w_up, w_down):
    experts = lax.axis_size("expert")
    plane = experts // 2
    token_count, width = tokens.shape
    top_count = expert_ids.shape[1]
    capacity = token_count * top_count * 3 // (2 * experts)
    columns = width // lax.axis_size("pipe")
    pipe = lax.axis_index("pipe")
    core, high = lax.rem(pipe, 2), pipe // 2
    low = lax.axis_index("expert") // plane
    after = lax.rem(2 * high + low + 1, 4) // 2
    place = jnp.stack([core, low, high]).astype(jnp.int32)
    place_after = jnp.stack([core, low, after]).astype(jnp.int32)
    weights = tuple(in_hbm(array[0]) for array in (w_gate, w_up, w_down))

    gain = norm_gain.reshape(1, width)
    make = functools.partial(
        make_message, place, in_hbm(tokens), in_hbm(cotangent), gain, expert_ids.T, gate_weights, capacity=capacity, plane=plane
    )
    other, inverse = make(inverse=None, other=True)
    own = make(inverse=inverse, other=False)
    other_ids = lax.ppermute(expert_ids, "expert", [(k, (k + plane) % experts) for k in range(experts)])
    gathers = [gather_matrix(place, ids, capacity, plane) for ids in (expert_ids, other_ids)]

    other = ring_permute(other, (1, 3))
    own = plane_exchange(own)
    own, *gathers = lax.optimization_barrier((own, *gathers))
    other = plane_exchange(other)

    def compute(rows, first):
        accs = project(place, rows, weights)
        swapped = core_swap(rows)
        accs, swapped, *first = lax.optimization_barrier((accs, swapped, *first))
        theirs, mine = expert(place, swapped, weights, accs)
        summed = mine.astype(F32) + core_swap(theirs).astype(F32)
        return summed.astype(BF16), first

    own_back, _ = compute(own, ())
    own_back, other = lax.optimization_barrier((own_back, other))
    own_back = plane_exchange(own_back)
    other_back, (own_back,) = compute(other, (own_back,))
    other_back = plane_exchange(other_back)

    kept, sent = combine(place, gathers[0], own_back, F32)
    from_far = ring_permute(sent, (2, 2))
    forth, back_ = combine(place_after, gathers[1], other_back, BF16)
    from_before = ring_permute(forth, (1, 1))
    from_after = ring_permute(back_, (3, 3))

    def own_columns(array):
        return lax.dynamic_slice_in_dim(array, pipe * columns, columns, array.ndim - 1)

    total = kept + from_far.astype(F32) + from_before.astype(F32) + from_after.astype(F32)
    normed_grad, product = total[:, :columns], total[:, columns : columns + 1]
    value_part = own_columns(tokens).astype(F32)
    cotangent_part = own_columns(cotangent).astype(F32)
    return (
        cotangent_part
        + inverse * own_columns(norm_gain) * normed_grad
        - value_part * (inverse * inverse * product / width)
    ).astype(BF16)


def solution(mesh):
    in_specs = (
        P("expert", None),
        P("expert", None),
        P(),
        P("expert", None),
        P("expert", None),
        P("expert", None, "pipe"),
        P("expert", None, "pipe"),
        P("expert", "pipe", None),
    )
    out_specs = P("expert", "pipe")
    return jax.shard_map(body, mesh=mesh, in_specs=in_specs, out_specs=out_specs, check_vma=False)
```

```python
import functools

import jax
import jax.numpy as jnp
from jax import lax
from jax.experimental import pallas as pl
from jax.experimental.pallas import tpu as pltpu
from jax.sharding import PartitionSpec as P

EPSILON = 1e-06
BF16 = jnp.bfloat16
F32 = jnp.float32
MIB = 1024 * 1024
FILL = 1792
DEPTH = 1792
AHEAD = 1
BACK = 896
LANES = 128
LAST = (((1,), (1,)), ((), ()))
CORE_SWAP = [(0, 1), (1, 0), (2, 3), (3, 2)]
HIGH_SWAP = [(0, 2), (2, 0), (1, 3), (3, 1)]


def params(mebibytes):
    return pltpu.CompilerParams(vmem_limit_bytes=mebibytes * MIB)


def in_hbm(array):
    return pltpu.with_memory_space_constraint(array, pltpu.HBM)


def whole(shape):
    return pl.BlockSpec(shape, lambda *_: (0,) * len(shape))


def grid_of(grid, in_specs, out_specs, scratch=()):
    return pltpu.PrefetchScalarGridSpec(
        num_scalar_prefetch=1, grid=grid, in_specs=in_specs, out_specs=out_specs, scratch_shapes=scratch
    )


def core_swap(array):
    return lax.ppermute(array, "pipe", CORE_SWAP)


def high_swap(array):
    return lax.ppermute(array, "pipe", HIGH_SWAP)


def exchange(rows):
    experts = lax.axis_size("expert")
    shaped = rows.reshape(experts, rows.shape[0] // experts, rows.shape[1])
    return lax.all_to_all(shaped, "expert", split_axis=0, concat_axis=0, tiled=True).reshape(rows.shape)


def message_kernel(capacity, place, all_tokens, tokens, cotangent, gain, ids, weights, rows, inverse, select, factors):
    top, count = ids.shape

    @pl.when(pl.program_id(0) == 0)
    def _():
        height = select.shape[0]
        experts = height // (2 * capacity)
        expert_of = lax.broadcasted_iota(jnp.int32, (experts, count), 0)
        earlier_of = lax.broadcasted_iota(jnp.int32, (count, count), 0)
        later_of = lax.broadcasted_iota(jnp.int32, (count, count), 1)
        before = (earlier_of < later_of).astype(F32).astype(BF16)
        row = lax.broadcasted_iota(jnp.int32, (height, count), 0)
        taken = jnp.zeros((experts, 1), F32)
        normed_part = jnp.zeros(row.shape, F32)
        for k in range(top):
            expert = ids[k : k + 1, :]
            named = (expert_of == expert).astype(F32)
            earlier = jnp.dot(named.astype(BF16), before, preferred_element_type=F32) + taken
            rank = jnp.sum(earlier * named, axis=0, keepdims=True).astype(jnp.int32)
            taken = taken + jnp.sum(named, axis=1, keepdims=True)
            at = expert * (2 * capacity) + rank
            normed_part = normed_part + (row == at).astype(F32)
            select[:, (k + 1) * count : (k + 2) * count] = (row == at + capacity).astype(F32).astype(BF16)
            column = jnp.sum(jnp.where(earlier_of == later_of, weights[k : k + 1, :], 0.0), axis=1, keepdims=True)
            factors[:, k : k + 1] = column
        select[:, :count] = normed_part.astype(BF16)
        values = all_tokens[...].astype(F32)
        inverse[...] = lax.rsqrt(jnp.mean(values * values, axis=1, keepdims=True) + EPSILON)

    normed = (tokens[...].astype(F32) * inverse[...] * gain[...]).astype(BF16)
    values = cotangent[...].astype(F32)
    parts = [normed] + [(factors[:, k : k + 1] * values).astype(BF16) for k in range(top)]
    rows[...] = jnp.dot(select[...], jnp.concatenate(parts, axis=0), preferred_element_type=F32).astype(BF16)


def make_message(place, tokens, cotangent, gain, ids, weights, capacity, experts):
    count, width = tokens.shape
    top = ids.shape[0]
    half = width // 2
    height = experts * 2 * capacity
    steps = half // FILL
    column = lambda i, place: (0, place[0] * steps + i)
    return pl.pallas_call(
        functools.partial(message_kernel, capacity),
        out_shape=(jax.ShapeDtypeStruct((height, half), BF16), jax.ShapeDtypeStruct((count, 1), F32)),
        grid_spec=grid_of(
            (steps,),
            [
                whole((count, width)),
                pl.BlockSpec((count, FILL), column),
                pl.BlockSpec((count, FILL), column),
                pl.BlockSpec((1, FILL), column),
                whole(ids.shape),
                whole(weights.shape),
            ],
            (pl.BlockSpec((height, FILL), lambda i, place: (0, i)), whole((count, 1))),
            [pltpu.VMEM((height, (top + 1) * count), BF16), pltpu.VMEM((count, top), F32)],
        ),
        compiler_params=params(32),
        name="message",
    )(place, tokens, tokens, cotangent, gain, ids, weights)


def gather_kernel(capacity, ids, out):
    top, count = ids.shape
    rows = out.shape[1]
    experts = rows // (2 * capacity)
    expert_of = lax.broadcasted_iota(jnp.int32, (experts, count), 0)
    earlier_of = lax.broadcasted_iota(jnp.int32, (count, count), 0)
    later_of = lax.broadcasted_iota(jnp.int32, (count, count), 1)
    before = (earlier_of < later_of).astype(F32).astype(BF16)
    row = lax.broadcasted_iota(jnp.int32, (count, rows), 1).astype(F32)
    taken = jnp.zeros((experts, 1), F32)
    first = jnp.zeros(row.shape, F32)
    second = jnp.zeros(row.shape, F32)
    for k in range(top):
        expert = ids[k : k + 1, :]
        named = (expert_of == expert).astype(F32)
        earlier = jnp.dot(named.astype(BF16), before, preferred_element_type=F32) + taken
        rank = jnp.sum(earlier * named, axis=0, keepdims=True)
        taken = taken + jnp.sum(named, axis=1, keepdims=True)
        at = expert.astype(F32) * (2 * capacity) + rank
        at = jnp.sum(jnp.where(earlier_of == later_of, at, 0.0), axis=1, keepdims=True)
        first = first + (row == at).astype(F32)
        second = second + (row == at + capacity).astype(F32)
    out[:count, :] = first.astype(BF16)
    out[count:, :] = second.astype(BF16)


def gather_matrix(ids, capacity, experts):
    count = ids.shape[1]
    return pl.pallas_call(
        functools.partial(gather_kernel, capacity),
        out_shape=jax.ShapeDtypeStruct((2 * count, experts * 2 * capacity), BF16),
        compiler_params=params(8),
        name="gather_matrix",
    )(ids)


def tiles(x, group):
    return x.reshape(x.shape[0] // (8 * group), group, 8, x.shape[1])


def upper(shape):
    return lax.broadcasted_iota(jnp.int32, shape, 1) < 4


def split_rows(x):
    rows, columns = x.shape
    x = x.astype(F32)
    a, b = tiles(x, 6), tiles(pltpu.roll(x, 4, 0), 6)
    top = upper((rows // 48, 8, columns))
    first = [a[:, 0], jnp.where(top, a[:, 1], b[:, 3]), b[:, 4]]
    second = [b[:, 2], jnp.where(top, b[:, 3], a[:, 4]), a[:, 5]]
    return [
        jnp.concatenate([p[:, None] for p in parts], axis=1).reshape(rows // 2, columns).astype(BF16)
        for parts in (first, second)
    ]


def interleave(x, y):
    rows, columns = x.shape
    x0, x1, x2 = tiles(x, 3), tiles(pltpu.roll(x, 4, 0), 3), tiles(pltpu.roll(x, rows - 4, 0), 3)
    y0, y1 = tiles(y, 3), tiles(pltpu.roll(y, 4, 0), 3)
    shape = (rows // 24, 8, columns)
    parts = [
        x0[:, 0],
        jnp.where(upper(shape), x0[:, 1], y1[:, 0]),
        y1[:, 1],
        x1[:, 2],
        jnp.where(upper(shape), x2[:, 2], y0[:, 1]),
        y0[:, 2],
    ]
    return jnp.concatenate([p[:, None] for p in parts], axis=1).reshape(2 * rows, columns)


def start_all(copies):
    for copy in copies:
        copy.start()


def wait_all(copies):
    for copy in copies:
        copy.wait()


def chunk_copies(side, half, rows, gate, up, down, rows_in, gate_in, up_in, down_in, gate_at, sems):
    copies = []
    for i in range(half // DEPTH):
        local = pl.ds(i * DEPTH, DEPTH)
        at = pl.ds(pl.multiple_of(side * half + i * DEPTH, DEPTH), DEPTH)
        to = pl.ds(pl.multiple_of(gate_at + i * DEPTH, DEPTH), DEPTH)
        copies.append(
            [
                pltpu.make_async_copy(rows.at[:, local], rows_in.at[:, local], sems.at[i, 0]),
                pltpu.make_async_copy(gate.at[at, :], gate_in.at[to, :], sems.at[i, 1]),
                pltpu.make_async_copy(up.at[at, :], up_in.at[to, :], sems.at[i, 2]),
                pltpu.make_async_copy(down.at[:, at], down_in.at[:, local], sems.at[i, 3]),
            ]
        )
    return copies


def project_half(copies, rows_in, gate_in, up_in, down_in, gate_at, accs, first, ahead):
    for i, copy in enumerate(copies):
        if i + AHEAD < len(copies):
            start_all(copies[i + AHEAD])
        elif ahead:
            start_all(ahead.pop(0))
        wait_all(copy)
        local = pl.ds(i * DEPTH, DEPTH)
        to = pl.ds(pl.multiple_of(gate_at + i * DEPTH, DEPTH), DEPTH)
        normed, routed = split_rows(rows_in[:, local])
        adds = (
            jnp.dot(normed, gate_in[to, :], preferred_element_type=F32),
            jnp.dot(normed, up_in[to, :], preferred_element_type=F32),
            lax.dot_general(routed, down_in[:, local], LAST, preferred_element_type=F32),
        )
        for acc, add in zip(accs, adds):
            acc[...] = add if first and i == 0 else acc[...] + add


def project_kernel(place, rows, gate, up, down, acc_gate, acc_up, acc_hidden, rows_in, gate_in, up_in, down_in, sems):
    half = rows.shape[1]
    copies = chunk_copies(place[0], half, rows, gate, up, down, rows_in, gate_in, up_in, down_in, 0, sems)
    for i in range(AHEAD):
        start_all(copies[i])
    project_half(copies, rows_in, gate_in, up_in, down_in, 0, (acc_gate, acc_up, acc_hidden), True, [])


def project(place, rows, weights):
    gate, up, down = weights
    height, half = rows.shape
    hidden = gate.shape[1]
    any_space = pl.BlockSpec(memory_space=pl.ANY)
    acc = jax.ShapeDtypeStruct((height // 2, hidden), F32)
    return pl.pallas_call(
        project_kernel,
        out_shape=(acc,) * 3,
        grid_spec=grid_of(
            (1,),
            [any_space] * 4,
            (whole(acc.shape),) * 3,
            [
                pltpu.VMEM((height, half), BF16),
                pltpu.VMEM((half, hidden), BF16),
                pltpu.VMEM((half, hidden), BF16),
                pltpu.VMEM((hidden, half), BF16),
                pltpu.SemaphoreType.DMA((half // DEPTH, 4)),
            ],
        ),
        compiler_params=params(32),
        name="project",
    )(place, rows, gate, up, down)


def expert_kernel(place, rows, gate, up, down, in_gate, in_up, in_hidden, theirs, mine, rows_in, gate_in, up_in, down_in, acc_gate, acc_up, acc_hidden, out, sems, more_sems, out_sems):
    half = rows.shape[1]
    core = place[0]
    side = 1 - core
    copies = chunk_copies(
        side, half, rows, gate, up, down, rows_in, gate_in, up_in, down_in, side * half, sems
    )
    rest = []
    for i in range(half // DEPTH):
        at = pl.ds(pl.multiple_of(core * half + i * DEPTH, DEPTH), DEPTH)
        rest.append(
            [
                pltpu.make_async_copy(gate.at[at, :], gate_in.at[at, :], more_sems.at[i, 0]),
                pltpu.make_async_copy(up.at[at, :], up_in.at[at, :], more_sems.at[i, 1]),
            ]
        )
    for i in range(AHEAD):
        start_all(copies[i])
    accs = (acc_gate, acc_up, acc_hidden)
    for acc, value in zip(accs, (in_gate, in_up, in_hidden)):
        acc[...] = value[...]
    ahead = list(rest)
    project_half(copies, rows_in, gate_in, up_in, down_in, side * half, accs, False, ahead)
    for copy in ahead:
        start_all(copy)

    pre_gate, pre_up, hidden = acc_gate[...], acc_up[...], acc_hidden[...]
    sigma = jax.nn.sigmoid(pre_gate)
    grad_gate = hidden * pre_up * sigma * (1.0 + pre_gate * (1.0 - sigma))
    grad_up = hidden * pre_gate * sigma
    product = jnp.sum(grad_gate * pre_gate + grad_up * pre_up, axis=1, keepdims=True)
    product = jnp.broadcast_to(product, (product.shape[0], LANES))
    product = interleave(product, product).astype(BF16)
    grad_gate, grad_up = grad_gate.astype(BF16), grad_up.astype(BF16)
    for copy in rest:
        wait_all(copy)

    columns = out.shape[2] - LANES

    def one(start):
        at = pl.ds(pl.multiple_of(start, LANES), BACK)
        total = lax.dot_general(grad_gate, gate_in[at, :], LAST, preferred_element_type=F32)
        return total + lax.dot_general(grad_up, up_in[at, :], LAST, preferred_element_type=F32)

    sent = []
    for slot, (to, whose) in enumerate(((theirs, side), (mine, core))):
        for at in range(0, columns, BACK):
            low, high = one(whose * columns + at), one((2 + whose) * columns + at)
            out[slot, :, at : at + BACK] = interleave(low, high).astype(BF16)
        out[slot, :, columns:] = product
        copy = pltpu.make_async_copy(out.at[slot], to, out_sems.at[slot])
        copy.start()
        sent.append(copy)
    wait_all(sent)


def expert(place, rows, weights, accs):
    gate, up, down = weights
    height, half = rows.shape
    width, hidden = gate.shape
    columns = width // 4
    any_space = pl.BlockSpec(memory_space=pl.ANY)
    message = jax.ShapeDtypeStruct((height, columns + LANES), BF16)
    acc = accs[0].shape
    return pl.pallas_call(
        expert_kernel,
        out_shape=(message, message),
        grid_spec=grid_of(
            (1,),
            [any_space] * 4 + [whole(acc)] * 3,
            (any_space, any_space),
            [
                pltpu.VMEM((height, half), BF16),
                pltpu.VMEM((width, hidden), BF16),
                pltpu.VMEM((width, hidden), BF16),
                pltpu.VMEM((hidden, half), BF16),
                pltpu.VMEM(acc, F32),
                pltpu.VMEM(acc, F32),
                pltpu.VMEM(acc, F32),
                pltpu.VMEM((2,) + message.shape, BF16),
                pltpu.SemaphoreType.DMA((half // DEPTH, 4)),
                pltpu.SemaphoreType.DMA((half // DEPTH, 2)),
                pltpu.SemaphoreType.DMA((2,)),
            ],
        ),
        compiler_params=params(48),
        name="expert",
    )(place, rows, gate, up, down, *accs)


def combine_kernel(place, gather, rows, first, second):
    count = first.shape[0]
    total = jnp.dot(gather[...], rows[...], preferred_element_type=F32)
    low, high = total[:count], total[count:]
    flip = place[1] == 1
    first[...] = jnp.where(flip, high, low).astype(first.dtype)
    second[...] = jnp.where(flip, low, high).astype(second.dtype)


def combine(place, gather, rows):
    count = gather.shape[0] // 2
    columns = rows.shape[1]
    part = columns // 3
    block = pl.BlockSpec((count, part), lambda i, place: (0, i))
    return pl.pallas_call(
        combine_kernel,
        out_shape=(
            jax.ShapeDtypeStruct((count, columns), F32),
            jax.ShapeDtypeStruct((count, columns), BF16),
        ),
        grid_spec=grid_of(
            (3,),
            [whole(gather.shape), pl.BlockSpec((rows.shape[0], part), lambda i, place: (0, i))],
            (block, block),
        ),
        compiler_params=params(12),
        name="combine",
    )(place, gather, rows)


def body(tokens, cotangent, norm_gain, expert_ids, gate_weights, w_gate, w_up, w_down):
    experts = lax.axis_size("expert")
    token_count, width = tokens.shape
    top_count = expert_ids.shape[1]
    capacity = token_count * top_count * 3 // (2 * experts)
    columns = width // lax.axis_size("pipe")
    pipe = lax.axis_index("pipe")
    place = jnp.stack([lax.rem(pipe, 2), pipe // 2]).astype(jnp.int32)
    weights = tuple(in_hbm(array[0]) for array in (w_gate, w_up, w_down))
    ids = in_hbm(expert_ids.T)

    rows, inverse = make_message(
        place,
        in_hbm(tokens),
        in_hbm(cotangent),
        in_hbm(norm_gain.reshape(1, width)),
        ids,
        in_hbm(gate_weights.T),
        capacity,
        experts,
    )
    gather = gather_matrix(ids, capacity, experts)
    rows, gather = lax.optimization_barrier((rows, gather))
    rows = exchange(rows)
    accs = project(place, rows, weights)
    theirs, mine = expert(place, in_hbm(core_swap(rows)), weights, accs)
    back = exchange((mine.astype(F32) + core_swap(theirs).astype(F32)).astype(BF16))
    kept, sent = combine(place, gather, back)
    total = kept + high_swap(sent).astype(F32)

    def own_columns(array):
        return lax.dynamic_slice_in_dim(array, pipe * columns, columns, array.ndim - 1)

    normed_grad, product = total[:, :columns], total[:, columns : columns + 1]
    value_part = own_columns(tokens).astype(F32)
    cotangent_part = own_columns(cotangent).astype(F32)
    return (
        cotangent_part
        + inverse * own_columns(norm_gain) * normed_grad
        - value_part * (inverse * inverse * product / width)
    ).astype(BF16)


def solution(mesh):
    in_specs = (
        P("expert", None),
        P("expert", None),
        P(),
        P("expert", None),
        P("expert", None),
        P("expert", None, "pipe"),
        P("expert", None, "pipe"),
        P("expert", "pipe", None),
    )
    out_specs = P("expert", "pipe")
    return jax.shard_map(body, mesh=mesh, in_specs=in_specs, out_specs=out_specs, check_vma=False)
```

```python
import functools

import jax
import jax.numpy as jnp
from jax import lax
from jax.experimental import pallas as pl
from jax.experimental.pallas import tpu as pltpu
from jax.sharding import PartitionSpec as P

EPSILON = 1e-06
BF16 = jnp.bfloat16
F32 = jnp.float32
MIB = 1024 * 1024
FILL = 1792
DEPTH = 1792
AHEAD = 1
BACK = 512
DIRECT = 1024
LANES = 128
SMALL = pl.CostEstimate(flops=0, bytes_accessed=0, transcendentals=0)
LAST = (((1,), (1,)), ((), ()))
CORE_SWAP = [(0, 1), (1, 0), (2, 3), (3, 2)]
HIGH_SWAP = [(0, 2), (2, 0), (1, 3), (3, 1)]


def params(mebibytes):
    return pltpu.CompilerParams(vmem_limit_bytes=mebibytes * MIB)


def in_hbm(array):
    return pltpu.with_memory_space_constraint(array, pltpu.HBM)


def whole(shape):
    return pl.BlockSpec(shape, lambda *_: (0,) * len(shape))


def grid_of(grid, in_specs, out_specs, scratch=()):
    return pltpu.PrefetchScalarGridSpec(
        num_scalar_prefetch=1, grid=grid, in_specs=in_specs, out_specs=out_specs, scratch_shapes=scratch
    )


def core_swap(array):
    return lax.ppermute(array, "pipe", CORE_SWAP)


def high_swap(array):
    return lax.ppermute(array, "pipe", HIGH_SWAP)


def exchange(rows):
    experts = lax.axis_size("expert")
    shaped = rows.reshape(experts, rows.shape[0] // experts, rows.shape[1])
    return lax.all_to_all(shaped, "expert", split_axis=0, concat_axis=0, tiled=True).reshape(rows.shape)


def message_kernel(capacity, place, all_tokens, tokens, cotangent, gain, ids, weights, rows, inverse, select, factors):
    top, count = ids.shape

    @pl.when(pl.program_id(0) == 0)
    def _():
        height = select.shape[0]
        experts = height // (2 * capacity)
        expert_of = lax.broadcasted_iota(jnp.int32, (experts, count), 0)
        earlier_of = lax.broadcasted_iota(jnp.int32, (count, count), 0)
        later_of = lax.broadcasted_iota(jnp.int32, (count, count), 1)
        before = (earlier_of < later_of).astype(F32).astype(BF16)
        row = lax.broadcasted_iota(jnp.int32, (height, count), 0)
        taken = jnp.zeros((experts, 1), F32)
        normed_part = jnp.zeros(row.shape, F32)
        for k in range(top):
            expert = ids[k : k + 1, :]
            named = (expert_of == expert).astype(F32)
            earlier = jnp.dot(named.astype(BF16), before, preferred_element_type=F32) + taken
            rank = jnp.sum(earlier * named, axis=0, keepdims=True).astype(jnp.int32)
            taken = taken + jnp.sum(named, axis=1, keepdims=True)
            at = expert * (2 * capacity) + rank
            normed_part = normed_part + (row == at).astype(F32)
            select[:, (k + 1) * count : (k + 2) * count] = (row == at + capacity).astype(F32).astype(BF16)
            column = jnp.sum(jnp.where(earlier_of == later_of, weights[k : k + 1, :], 0.0), axis=1, keepdims=True)
            factors[:, k : k + 1] = column
        select[:, :count] = normed_part.astype(BF16)
        values = all_tokens[...].astype(F32)
        inverse[...] = lax.rsqrt(jnp.mean(values * values, axis=1, keepdims=True) + EPSILON)

    normed = (tokens[...].astype(F32) * inverse[...] * gain[...]).astype(BF16)
    values = cotangent[...].astype(F32)
    parts = [normed] + [(factors[:, k : k + 1] * values).astype(BF16) for k in range(top)]
    rows[...] = jnp.dot(select[...], jnp.concatenate(parts, axis=0), preferred_element_type=F32).astype(BF16)


def make_message(place, tokens, cotangent, gain, ids, weights, capacity, experts):
    count, width = tokens.shape
    top = ids.shape[0]
    half = width // 2
    height = experts * 2 * capacity
    steps = half // FILL
    column = lambda i, place: (0, place[0] * steps + i)
    return pl.pallas_call(
        functools.partial(message_kernel, capacity),
        out_shape=(jax.ShapeDtypeStruct((height, half), BF16), jax.ShapeDtypeStruct((count, 1), F32)),
        grid_spec=grid_of(
            (steps,),
            [
                whole((count, width)),
                pl.BlockSpec((count, FILL), column),
                pl.BlockSpec((count, FILL), column),
                pl.BlockSpec((1, FILL), column),
                whole(ids.shape),
                whole(weights.shape),
            ],
            (pl.BlockSpec((height, FILL), lambda i, place: (0, i)), whole((count, 1))),
            [pltpu.VMEM((height, (top + 1) * count), BF16), pltpu.VMEM((count, top), F32)],
        ),
        compiler_params=params(32),
        name="message",
    )(place, tokens, tokens, cotangent, gain, ids, weights)


def gather_kernel(capacity, ids, out):
    top, count = ids.shape
    rows = out.shape[1]
    experts = rows // (2 * capacity)
    expert_of = lax.broadcasted_iota(jnp.int32, (experts, count), 0)
    earlier_of = lax.broadcasted_iota(jnp.int32, (count, count), 0)
    later_of = lax.broadcasted_iota(jnp.int32, (count, count), 1)
    before = (earlier_of < later_of).astype(F32).astype(BF16)
    row = lax.broadcasted_iota(jnp.int32, (count, rows), 1).astype(F32)
    taken = jnp.zeros((experts, 1), F32)
    first = jnp.zeros(row.shape, F32)
    second = jnp.zeros(row.shape, F32)
    for k in range(top):
        expert = ids[k : k + 1, :]
        named = (expert_of == expert).astype(F32)
        earlier = jnp.dot(named.astype(BF16), before, preferred_element_type=F32) + taken
        rank = jnp.sum(earlier * named, axis=0, keepdims=True)
        taken = taken + jnp.sum(named, axis=1, keepdims=True)
        at = expert.astype(F32) * (2 * capacity) + rank
        at = jnp.sum(jnp.where(earlier_of == later_of, at, 0.0), axis=1, keepdims=True)
        first = first + (row == at).astype(F32)
        second = second + (row == at + capacity).astype(F32)
    out[:count, :] = first.astype(BF16)
    out[count:, :] = second.astype(BF16)


def gather_matrix(ids, capacity, experts):
    count = ids.shape[1]
    return pl.pallas_call(
        functools.partial(gather_kernel, capacity),
        out_shape=jax.ShapeDtypeStruct((2 * count, experts * 2 * capacity), BF16),
        compiler_params=params(8),
        name="gather_matrix",
    )(ids)


def tiles(x, group):
    return x.reshape(x.shape[0] // (8 * group), group, 8, x.shape[1])


def upper(shape):
    return lax.broadcasted_iota(jnp.int32, shape, 1) < 4


def split_rows(x):
    rows, columns = x.shape
    x = x.astype(F32)
    a, b = tiles(x, 6), tiles(pltpu.roll(x, 4, 0), 6)
    top = upper((rows // 48, 8, columns))
    first = [a[:, 0], jnp.where(top, a[:, 1], b[:, 3]), b[:, 4]]
    second = [b[:, 2], jnp.where(top, b[:, 3], a[:, 4]), a[:, 5]]
    return [
        jnp.concatenate([p[:, None] for p in parts], axis=1).reshape(rows // 2, columns).astype(BF16)
        for parts in (first, second)
    ]


def interleave(x, y):
    rows, columns = x.shape
    x0, x1, x2 = tiles(x, 3), tiles(pltpu.roll(x, 4, 0), 3), tiles(pltpu.roll(x, rows - 4, 0), 3)
    y0, y1 = tiles(y, 3), tiles(pltpu.roll(y, 4, 0), 3)
    shape = (rows // 24, 8, columns)
    parts = [
        x0[:, 0],
        jnp.where(upper(shape), x0[:, 1], y1[:, 0]),
        y1[:, 1],
        x1[:, 2],
        jnp.where(upper(shape), x2[:, 2], y0[:, 1]),
        y0[:, 2],
    ]
    return jnp.concatenate([p[:, None] for p in parts], axis=1).reshape(2 * rows, columns)


def start_all(copies):
    for copy in copies:
        copy.start()


def wait_all(copies):
    for copy in copies:
        copy.wait()


def chunk_copies(side, half, rows, gate, up, down, rows_in, gate_in, up_in, down_in, gate_at, sems):
    copies = []
    for i in range(half // DEPTH):
        local = pl.ds(i * DEPTH, DEPTH)
        at = pl.ds(pl.multiple_of(side * half + i * DEPTH, DEPTH), DEPTH)
        to = pl.ds(pl.multiple_of(gate_at + i * DEPTH, DEPTH), DEPTH)
        copy = [
            pltpu.make_async_copy(gate.at[at, :], gate_in.at[to, :], sems.at[i, 1]),
            pltpu.make_async_copy(up.at[at, :], up_in.at[to, :], sems.at[i, 2]),
            pltpu.make_async_copy(down.at[:, at], down_in.at[:, local], sems.at[i, 3]),
        ]
        if rows is not None:
            copy.append(pltpu.make_async_copy(rows.at[:, local], rows_in.at[:, local], sems.at[i, 0]))
        copies.append(copy)
    return copies


def project_half(copies, rows_in, gate_in, up_in, down_in, gate_at, accs, first, ahead):
    for i, copy in enumerate(copies):
        if i + AHEAD < len(copies):
            start_all(copies[i + AHEAD])
        elif ahead:
            start_all(ahead.pop(0))
        wait_all(copy)
        local = pl.ds(i * DEPTH, DEPTH)
        to = pl.ds(pl.multiple_of(gate_at + i * DEPTH, DEPTH), DEPTH)
        normed, routed = split_rows(rows_in[:, local])
        adds = (
            jnp.dot(normed, gate_in[to, :], preferred_element_type=F32),
            jnp.dot(normed, up_in[to, :], preferred_element_type=F32),
            lax.dot_general(routed, down_in[:, local], LAST, preferred_element_type=F32),
        )
        for acc, add in zip(accs, adds):
            acc[...] = add if first and i == 0 else acc[...] + add


def project_kernel(place, rows, gate, up, down, acc_gate, acc_up, acc_hidden, rows_in, gate_in, up_in, down_in, sems):
    half = rows.shape[1]
    copies = chunk_copies(place[0], half, rows, gate, up, down, rows_in, gate_in, up_in, down_in, 0, sems)
    for i in range(AHEAD):
        start_all(copies[i])
    project_half(copies, rows_in, gate_in, up_in, down_in, 0, (acc_gate, acc_up, acc_hidden), True, [])


def project(place, rows, weights):
    gate, up, down = weights
    height, half = rows.shape
    hidden = gate.shape[1]
    any_space = pl.BlockSpec(memory_space=pl.ANY)
    acc = jax.ShapeDtypeStruct((height // 2, hidden), F32)
    return pl.pallas_call(
        project_kernel,
        out_shape=(acc,) * 3,
        grid_spec=grid_of(
            (1,),
            [any_space] * 4,
            (whole(acc.shape),) * 3,
            [
                pltpu.VMEM((height, half), BF16),
                pltpu.VMEM((half, hidden), BF16),
                pltpu.VMEM((half, hidden), BF16),
                pltpu.VMEM((hidden, half), BF16),
                pltpu.SemaphoreType.DMA((half // DEPTH, 4)),
            ],
        ),
        compiler_params=params(32),
        name="project",
    )(place, rows, gate, up, down)


def expert_kernel(place, rows, gate, up, down, in_gate, in_up, in_hidden, theirs, mine, grad_gate, grad_up, gate_in, up_in, down_in, acc_gate, acc_up, acc_hidden, out, sems, more_sems, out_sems):
    half = rows.shape[1]
    core = place[0]
    side = 1 - core
    copies = chunk_copies(side, half, None, gate, up, down, None, gate_in, up_in, down_in, side * half, sems)
    rest = []
    for i in range(half // DEPTH):
        at = pl.ds(pl.multiple_of(core * half + i * DEPTH, DEPTH), DEPTH)
        rest.append(
            [
                pltpu.make_async_copy(gate.at[at, :], gate_in.at[at, :], more_sems.at[i, 0]),
                pltpu.make_async_copy(up.at[at, :], up_in.at[at, :], more_sems.at[i, 1]),
            ]
        )
    for i in range(AHEAD):
        start_all(copies[i])
    accs = (acc_gate, acc_up, acc_hidden)
    for acc, value in zip(accs, (in_gate, in_up, in_hidden)):
        acc[...] = value[...]
    ahead = list(rest)
    project_half(copies, rows, gate_in, up_in, down_in, side * half, accs, False, ahead)
    for copy in ahead:
        start_all(copy)

    pre_gate, pre_up, hidden = acc_gate[...], acc_up[...], acc_hidden[...]
    sigma = jax.nn.sigmoid(pre_gate)
    to_gate = hidden * pre_up * sigma * (1.0 + pre_gate * (1.0 - sigma))
    to_up = hidden * pre_gate * sigma
    product = jnp.sum(to_gate * pre_gate + to_up * pre_up, axis=1, keepdims=True)
    product = jnp.broadcast_to(product, (product.shape[0], LANES))
    product = interleave(product, product).astype(BF16)
    grad_gate[...] = to_gate.astype(BF16)
    grad_up[...] = to_up.astype(BF16)
    for copy in rest:
        wait_all(copy)

    columns = gate.shape[0] // 4

    def one(start):
        at = pl.ds(pl.multiple_of(start, LANES), BACK)
        total = lax.dot_general(grad_gate[...], gate_in[at, :], LAST, preferred_element_type=F32)
        return total + lax.dot_general(grad_up[...], up_in[at, :], LAST, preferred_element_type=F32)

    sent = []
    for slot, (to, whose) in enumerate(((theirs, side), (mine, core))):
        for at in range(0, DIRECT, BACK):
            low, high = one(whose * columns + at), one((2 + whose) * columns + at)
            out[slot, :, at : at + BACK] = interleave(low, high).astype(BF16)
        out[slot, :, DIRECT:] = product
        copy = pltpu.make_async_copy(out.at[slot], to, out_sems.at[slot])
        copy.start()
        sent.append(copy)
    wait_all(sent)


def expert(place, rows, weights, accs):
    gate, up, down = weights
    height, half = rows.shape
    width, hidden = gate.shape
    any_space = pl.BlockSpec(memory_space=pl.ANY)
    message = jax.ShapeDtypeStruct((height, DIRECT + LANES), BF16)
    acc = accs[0].shape
    grad = jax.ShapeDtypeStruct(acc, BF16)
    return pl.pallas_call(
        expert_kernel,
        out_shape=(message, message, grad, grad),
        grid_spec=grid_of(
            (1,),
            [pl.BlockSpec(memory_space=pltpu.VMEM)] + [any_space] * 3 + [whole(acc)] * 3,
            (any_space, any_space, whole(acc), whole(acc)),
            [
                pltpu.VMEM((width, hidden), BF16),
                pltpu.VMEM((width, hidden), BF16),
                pltpu.VMEM((hidden, half), BF16),
                pltpu.VMEM(acc, F32),
                pltpu.VMEM(acc, F32),
                pltpu.VMEM(acc, F32),
                pltpu.VMEM((2,) + message.shape, BF16),
                pltpu.SemaphoreType.DMA((half // DEPTH, 4)),
                pltpu.SemaphoreType.DMA((half // DEPTH, 2)),
                pltpu.SemaphoreType.DMA((2,)),
            ],
        ),
        compiler_params=params(40),
        name="expert",
    )(place, rows, gate, up, down, *accs)


def rest_kernel(place, grad_gate, grad_up, gate, up, theirs, mine, gate_in, up_in, out, sems, out_sems):
    columns = gate.shape[0] // 4
    core, high = place[0], place[1]
    width = columns - DIRECT
    half = width // 2
    copies = []
    for slot, whose in enumerate((1 - core, core)):
        for turn, part in enumerate((high, 1 - high)):
            at = pl.ds(pl.multiple_of((2 * part + whose) * columns + DIRECT, 256), width)
            to = 2 * slot + turn
            copies.append(
                [
                    pltpu.make_async_copy(gate.at[at, :], gate_in.at[to], sems.at[to, 0]),
                    pltpu.make_async_copy(up.at[at, :], up_in.at[to], sems.at[to, 1]),
                ]
            )
    for copy in copies:
        start_all(copy)
    sent = []
    for slot, to in enumerate((theirs, mine)):
        for turn in range(2):
            at = 2 * slot + turn
            wait_all(copies[at])
            rows = lax.dot_general(grad_gate[...], gate_in[at], LAST, preferred_element_type=F32)
            rows = rows + lax.dot_general(grad_up[...], up_in[at], LAST, preferred_element_type=F32)
            out[slot, :, turn * half : (turn + 1) * half] = interleave(rows[:, :half], rows[:, half:]).astype(BF16)
        copy = pltpu.make_async_copy(out.at[slot], to, out_sems.at[slot])
        copy.start()
        sent.append(copy)
    wait_all(sent)


def rest(place, grads, weights):
    gate, up, _ = weights
    rows, hidden = grads[0].shape
    width = gate.shape[0] // 4 - DIRECT
    any_space = pl.BlockSpec(memory_space=pl.ANY)
    message = jax.ShapeDtypeStruct((2 * rows, width), BF16)
    return pl.pallas_call(
        rest_kernel,
        out_shape=(message, message),
        grid_spec=grid_of(
            (1,),
            [whole((rows, hidden))] * 2 + [any_space] * 2,
            (any_space, any_space),
            [
                pltpu.VMEM((4, width, hidden), BF16),
                pltpu.VMEM((4, width, hidden), BF16),
                pltpu.VMEM((2,) + message.shape, BF16),
                pltpu.SemaphoreType.DMA((4, 2)),
                pltpu.SemaphoreType.DMA((2,)),
            ],
        ),
        compiler_params=params(24),
        cost_estimate=SMALL,
        name="rest",
    )(place, *grads, gate, up)


def combine_kernel(place, gather, rows, first, second):
    count = first.shape[0]
    total = jnp.dot(gather[...], rows[...], preferred_element_type=F32)
    low, high = total[:count], total[count:]
    flip = place[1] == 1
    first[...] = jnp.where(flip, high, low).astype(first.dtype)
    second[...] = jnp.where(flip, low, high).astype(second.dtype)


def combine(place, gather, rows):
    count = gather.shape[0] // 2
    columns = rows.shape[1]
    part = columns // 3
    block = pl.BlockSpec((count, part), lambda i, place: (0, i))
    return pl.pallas_call(
        combine_kernel,
        out_shape=(
            jax.ShapeDtypeStruct((count, columns), F32),
            jax.ShapeDtypeStruct((count, columns), BF16),
        ),
        grid_spec=grid_of(
            (3,),
            [whole(gather.shape), pl.BlockSpec((rows.shape[0], part), lambda i, place: (0, i))],
            (block, block),
        ),
        compiler_params=params(12),
        name="combine",
    )(place, gather, rows)


def final_kernel(width, place, gather, rows, kept, arrived, tokens, cotangent, gain, inverse, out):
    count = tokens.shape[0]
    total = jnp.dot(gather[...], rows[...], preferred_element_type=F32)
    direct = kept[...] + arrived[...].astype(F32)
    scale = inverse[...]
    product = scale * scale * direct[:, DIRECT : DIRECT + 1] / width
    half = rows.shape[1]
    for at, size, grad in (
        (0, DIRECT, direct[:, :DIRECT]),
        (DIRECT, half, total[:count]),
        (DIRECT + half, half, total[count:]),
    ):
        part = slice(at, at + size)
        value = cotangent[:, part].astype(F32) + scale * gain[:, part] * grad
        out[:, part] = (value - tokens[:, part].astype(F32) * product).astype(BF16)


def final(place, gather, rows, kept, arrived, tokens, cotangent, gain, inverse):
    count, width = tokens.shape
    columns = width // 4
    quarter = lambda height: pl.BlockSpec((height, columns), lambda i, place: (0, place[2]))
    return pl.pallas_call(
        functools.partial(final_kernel, width),
        out_shape=jax.ShapeDtypeStruct((count, columns), BF16),
        grid_spec=grid_of(
            (1,),
            [whole(array.shape) for array in (gather, rows, kept, arrived)]
            + [quarter(count), quarter(count), quarter(1), whole(inverse.shape)],
            whole((count, columns)),
        ),
        compiler_params=params(16),
        name="final",
    )(place, gather, rows, kept, arrived, tokens, cotangent, gain, inverse)


def body(tokens, cotangent, norm_gain, expert_ids, gate_weights, w_gate, w_up, w_down):
    experts = lax.axis_size("expert")
    token_count, width = tokens.shape
    top_count = expert_ids.shape[1]
    capacity = token_count * top_count * 3 // (2 * experts)
    pipe = lax.axis_index("pipe")
    place = jnp.stack([lax.rem(pipe, 2), pipe // 2, pipe]).astype(jnp.int32)
    weights = tuple(in_hbm(array[0]) for array in (w_gate, w_up, w_down))
    ids = in_hbm(expert_ids.T)
    tokens, cotangent, gain = in_hbm(tokens), in_hbm(cotangent), in_hbm(norm_gain.reshape(1, width))

    rows, inverse = make_message(
        place, tokens, cotangent, gain, ids, in_hbm(gate_weights.T), capacity, experts
    )
    gather = gather_matrix(ids, capacity, experts)
    rows, gather = lax.optimization_barrier((rows, gather))
    rows = exchange(rows)
    accs = project(place, rows, weights)
    theirs, mine, *grads = expert(place, core_swap(rows), weights, accs)
    direct = (mine.astype(F32) + core_swap(theirs).astype(F32)).astype(BF16)

    theirs, mine = rest(place, grads, weights)
    summed = mine.astype(F32) + core_swap(theirs).astype(F32)
    half = summed.shape[1] // 2
    summed = summed[:, :half] + high_swap(summed[:, half:].astype(BF16)).astype(F32)
    direct = exchange(direct)
    direct, summed = lax.optimization_barrier((direct, summed.astype(BF16)))
    kept, sent = combine(place, gather, direct)
    arrived = high_swap(sent)
    return final(place, gather, exchange(summed), kept, arrived, tokens, cotangent, gain, inverse)


def solution(mesh):
    in_specs = (
        P("expert", None),
        P("expert", None),
        P(),
        P("expert", None),
        P("expert", None),
        P("expert", None, "pipe"),
        P("expert", None, "pipe"),
        P("expert", "pipe", None),
    )
    out_specs = P("expert", "pipe")
    return jax.shard_map(body, mesh=mesh, in_specs=in_specs, out_specs=out_specs, check_vma=False)
```

```python
import functools

import jax
import jax.numpy as jnp
from jax import lax
from jax.experimental import pallas as pl
from jax.experimental.pallas import tpu as pltpu
from jax.sharding import PartitionSpec as P

EPSILON = 1e-06
BF16 = jnp.bfloat16
F32 = jnp.float32
MIB = 1024 * 1024
FILL = 1792
DEPTH = 1792
AHEAD = 1
BACK = 512
DIRECT = 1024
LANES = 128
LAST = (((1,), (1,)), ((), ()))
CORE_SWAP = [(0, 1), (1, 0), (2, 3), (3, 2)]
HIGH_SWAP = [(0, 2), (2, 0), (1, 3), (3, 1)]


def params(mebibytes):
    return pltpu.CompilerParams(vmem_limit_bytes=mebibytes * MIB)


def in_hbm(array):
    return pltpu.with_memory_space_constraint(array, pltpu.HBM)


def whole(shape):
    return pl.BlockSpec(shape, lambda *_: (0,) * len(shape))


def grid_of(grid, in_specs, out_specs, scratch=()):
    return pltpu.PrefetchScalarGridSpec(
        num_scalar_prefetch=1, grid=grid, in_specs=in_specs, out_specs=out_specs, scratch_shapes=scratch
    )


def core_swap(array):
    return lax.ppermute(array, "pipe", CORE_SWAP)


def high_swap(array):
    return lax.ppermute(array, "pipe", HIGH_SWAP)


def exchange(rows):
    experts = lax.axis_size("expert")
    shaped = rows.reshape(experts, rows.shape[0] // experts, rows.shape[1])
    return lax.all_to_all(shaped, "expert", split_axis=0, concat_axis=0, tiled=True).reshape(rows.shape)


def message_kernel(capacity, place, all_tokens, tokens, cotangent, gain, ids, weights, rows, inverse, select, factors):
    top, count = ids.shape

    @pl.when(pl.program_id(0) == 0)
    def _():
        height = select.shape[0]
        experts = height // (2 * capacity)
        expert_of = lax.broadcasted_iota(jnp.int32, (experts, count), 0)
        earlier_of = lax.broadcasted_iota(jnp.int32, (count, count), 0)
        later_of = lax.broadcasted_iota(jnp.int32, (count, count), 1)
        before = (earlier_of < later_of).astype(F32).astype(BF16)
        row = lax.broadcasted_iota(jnp.int32, (height, count), 0)
        taken = jnp.zeros((experts, 1), F32)
        normed_part = jnp.zeros(row.shape, F32)
        for k in range(top):
            expert = ids[k : k + 1, :]
            named = (expert_of == expert).astype(F32)
            earlier = jnp.dot(named.astype(BF16), before, preferred_element_type=F32) + taken
            rank = jnp.sum(earlier * named, axis=0, keepdims=True).astype(jnp.int32)
            taken = taken + jnp.sum(named, axis=1, keepdims=True)
            at = expert * (2 * capacity) + rank
            normed_part = normed_part + (row == at).astype(F32)
            select[:, (k + 1) * count : (k + 2) * count] = (row == at + capacity).astype(F32).astype(BF16)
            column = jnp.sum(jnp.where(earlier_of == later_of, weights[k : k + 1, :], 0.0), axis=1, keepdims=True)
            factors[:, k : k + 1] = column
        select[:, :count] = normed_part.astype(BF16)
        values = all_tokens[...].astype(F32)
        inverse[...] = lax.rsqrt(jnp.mean(values * values, axis=1, keepdims=True) + EPSILON)

    normed = (tokens[...].astype(F32) * inverse[...] * gain[...]).astype(BF16)
    values = cotangent[...].astype(F32)
    parts = [normed] + [(factors[:, k : k + 1] * values).astype(BF16) for k in range(top)]
    rows[...] = jnp.dot(select[...], jnp.concatenate(parts, axis=0), preferred_element_type=F32).astype(BF16)


def make_message(place, tokens, cotangent, gain, ids, weights, capacity, experts):
    count, width = tokens.shape
    top = ids.shape[0]
    half = width // 2
    height = experts * 2 * capacity
    steps = half // FILL
    column = lambda i, place: (0, place[0] * steps + i)
    return pl.pallas_call(
        functools.partial(message_kernel, capacity),
        out_shape=(jax.ShapeDtypeStruct((height, half), BF16), jax.ShapeDtypeStruct((count, 1), F32)),
        grid_spec=grid_of(
            (steps,),
            [
                whole((count, width)),
                pl.BlockSpec((count, FILL), column),
                pl.BlockSpec((count, FILL), column),
                pl.BlockSpec((1, FILL), column),
                whole(ids.shape),
                whole(weights.shape),
            ],
            (pl.BlockSpec((height, FILL), lambda i, place: (0, i)), whole((count, 1))),
            [pltpu.VMEM((height, (top + 1) * count), BF16), pltpu.VMEM((count, top), F32)],
        ),
        compiler_params=params(32),
        name="message",
    )(place, tokens, tokens, cotangent, gain, ids, weights)


def gather_kernel(capacity, ids, out):
    top, count = ids.shape
    rows = out.shape[1]
    experts = rows // (2 * capacity)
    expert_of = lax.broadcasted_iota(jnp.int32, (experts, count), 0)
    earlier_of = lax.broadcasted_iota(jnp.int32, (count, count), 0)
    later_of = lax.broadcasted_iota(jnp.int32, (count, count), 1)
    before = (earlier_of < later_of).astype(F32).astype(BF16)
    row = lax.broadcasted_iota(jnp.int32, (count, rows), 1).astype(F32)
    taken = jnp.zeros((experts, 1), F32)
    first = jnp.zeros(row.shape, F32)
    second = jnp.zeros(row.shape, F32)
    for k in range(top):
        expert = ids[k : k + 1, :]
        named = (expert_of == expert).astype(F32)
        earlier = jnp.dot(named.astype(BF16), before, preferred_element_type=F32) + taken
        rank = jnp.sum(earlier * named, axis=0, keepdims=True)
        taken = taken + jnp.sum(named, axis=1, keepdims=True)
        at = expert.astype(F32) * (2 * capacity) + rank
        at = jnp.sum(jnp.where(earlier_of == later_of, at, 0.0), axis=1, keepdims=True)
        first = first + (row == at).astype(F32)
        second = second + (row == at + capacity).astype(F32)
    out[:count, :] = first.astype(BF16)
    out[count:, :] = second.astype(BF16)


def gather_matrix(ids, capacity, experts):
    count = ids.shape[1]
    return pl.pallas_call(
        functools.partial(gather_kernel, capacity),
        out_shape=jax.ShapeDtypeStruct((2 * count, experts * 2 * capacity), BF16),
        compiler_params=params(8),
        name="gather_matrix",
    )(ids)


def tiles(x, group):
    return x.reshape(x.shape[0] // (8 * group), group, 8, x.shape[1])


def upper(shape):
    return lax.broadcasted_iota(jnp.int32, shape, 1) < 4


def split_rows(x):
    rows, columns = x.shape
    x = x.astype(F32)
    a, b = tiles(x, 6), tiles(pltpu.roll(x, 4, 0), 6)
    top = upper((rows // 48, 8, columns))
    first = [a[:, 0], jnp.where(top, a[:, 1], b[:, 3]), b[:, 4]]
    second = [b[:, 2], jnp.where(top, b[:, 3], a[:, 4]), a[:, 5]]
    return [
        jnp.concatenate([p[:, None] for p in parts], axis=1).reshape(rows // 2, columns).astype(BF16)
        for parts in (first, second)
    ]


def interleave(x, y):
    rows, columns = x.shape
    x0, x1, x2 = tiles(x, 3), tiles(pltpu.roll(x, 4, 0), 3), tiles(pltpu.roll(x, rows - 4, 0), 3)
    y0, y1 = tiles(y, 3), tiles(pltpu.roll(y, 4, 0), 3)
    shape = (rows // 24, 8, columns)
    parts = [
        x0[:, 0],
        jnp.where(upper(shape), x0[:, 1], y1[:, 0]),
        y1[:, 1],
        x1[:, 2],
        jnp.where(upper(shape), x2[:, 2], y0[:, 1]),
        y0[:, 2],
    ]
    return jnp.concatenate([p[:, None] for p in parts], axis=1).reshape(2 * rows, columns)


def start_all(copies):
    for copy in copies:
        copy.start()


def wait_all(copies):
    for copy in copies:
        copy.wait()


def chunk_copies(side, half, rows, gate, up, down, rows_in, gate_in, up_in, down_in, gate_at, sems):
    copies = []
    for i in range(half // DEPTH):
        local = pl.ds(i * DEPTH, DEPTH)
        at = pl.ds(pl.multiple_of(side * half + i * DEPTH, DEPTH), DEPTH)
        to = pl.ds(pl.multiple_of(gate_at + i * DEPTH, DEPTH), DEPTH)
        copy = [
            pltpu.make_async_copy(gate.at[at, :], gate_in.at[to, :], sems.at[i, 1]),
            pltpu.make_async_copy(up.at[at, :], up_in.at[to, :], sems.at[i, 2]),
            pltpu.make_async_copy(down.at[:, at], down_in.at[:, local], sems.at[i, 3]),
        ]
        if rows is not None:
            copy.append(pltpu.make_async_copy(rows.at[:, local], rows_in.at[:, local], sems.at[i, 0]))
        copies.append(copy)
    return copies


def project_half(copies, rows_in, gate_in, up_in, down_in, gate_at, accs, first, ahead):
    for i, copy in enumerate(copies):
        if i + AHEAD < len(copies):
            start_all(copies[i + AHEAD])
        elif ahead:
            start_all(ahead.pop(0))
        wait_all(copy)
        local = pl.ds(i * DEPTH, DEPTH)
        to = pl.ds(pl.multiple_of(gate_at + i * DEPTH, DEPTH), DEPTH)
        normed, routed = split_rows(rows_in[:, local])
        adds = (
            jnp.dot(normed, gate_in[to, :], preferred_element_type=F32),
            jnp.dot(normed, up_in[to, :], preferred_element_type=F32),
            lax.dot_general(routed, down_in[:, local], LAST, preferred_element_type=F32),
        )
        for acc, add in zip(accs, adds):
            acc[...] = add if first and i == 0 else acc[...] + add


def project_kernel(place, rows, gate, up, down, acc_gate, acc_up, acc_hidden, rows_in, gate_in, up_in, down_in, sems):
    half = rows.shape[1]
    copies = chunk_copies(place[0], half, rows, gate, up, down, rows_in, gate_in, up_in, down_in, 0, sems)
    for i in range(AHEAD):
        start_all(copies[i])
    project_half(copies, rows_in, gate_in, up_in, down_in, 0, (acc_gate, acc_up, acc_hidden), True, [])


def project(place, rows, weights):
    gate, up, down = weights
    height, half = rows.shape
    hidden = gate.shape[1]
    any_space = pl.BlockSpec(memory_space=pl.ANY)
    acc = jax.ShapeDtypeStruct((height // 2, hidden), F32)
    return pl.pallas_call(
        project_kernel,
        out_shape=(acc,) * 3,
        grid_spec=grid_of(
            (1,),
            [any_space] * 4,
            (whole(acc.shape),) * 3,
            [
                pltpu.VMEM((height, half), BF16),
                pltpu.VMEM((half, hidden), BF16),
                pltpu.VMEM((half, hidden), BF16),
                pltpu.VMEM((hidden, half), BF16),
                pltpu.SemaphoreType.DMA((half // DEPTH, 4)),
            ],
        ),
        compiler_params=params(32),
        name="project",
    )(place, rows, gate, up, down)


def expert_kernel(place, rows, gate, up, down, in_gate, in_up, in_hidden, theirs, mine, grad_gate, grad_up, product, gate_in, up_in, down_in, acc_gate, acc_up, acc_hidden, out, sems, more_sems, out_sems):
    half = rows.shape[1]
    core = place[0]
    side = 1 - core
    copies = chunk_copies(side, half, None, gate, up, down, None, gate_in, up_in, down_in, side * half, sems)
    rest = []
    for i in range(half // DEPTH):
        at = pl.ds(pl.multiple_of(core * half + i * DEPTH, DEPTH), DEPTH)
        rest.append(
            [
                pltpu.make_async_copy(gate.at[at, :], gate_in.at[at, :], more_sems.at[i, 0]),
                pltpu.make_async_copy(up.at[at, :], up_in.at[at, :], more_sems.at[i, 1]),
            ]
        )
    for i in range(AHEAD):
        start_all(copies[i])
    accs = (acc_gate, acc_up, acc_hidden)
    for acc, value in zip(accs, (in_gate, in_up, in_hidden)):
        acc[...] = value[...]
    ahead = list(rest)
    project_half(copies, rows, gate_in, up_in, down_in, side * half, accs, False, ahead)
    for copy in ahead:
        start_all(copy)

    pre_gate, pre_up, hidden = acc_gate[...], acc_up[...], acc_hidden[...]
    sigma = jax.nn.sigmoid(pre_gate)
    to_gate = hidden * pre_up * sigma * (1.0 + pre_gate * (1.0 - sigma))
    to_up = hidden * pre_gate * sigma
    total = jnp.sum(to_gate * pre_gate + to_up * pre_up, axis=1, keepdims=True)
    product[...] = jnp.broadcast_to(total, product.shape)
    grad_gate[...] = to_gate.astype(BF16)
    grad_up[...] = to_up.astype(BF16)
    for copy in rest:
        wait_all(copy)

    columns = gate.shape[0] // 4
    width = columns - DIRECT
    part = width // 2
    sent = []
    for slot, (to, whose) in enumerate(((theirs, side), (mine, core))):
        for turn, high in enumerate((place[1], 1 - place[1])):
            at = pl.ds(pl.multiple_of((2 * high + whose) * columns + DIRECT, LANES), width)
            rows_out = lax.dot_general(grad_gate[...], gate_in[at, :], LAST, preferred_element_type=F32)
            rows_out = rows_out + lax.dot_general(grad_up[...], up_in[at, :], LAST, preferred_element_type=F32)
            rows_out = interleave(rows_out[:, :part], rows_out[:, part:]).astype(BF16)
            out[slot, :, turn * part : (turn + 1) * part] = rows_out
        copy = pltpu.make_async_copy(out.at[slot], to, out_sems.at[slot])
        copy.start()
        sent.append(copy)
    wait_all(sent)


def expert(place, rows, weights, accs):
    gate, up, down = weights
    height, half = rows.shape
    width, hidden = gate.shape
    any_space = pl.BlockSpec(memory_space=pl.ANY)
    message = jax.ShapeDtypeStruct((height, width // 4 - DIRECT), BF16)
    acc = accs[0].shape
    grad = jax.ShapeDtypeStruct(acc, BF16)
    product = jax.ShapeDtypeStruct((acc[0], LANES), F32)
    return pl.pallas_call(
        expert_kernel,
        out_shape=(message, message, grad, grad, product),
        grid_spec=grid_of(
            (1,),
            [pl.BlockSpec(memory_space=pltpu.VMEM)] + [any_space] * 3 + [whole(acc)] * 3,
            (any_space, any_space, whole(acc), whole(acc), whole(product.shape)),
            [
                pltpu.VMEM((width, hidden), BF16),
                pltpu.VMEM((width, hidden), BF16),
                pltpu.VMEM((hidden, half), BF16),
                pltpu.VMEM(acc, F32),
                pltpu.VMEM(acc, F32),
                pltpu.VMEM(acc, F32),
                pltpu.VMEM((2,) + message.shape, BF16),
                pltpu.SemaphoreType.DMA((half // DEPTH, 4)),
                pltpu.SemaphoreType.DMA((half // DEPTH, 2)),
                pltpu.SemaphoreType.DMA((2,)),
            ],
        ),
        compiler_params=params(40),
        name="expert",
    )(place, rows, gate, up, down, *accs)


def direct_kernel(place, grad_gate, grad_up, product, gate, up, theirs, mine, gate_in, up_in, out, sems, out_sems):
    columns = gate.shape[0] // 4
    core = place[0]
    copies = []
    for slot, whose in enumerate((1 - core, core)):
        for high in range(2):
            at = pl.ds(pl.multiple_of((2 * high + whose) * columns, 256), DIRECT)
            to = 2 * slot + high
            copies.append(
                [
                    pltpu.make_async_copy(gate.at[at, :], gate_in.at[to], sems.at[to, 0]),
                    pltpu.make_async_copy(up.at[at, :], up_in.at[to], sems.at[to, 1]),
                ]
            )
    for copy in copies:
        start_all(copy)
    products = interleave(product[...], product[...]).astype(BF16)

    def one(index, at):
        part = slice(at, at + BACK)
        total = lax.dot_general(grad_gate[...], gate_in[index, part, :], LAST, preferred_element_type=F32)
        return total + lax.dot_general(grad_up[...], up_in[index, part, :], LAST, preferred_element_type=F32)

    sent = []
    for slot, to in enumerate((theirs, mine)):
        wait_all(copies[2 * slot])
        wait_all(copies[2 * slot + 1])
        for at in range(0, DIRECT, BACK):
            rows = interleave(one(2 * slot, at), one(2 * slot + 1, at))
            out[slot, :, at : at + BACK] = rows.astype(BF16)
        out[slot, :, DIRECT:] = products
        copy = pltpu.make_async_copy(out.at[slot], to, out_sems.at[slot])
        copy.start()
        sent.append(copy)
    wait_all(sent)


def direct_rows(place, grads, product, weights):
    gate, up, _ = weights
    rows, hidden = grads[0].shape
    any_space = pl.BlockSpec(memory_space=pl.ANY)
    message = jax.ShapeDtypeStruct((2 * rows, DIRECT + LANES), BF16)
    return pl.pallas_call(
        direct_kernel,
        out_shape=(message, message),
        grid_spec=grid_of(
            (1,),
            [whole((rows, hidden))] * 2 + [whole(product.shape)] + [any_space] * 2,
            (any_space, any_space),
            [
                pltpu.VMEM((4, DIRECT, hidden), BF16),
                pltpu.VMEM((4, DIRECT, hidden), BF16),
                pltpu.VMEM((2,) + message.shape, BF16),
                pltpu.SemaphoreType.DMA((4, 2)),
                pltpu.SemaphoreType.DMA((2,)),
            ],
        ),
        compiler_params=params(32),
        name="direct_rows",
    )(place, *grads, product, gate, up)


def merge_kernel(mine, other, kept, arrived, out):
    columns = mine.shape[1]
    out[:, :columns] = (mine[...].astype(F32) + other[...].astype(F32)).astype(BF16)
    out[:, columns:] = (kept[...] + arrived[...].astype(F32)).astype(BF16)


def merge(mine, other, kept, arrived):
    rows = mine.shape[0]
    block = rows // 4
    columns = mine.shape[1] + kept.shape[1]
    spec = lambda array: pl.BlockSpec((block, array.shape[1]), lambda i: (i, 0))
    return pl.pallas_call(
        merge_kernel,
        out_shape=jax.ShapeDtypeStruct((rows, columns), BF16),
        grid=(4,),
        in_specs=[spec(array) for array in (mine, other, kept, arrived)],
        out_specs=pl.BlockSpec((block, columns), lambda i: (i, 0)),
        compiler_params=params(12),
        name="merge",
    )(mine, other, kept, arrived)


def combine_kernel(place, gather, rows, first, second):
    count = first.shape[0]
    total = jnp.dot(gather[...], rows[...], preferred_element_type=F32)
    low, high = total[:count], total[count:]
    flip = place[1] == 1
    first[...] = jnp.where(flip, high, low).astype(first.dtype)
    second[...] = jnp.where(flip, low, high).astype(second.dtype)


def combine(place, gather, rows):
    count = gather.shape[0] // 2
    columns = DIRECT + LANES
    part = columns // 3
    block = pl.BlockSpec((count, part), lambda i, place: (0, i))
    return pl.pallas_call(
        combine_kernel,
        out_shape=(
            jax.ShapeDtypeStruct((count, columns), F32),
            jax.ShapeDtypeStruct((count, columns), BF16),
        ),
        grid_spec=grid_of(
            (3,),
            [whole(gather.shape), pl.BlockSpec((rows.shape[0], part), lambda i, place: (0, i))],
            (block, block),
        ),
        compiler_params=params(12),
        name="combine",
    )(place, gather, rows)


def final_kernel(width, place, gather, rows, kept, arrived, tokens, cotangent, gain, inverse, out):
    count = tokens.shape[0]
    total = jnp.dot(gather[...], rows[...], preferred_element_type=F32)
    direct = kept[...] + arrived[...].astype(F32)
    scale = inverse[...]
    product = scale * scale * direct[:, DIRECT : DIRECT + 1] / width
    half = rows.shape[1]
    for at, size, grad in (
        (0, DIRECT, direct[:, :DIRECT]),
        (DIRECT, half, total[:count]),
        (DIRECT + half, half, total[count:]),
    ):
        part = slice(at, at + size)
        value = cotangent[:, part].astype(F32) + scale * gain[:, part] * grad
        out[:, part] = (value - tokens[:, part].astype(F32) * product).astype(BF16)


def final(place, gather, rows, kept, arrived, tokens, cotangent, gain, inverse):
    count, width = tokens.shape
    columns = width // 4
    half = (columns - DIRECT) // 2
    quarter = lambda height: pl.BlockSpec((height, columns), lambda i, place: (0, place[2]))
    return pl.pallas_call(
        functools.partial(final_kernel, width),
        out_shape=jax.ShapeDtypeStruct((count, columns), BF16),
        grid_spec=grid_of(
            (1,),
            [
                whole(gather.shape),
                pl.BlockSpec((rows.shape[0], half), lambda i, place: (0, (DIRECT + LANES) // half)),
                whole(kept.shape),
                whole(arrived.shape),
            ]
            + [quarter(count), quarter(count), quarter(1), whole(inverse.shape)],
            whole((count, columns)),
        ),
        compiler_params=params(16),
        name="final",
    )(place, gather, rows, kept, arrived, tokens, cotangent, gain, inverse)


def body(tokens, cotangent, norm_gain, expert_ids, gate_weights, w_gate, w_up, w_down):
    experts = lax.axis_size("expert")
    token_count, width = tokens.shape
    top_count = expert_ids.shape[1]
    capacity = token_count * top_count * 3 // (2 * experts)
    pipe = lax.axis_index("pipe")
    place = jnp.stack([lax.rem(pipe, 2), pipe // 2, pipe]).astype(jnp.int32)
    weights = tuple(in_hbm(array[0]) for array in (w_gate, w_up, w_down))
    ids = in_hbm(expert_ids.T)
    tokens, cotangent, gain = in_hbm(tokens), in_hbm(cotangent), in_hbm(norm_gain.reshape(1, width))

    rows, inverse = make_message(
        place, tokens, cotangent, gain, ids, in_hbm(gate_weights.T), capacity, experts
    )
    gather = gather_matrix(ids, capacity, experts)
    rows, gather = lax.optimization_barrier((rows, gather))
    rows = exchange(rows)
    accs = project(place, rows, weights)
    theirs, mine, *grads, product = expert(place, core_swap(rows), weights, accs)
    summed = mine.astype(F32) + core_swap(theirs).astype(F32)
    half = summed.shape[1] // 2
    kept, sent = summed[:, :half], summed[:, half:].astype(BF16)
    kept, sent, product, *grads = lax.optimization_barrier((kept, sent, product, *grads))
    arrived = high_swap(sent)
    theirs, mine = direct_rows(place, grads, product, weights)
    theirs, arrived = lax.optimization_barrier((theirs, arrived))
    back = exchange(merge(mine, core_swap(theirs), kept, arrived))
    kept, sent = combine(place, gather, back)
    return final(place, gather, back, kept, high_swap(sent), tokens, cotangent, gain, inverse)


def solution(mesh):
    in_specs = (
        P("expert", None),
        P("expert", None),
        P(),
        P("expert", None),
        P("expert", None),
        P("expert", None, "pipe"),
        P("expert", None, "pipe"),
        P("expert", "pipe", None),
    )
    out_specs = P("expert", "pipe")
    return jax.shard_map(body, mesh=mesh, in_specs=in_specs, out_specs=out_specs, check_vma=False)
```

```python
import functools

import jax
import jax.numpy as jnp
from jax import lax
from jax.experimental import pallas as pl
from jax.experimental.pallas import tpu as pltpu
from jax.sharding import PartitionSpec as P

EPSILON = 1e-06
BF16 = jnp.bfloat16
F32 = jnp.float32
MIB = 1024 * 1024
FILL = 1792
DEPTH = 1792
BACK = 896
LANES = 128
LAST = (((1,), (1,)), ((), ()))
CORE_SWAP = [(0, 1), (1, 0), (2, 3), (3, 2)]
HIGH_SWAP = [(0, 2), (2, 0), (1, 3), (3, 1)]


def params(mebibytes):
    return pltpu.CompilerParams(vmem_limit_bytes=mebibytes * MIB)


def in_hbm(array):
    return pltpu.with_memory_space_constraint(array, pltpu.HBM)


def whole(shape):
    return pl.BlockSpec(shape, lambda *_: (0,) * len(shape))


def grid_of(grid, in_specs, out_specs, scratch=()):
    return pltpu.PrefetchScalarGridSpec(
        num_scalar_prefetch=1, grid=grid, in_specs=in_specs, out_specs=out_specs, scratch_shapes=scratch
    )


def core_swap(array):
    return lax.ppermute(array, "pipe", CORE_SWAP)


def high_swap(array):
    return lax.ppermute(array, "pipe", HIGH_SWAP)


def exchange(rows):
    experts = lax.axis_size("expert")
    shaped = rows.reshape(experts, rows.shape[0] // experts, rows.shape[1])
    return lax.all_to_all(shaped, "expert", split_axis=0, concat_axis=0, tiled=True).reshape(rows.shape)


def message_kernel(capacity, place, all_tokens, tokens, cotangent, gain, ids, weights, rows, inverse, select, factors):
    top, count = ids.shape

    @pl.when(pl.program_id(0) == 0)
    def _():
        height = select.shape[0]
        experts = height // (2 * capacity)
        expert_of = lax.broadcasted_iota(jnp.int32, (experts, count), 0)
        earlier_of = lax.broadcasted_iota(jnp.int32, (count, count), 0)
        later_of = lax.broadcasted_iota(jnp.int32, (count, count), 1)
        before = (earlier_of < later_of).astype(F32).astype(BF16)
        row = lax.broadcasted_iota(jnp.int32, (height, count), 0)
        taken = jnp.zeros((experts, 1), F32)
        normed_part = jnp.zeros(row.shape, F32)
        for k in range(top):
            expert = ids[k : k + 1, :]
            named = (expert_of == expert).astype(F32)
            earlier = jnp.dot(named.astype(BF16), before, preferred_element_type=F32) + taken
            rank = jnp.sum(earlier * named, axis=0, keepdims=True).astype(jnp.int32)
            taken = taken + jnp.sum(named, axis=1, keepdims=True)
            at = expert * (2 * capacity) + rank
            normed_part = normed_part + (row == at).astype(F32)
            select[:, (k + 1) * count : (k + 2) * count] = (row == at + capacity).astype(F32).astype(BF16)
            column = jnp.sum(jnp.where(earlier_of == later_of, weights[k : k + 1, :], 0.0), axis=1, keepdims=True)
            factors[:, k : k + 1] = column
        select[:, :count] = normed_part.astype(BF16)
        values = all_tokens[...].astype(F32)
        inverse[...] = lax.rsqrt(jnp.mean(values * values, axis=1, keepdims=True) + EPSILON)

    normed = (tokens[...].astype(F32) * inverse[...] * gain[...]).astype(BF16)
    values = cotangent[...].astype(F32)
    parts = [normed] + [(factors[:, k : k + 1] * values).astype(BF16) for k in range(top)]
    rows[...] = jnp.dot(select[...], jnp.concatenate(parts, axis=0), preferred_element_type=F32).astype(BF16)


def make_message(place, tokens, cotangent, gain, ids, weights, capacity, experts):
    count, width = tokens.shape
    top = ids.shape[0]
    half = width // 2
    height = experts * 2 * capacity
    steps = half // FILL
    column = lambda i, place: (0, place[0] * steps + i)
    return pl.pallas_call(
        functools.partial(message_kernel, capacity),
        out_shape=(jax.ShapeDtypeStruct((height, half), BF16), jax.ShapeDtypeStruct((count, 1), F32)),
        grid_spec=grid_of(
            (steps,),
            [
                whole((count, width)),
                pl.BlockSpec((count, FILL), column),
                pl.BlockSpec((count, FILL), column),
                pl.BlockSpec((1, FILL), column),
                whole(ids.shape),
                whole(weights.shape),
            ],
            (pl.BlockSpec((height, FILL), lambda i, place: (0, i)), whole((count, 1))),
            [pltpu.VMEM((height, (top + 1) * count), BF16), pltpu.VMEM((count, top), F32)],
        ),
        compiler_params=params(32),
        name="message",
    )(place, tokens, tokens, cotangent, gain, ids, weights)


def gather_kernel(capacity, ids, out):
    top, count = ids.shape
    rows = out.shape[1]
    experts = rows // (2 * capacity)
    expert_of = lax.broadcasted_iota(jnp.int32, (experts, count), 0)
    earlier_of = lax.broadcasted_iota(jnp.int32, (count, count), 0)
    later_of = lax.broadcasted_iota(jnp.int32, (count, count), 1)
    before = (earlier_of < later_of).astype(F32).astype(BF16)
    row = lax.broadcasted_iota(jnp.int32, (count, rows), 1).astype(F32)
    taken = jnp.zeros((experts, 1), F32)
    first = jnp.zeros(row.shape, F32)
    second = jnp.zeros(row.shape, F32)
    for k in range(top):
        expert = ids[k : k + 1, :]
        named = (expert_of == expert).astype(F32)
        earlier = jnp.dot(named.astype(BF16), before, preferred_element_type=F32) + taken
        rank = jnp.sum(earlier * named, axis=0, keepdims=True)
        taken = taken + jnp.sum(named, axis=1, keepdims=True)
        at = expert.astype(F32) * (2 * capacity) + rank
        at = jnp.sum(jnp.where(earlier_of == later_of, at, 0.0), axis=1, keepdims=True)
        first = first + (row == at).astype(F32)
        second = second + (row == at + capacity).astype(F32)
    out[:count, :] = first.astype(BF16)
    out[count:, :] = second.astype(BF16)


def gather_matrix(ids, capacity, experts):
    count = ids.shape[1]
    return pl.pallas_call(
        functools.partial(gather_kernel, capacity),
        out_shape=jax.ShapeDtypeStruct((2 * count, experts * 2 * capacity), BF16),
        compiler_params=params(8),
        name="gather_matrix",
    )(ids)


def tiles(x, group):
    return x.reshape(x.shape[0] // (8 * group), group, 8, x.shape[1])


def upper(shape):
    return lax.broadcasted_iota(jnp.int32, shape, 1) < 4


def split_rows(x):
    rows, columns = x.shape
    x = x.astype(F32)
    a, b = tiles(x, 6), tiles(pltpu.roll(x, 4, 0), 6)
    top = upper((rows // 48, 8, columns))
    first = [a[:, 0], jnp.where(top, a[:, 1], b[:, 3]), b[:, 4]]
    second = [b[:, 2], jnp.where(top, b[:, 3], a[:, 4]), a[:, 5]]
    return [
        jnp.concatenate([p[:, None] for p in parts], axis=1).reshape(rows // 2, columns).astype(BF16)
        for parts in (first, second)
    ]


def interleave(x, y):
    rows, columns = x.shape
    x0, x1, x2 = tiles(x, 3), tiles(pltpu.roll(x, 4, 0), 3), tiles(pltpu.roll(x, rows - 4, 0), 3)
    y0, y1 = tiles(y, 3), tiles(pltpu.roll(y, 4, 0), 3)
    shape = (rows // 24, 8, columns)
    parts = [
        x0[:, 0],
        jnp.where(upper(shape), x0[:, 1], y1[:, 0]),
        y1[:, 1],
        x1[:, 2],
        jnp.where(upper(shape), x2[:, 2], y0[:, 1]),
        y0[:, 2],
    ]
    return jnp.concatenate([p[:, None] for p in parts], axis=1).reshape(2 * rows, columns)


def project_half(rows, gate, up, down, down_in, sems, side, accs, first):
    half = rows.shape[1]
    copies = []
    for i in range(half // DEPTH):
        at = pl.ds(pl.multiple_of(side * half + i * DEPTH, DEPTH), DEPTH)
        to = pl.ds(i * DEPTH, DEPTH)
        copies.append(pltpu.make_async_copy(down.at[:, at], down_in.at[:, to], sems.at[i]))
        copies[i].start()
    for i in range(half // DEPTH):
        at = pl.ds(pl.multiple_of(side * half + i * DEPTH, DEPTH), DEPTH)
        to = slice(i * DEPTH, (i + 1) * DEPTH)
        normed, routed = split_rows(rows[:, to])
        to_gate = jnp.dot(normed, gate[at, :], preferred_element_type=F32)
        to_up = jnp.dot(normed, up[at, :], preferred_element_type=F32)
        copies[i].wait()
        to_hidden = lax.dot_general(routed, down_in[:, to], LAST, preferred_element_type=F32)
        for acc, add in zip(accs, (to_gate, to_up, to_hidden)):
            acc[...] = add if first and i == 0 else acc[...] + add


def back_rows(place, side, grad_gate, grad_up, gate, up, out):
    columns = out.shape[1]

    def one(start):
        at = pl.ds(pl.multiple_of(start, LANES), BACK)
        total = lax.dot_general(grad_gate[...], gate[at, :], LAST, preferred_element_type=F32)
        return total + lax.dot_general(grad_up[...], up[at, :], LAST, preferred_element_type=F32)

    for at in range(0, columns, BACK):
        rows = interleave(one(side * columns + at), one((2 + side) * columns + at))
        out[:, at : at + BACK] = rows.astype(BF16)


def down_scratch(half, hidden):
    return [pltpu.VMEM((hidden, half), BF16), pltpu.SemaphoreType.DMA((half // DEPTH,))]


def project_kernel(place, rows, gate, up, down, acc_gate, acc_up, acc_hidden, down_in, sems):
    project_half(rows, gate, up, down, down_in, sems, place[0], (acc_gate, acc_up, acc_hidden), True)


def project(place, rows, weights):
    acc = jax.ShapeDtypeStruct((rows.shape[0] // 2, weights[0].shape[1]), F32)
    resident = pl.BlockSpec(memory_space=pltpu.VMEM)
    return pl.pallas_call(
        project_kernel,
        out_shape=(acc,) * 3,
        grid_spec=grid_of(
            (1,),
            [resident] * 3 + [pl.BlockSpec(memory_space=pl.ANY)],
            (resident,) * 3,
            down_scratch(rows.shape[1], acc.shape[1]),
        ),
        compiler_params=params(20),
        name="project",
    )(place, rows, *weights)


def expert_kernel(place, rows, gate, up, down, in_gate, in_up, in_hidden, theirs, grad_gate, grad_up, acc_gate, acc_up, acc_hidden, down_in, sems):
    side = 1 - place[0]
    accs = (acc_gate, acc_up, acc_hidden)
    for acc, value in zip(accs, (in_gate, in_up, in_hidden)):
        acc[...] = value[...]
    project_half(rows, gate, up, down, down_in, sems, side, accs, False)
    pre_gate, pre_up, hidden = acc_gate[...], acc_up[...], acc_hidden[...]
    sigma = jax.nn.sigmoid(pre_gate)
    grad_gate[...] = (hidden * pre_up * sigma * (1.0 + pre_gate * (1.0 - sigma))).astype(BF16)
    grad_up[...] = (hidden * pre_gate * sigma).astype(BF16)
    back_rows(place, side, grad_gate, grad_up, gate, up, theirs)


def expert(place, rows, weights, accs):
    height = rows.shape[0]
    acc = accs[0].shape
    grad = jax.ShapeDtypeStruct(acc, BF16)
    resident = pl.BlockSpec(memory_space=pltpu.VMEM)
    return pl.pallas_call(
        expert_kernel,
        out_shape=(jax.ShapeDtypeStruct((height, weights[0].shape[0] // 4), BF16), grad, grad),
        grid_spec=grid_of(
            (1,),
            [resident] * 3 + [pl.BlockSpec(memory_space=pl.ANY)] + [resident] * 3,
            (resident,) * 3,
            [pltpu.VMEM(acc, F32)] * 3 + down_scratch(rows.shape[1], acc[1]),
        ),
        compiler_params=params(24),
        name="expert",
    )(place, rows, *weights, *accs)


def mine_kernel(place, grad_gate, grad_up, gate, up, mine):
    back_rows(place, place[0], grad_gate, grad_up, gate, up, mine)


def mine_rows(place, grads, weights):
    gate, up, _ = weights
    resident = pl.BlockSpec(memory_space=pltpu.VMEM)
    return pl.pallas_call(
        mine_kernel,
        out_shape=jax.ShapeDtypeStruct((2 * grads[0].shape[0], gate.shape[0] // 4), BF16),
        grid_spec=grid_of((1,), [resident] * 4, resident),
        compiler_params=params(16),
        name="mine_rows",
    )(place, *grads, gate, up)


def merge_kernel(mine, other, out):
    out[...] = (mine[...].astype(F32) + other[...].astype(F32)).astype(BF16)


def merge(mine, other):
    rows, columns = mine.shape
    spec = pl.BlockSpec((rows // 4, columns), lambda i: (i, 0))
    return pl.pallas_call(
        merge_kernel,
        out_shape=jax.ShapeDtypeStruct((rows, columns), BF16),
        grid=(4,),
        in_specs=[spec, spec],
        out_specs=spec,
        compiler_params=params(12),
        name="merge",
    )(mine, other)


def combine_kernel(place, gather, rows, tokens_0, tokens_1, gain_0, gain_1, kept, sent, product):
    count = kept.shape[0]
    total = jnp.dot(gather[...], rows[...], preferred_element_type=F32)
    low, high = total[:count], total[count:]
    flip = place[1] == 1
    kept[...] = jnp.where(flip, high, low)
    sent[...] = jnp.where(flip, low, high).astype(BF16)
    part = low * (tokens_0[...].astype(F32) * gain_0[...]) + high * (tokens_1[...].astype(F32) * gain_1[...])
    part = jnp.broadcast_to(jnp.sum(part, axis=1, keepdims=True), product.shape)

    @pl.when(pl.program_id(0) == 0)
    def _():
        product[...] = part

    @pl.when(pl.program_id(0) > 0)
    def _():
        product[...] += part


def combine(place, gather, rows, tokens, gain):
    count = gather.shape[0] // 2
    height, columns = rows.shape
    steps = 2
    part = columns // steps
    block = pl.BlockSpec((count, part), lambda i, place: (0, i))

    def quarter(size, high):
        return pl.BlockSpec((size, part), lambda i, place: (0, (2 * high + place[0]) * steps + i))

    return pl.pallas_call(
        combine_kernel,
        out_shape=(
            jax.ShapeDtypeStruct((count, columns), F32),
            jax.ShapeDtypeStruct((count, columns), BF16),
            jax.ShapeDtypeStruct((count, LANES), F32),
        ),
        grid_spec=grid_of(
            (steps,),
            [
                whole(gather.shape),
                pl.BlockSpec((height, part), lambda i, place: (0, i)),
                quarter(count, 0),
                quarter(count, 1),
                quarter(1, 0),
                quarter(1, 1),
            ],
            (block, block, whole((count, LANES))),
        ),
        compiler_params=params(16),
        name="combine",
    )(place, gather, rows, tokens, tokens, gain, gain)


def final_kernel(width, place, kept, arrived, own_product, other_product, tokens, cotangent, gain, inverse, out):
    scale = inverse[...]
    row_product = own_product[:, :1] + other_product[:, :1]
    grad = kept[...] + arrived[...].astype(F32)
    value = cotangent[...].astype(F32) + scale * gain[...] * grad
    out[...] = (value - tokens[...].astype(F32) * (scale * scale * scale * row_product / width)).astype(BF16)


def final(place, kept, arrived, own_product, other_product, tokens, cotangent, gain, inverse):
    count, width = tokens.shape
    columns = width // 4
    quarter = lambda height: pl.BlockSpec((height, columns), lambda i, place: (0, place[2]))
    return pl.pallas_call(
        functools.partial(final_kernel, width),
        out_shape=jax.ShapeDtypeStruct((count, columns), BF16),
        grid_spec=grid_of(
            (1,),
            [whole(array.shape) for array in (kept, arrived, own_product, other_product)]
            + [quarter(count), quarter(count), quarter(1), whole(inverse.shape)],
            whole((count, columns)),
        ),
        compiler_params=params(16),
        name="final",
    )(place, kept, arrived, own_product, other_product, tokens, cotangent, gain, inverse)


def body(tokens, cotangent, norm_gain, expert_ids, gate_weights, w_gate, w_up, w_down):
    experts = lax.axis_size("expert")
    token_count, width = tokens.shape
    top_count = expert_ids.shape[1]
    capacity = token_count * top_count * 3 // (2 * experts)
    pipe = lax.axis_index("pipe")
    place = jnp.stack([lax.rem(pipe, 2), pipe // 2, pipe]).astype(jnp.int32)
    weights = (w_gate[0], w_up[0], in_hbm(w_down[0]))
    ids = in_hbm(expert_ids.T)
    tokens, cotangent, gain = in_hbm(tokens), in_hbm(cotangent), in_hbm(norm_gain.reshape(1, width))

    rows, inverse = make_message(
        place, tokens, cotangent, gain, ids, in_hbm(gate_weights.T), capacity, experts
    )
    rows, ids = lax.optimization_barrier((exchange(rows), ids))
    accs = project(place, rows, weights)
    theirs, *grads = expert(place, core_swap(rows), weights, accs)
    back = merge(mine_rows(place, grads, weights), core_swap(theirs))
    back, gather = lax.optimization_barrier((back, gather_matrix(ids, capacity, experts)))
    kept, sent, product = combine(place, gather, exchange(back), tokens, gain)
    product = product + core_swap(product)
    return final(
        place, kept, high_swap(sent), product, high_swap(product), tokens, cotangent, gain, inverse
    )


def solution(mesh):
    in_specs = (
        P("expert", None),
        P("expert", None),
        P(),
        P("expert", None),
        P("expert", None),
        P("expert", None, "pipe"),
        P("expert", None, "pipe"),
        P("expert", "pipe", None),
    )
    out_specs = P("expert", "pipe")
    return jax.shard_map(body, mesh=mesh, in_specs=in_specs, out_specs=out_specs, check_vma=False)
```

```python
import functools

import jax
import jax.numpy as jnp
from jax import lax
from jax.experimental import pallas as pl
from jax.experimental.pallas import tpu as pltpu
from jax.sharding import PartitionSpec as P

EPSILON = 1e-06
BF16 = jnp.bfloat16
F32 = jnp.float32
MIB = 1024 * 1024
FILL = 1792
DEPTH = 1792
BACK = 896
LANES = 128
LAST = (((1,), (1,)), ((), ()))
CORE_SWAP = [(0, 1), (1, 0), (2, 3), (3, 2)]
HIGH_SWAP = [(0, 2), (2, 0), (1, 3), (3, 1)]


def params(mebibytes):
    return pltpu.CompilerParams(vmem_limit_bytes=mebibytes * MIB)


def in_hbm(array):
    return pltpu.with_memory_space_constraint(array, pltpu.HBM)


def whole(shape):
    return pl.BlockSpec(shape, lambda *_: (0,) * len(shape))


def grid_of(grid, in_specs, out_specs, scratch=()):
    return pltpu.PrefetchScalarGridSpec(
        num_scalar_prefetch=1, grid=grid, in_specs=in_specs, out_specs=out_specs, scratch_shapes=scratch
    )


def core_swap(array):
    return lax.ppermute(array, "pipe", CORE_SWAP)


def high_swap(array):
    return lax.ppermute(array, "pipe", HIGH_SWAP)


def exchange(rows):
    experts = lax.axis_size("expert")
    shaped = rows.reshape(experts, rows.shape[0] // experts, rows.shape[1])
    return lax.all_to_all(shaped, "expert", split_axis=0, concat_axis=0, tiled=True).reshape(rows.shape)


def message_kernel(capacity, place, all_tokens, tokens, cotangent, gain, ids, weights, rows, inverse, select, factors):
    top, count = ids.shape

    @pl.when(pl.program_id(0) == 0)
    def _():
        height = select.shape[0]
        experts = height // (2 * capacity)
        expert_of = lax.broadcasted_iota(jnp.int32, (experts, count), 0)
        earlier_of = lax.broadcasted_iota(jnp.int32, (count, count), 0)
        later_of = lax.broadcasted_iota(jnp.int32, (count, count), 1)
        before = (earlier_of < later_of).astype(F32).astype(BF16)
        row = lax.broadcasted_iota(jnp.int32, (height, count), 0)
        taken = jnp.zeros((experts, 1), F32)
        normed_part = jnp.zeros(row.shape, F32)
        routed_part = jnp.zeros(row.shape, F32)
        factor = jnp.zeros(row.shape, F32)
        for k in range(top):
            expert = ids[k : k + 1, :]
            named = (expert_of == expert).astype(F32)
            earlier = jnp.dot(named.astype(BF16), before, preferred_element_type=F32) + taken
            rank = jnp.sum(earlier * named, axis=0, keepdims=True).astype(jnp.int32)
            taken = taken + jnp.sum(named, axis=1, keepdims=True)
            at = expert * (2 * capacity) + rank
            hit = row == at
            hit_routed = row == at + capacity
            normed_part = jnp.where(hit, 1.0, normed_part)
            routed_part = jnp.where(hit_routed, 1.0, routed_part)
            factor = jnp.where(hit, 1.0, jnp.where(hit_routed, weights[k : k + 1, :], factor))
        select[:, :count] = normed_part.astype(BF16)
        select[:, count:] = routed_part.astype(BF16)
        factors[...] = jnp.broadcast_to(jnp.sum(factor, axis=1, keepdims=True), factors.shape)
        values = all_tokens[...].astype(F32)
        inverse[...] = lax.rsqrt(jnp.mean(values * values, axis=1, keepdims=True) + EPSILON)

    normed = (tokens[...].astype(F32) * inverse[...] * gain[...]).astype(BF16)
    both = jnp.concatenate([normed, cotangent[...]], axis=0)
    picked = jnp.dot(select[...], both, preferred_element_type=F32)
    rows[...] = (picked * factors[:, :1]).astype(BF16)


def make_message(place, tokens, cotangent, gain, ids, weights, capacity, experts):
    count, width = tokens.shape
    half = width // 2
    height = experts * 2 * capacity
    steps = half // FILL
    column = lambda i, place: (0, place[0] * steps + i)
    return pl.pallas_call(
        functools.partial(message_kernel, capacity),
        out_shape=(jax.ShapeDtypeStruct((height, half), BF16), jax.ShapeDtypeStruct((count, 1), F32)),
        grid_spec=grid_of(
            (steps,),
            [
                whole((count, width)),
                pl.BlockSpec((count, FILL), column),
                pl.BlockSpec((count, FILL), column),
                pl.BlockSpec((1, FILL), column),
                whole(ids.shape),
                whole(weights.shape),
            ],
            (pl.BlockSpec((height, FILL), lambda i, place: (0, i)), whole((count, 1))),
            [pltpu.VMEM((height, 2 * count), BF16), pltpu.VMEM((height, LANES), F32)],
        ),
        compiler_params=params(32),
        name="message",
    )(place, tokens, tokens, cotangent, gain, ids, weights)


def gather_kernel(capacity, ids, out):
    top, count = ids.shape
    rows = out.shape[1]
    experts = rows // (2 * capacity)
    expert_of = lax.broadcasted_iota(jnp.int32, (experts, count), 0)
    earlier_of = lax.broadcasted_iota(jnp.int32, (count, count), 0)
    later_of = lax.broadcasted_iota(jnp.int32, (count, count), 1)
    before = (earlier_of < later_of).astype(F32).astype(BF16)
    row = lax.broadcasted_iota(jnp.int32, (count, rows), 1).astype(F32)
    taken = jnp.zeros((experts, 1), F32)
    first = jnp.zeros(row.shape, F32)
    second = jnp.zeros(row.shape, F32)
    for k in range(top):
        expert = ids[k : k + 1, :]
        named = (expert_of == expert).astype(F32)
        earlier = jnp.dot(named.astype(BF16), before, preferred_element_type=F32) + taken
        rank = jnp.sum(earlier * named, axis=0, keepdims=True)
        taken = taken + jnp.sum(named, axis=1, keepdims=True)
        at = expert.astype(F32) * (2 * capacity) + rank
        at = jnp.sum(jnp.where(earlier_of == later_of, at, 0.0), axis=1, keepdims=True)
        first = first + (row == at).astype(F32)
        second = second + (row == at + capacity).astype(F32)
    out[:count, :] = first.astype(BF16)
    out[count:, :] = second.astype(BF16)


def gather_matrix(ids, capacity, experts):
    count = ids.shape[1]
    return pl.pallas_call(
        functools.partial(gather_kernel, capacity),
        out_shape=jax.ShapeDtypeStruct((2 * count, experts * 2 * capacity), BF16),
        compiler_params=params(8),
        name="gather_matrix",
    )(ids)


def tiles(x, group):
    return x.reshape(x.shape[0] // (8 * group), group, 8, x.shape[1])


def upper(shape):
    return lax.broadcasted_iota(jnp.int32, shape, 1) < 4


def split_rows(x):
    rows, columns = x.shape
    x = x.astype(F32)
    a, b = tiles(x, 6), tiles(pltpu.roll(x, 4, 0), 6)
    top = upper((rows // 48, 8, columns))
    first = [a[:, 0], jnp.where(top, a[:, 1], b[:, 3]), b[:, 4]]
    second = [b[:, 2], jnp.where(top, b[:, 3], a[:, 4]), a[:, 5]]
    return [
        jnp.concatenate([p[:, None] for p in parts], axis=1).reshape(rows // 2, columns).astype(BF16)
        for parts in (first, second)
    ]


def interleave(x, y):
    rows, columns = x.shape
    x0, x1, x2 = tiles(x, 3), tiles(pltpu.roll(x, 4, 0), 3), tiles(pltpu.roll(x, rows - 4, 0), 3)
    y0, y1 = tiles(y, 3), tiles(pltpu.roll(y, 4, 0), 3)
    shape = (rows // 24, 8, columns)
    parts = [
        x0[:, 0],
        jnp.where(upper(shape), x0[:, 1], y1[:, 0]),
        y1[:, 1],
        x1[:, 2],
        jnp.where(upper(shape), x2[:, 2], y0[:, 1]),
        y0[:, 2],
    ]
    return jnp.concatenate([p[:, None] for p in parts], axis=1).reshape(2 * rows, columns)


def project_half(rows, gate, up, down, down_in, sems, side, accs, first):
    half = rows.shape[1]
    copies = []
    for i in range(half // DEPTH):
        at = pl.ds(pl.multiple_of(side * half + i * DEPTH, DEPTH), DEPTH)
        to = pl.ds(i * DEPTH, DEPTH)
        copies.append(pltpu.make_async_copy(down.at[:, at], down_in.at[:, to], sems.at[i]))
        copies[i].start()
    for i in range(half // DEPTH):
        at = pl.ds(pl.multiple_of(side * half + i * DEPTH, DEPTH), DEPTH)
        to = slice(i * DEPTH, (i + 1) * DEPTH)
        normed, routed = split_rows(rows[:, to])
        to_gate = jnp.dot(normed, gate[at, :], preferred_element_type=F32)
        to_up = jnp.dot(normed, up[at, :], preferred_element_type=F32)
        copies[i].wait()
        to_hidden = lax.dot_general(routed, down_in[:, to], LAST, preferred_element_type=F32)
        for acc, add in zip(accs, (to_gate, to_up, to_hidden)):
            acc[...] = add if first and i == 0 else acc[...] + add


def back_rows(place, side, grad_gate, grad_up, gate, up, out):
    columns = out.shape[1]

    def one(start):
        at = pl.ds(pl.multiple_of(start, LANES), BACK)
        total = lax.dot_general(grad_gate[...], gate[at, :], LAST, preferred_element_type=F32)
        return total + lax.dot_general(grad_up[...], up[at, :], LAST, preferred_element_type=F32)

    for at in range(0, columns, BACK):
        rows = interleave(one(side * columns + at), one((2 + side) * columns + at))
        out[:, at : at + BACK] = rows.astype(BF16)


def down_scratch(half, hidden):
    return [pltpu.VMEM((hidden, half), BF16), pltpu.SemaphoreType.DMA((half // DEPTH,))]


def project_kernel(place, rows, gate, up, down, acc_gate, acc_up, acc_hidden, down_in, sems):
    project_half(rows, gate, up, down, down_in, sems, place[0], (acc_gate, acc_up, acc_hidden), True)


def project(place, rows, weights):
    acc = jax.ShapeDtypeStruct((rows.shape[0] // 2, weights[0].shape[1]), F32)
    resident = pl.BlockSpec(memory_space=pltpu.VMEM)
    return pl.pallas_call(
        project_kernel,
        out_shape=(acc,) * 3,
        grid_spec=grid_of(
            (1,),
            [resident] * 3 + [pl.BlockSpec(memory_space=pl.ANY)],
            (resident,) * 3,
            down_scratch(rows.shape[1], acc.shape[1]),
        ),
        compiler_params=params(20),
        name="project",
    )(place, rows, *weights)


def expert_kernel(place, rows, gate, up, down, in_gate, in_up, in_hidden, theirs, grad_gate, grad_up, acc_gate, acc_up, acc_hidden, down_in, sems):
    side = 1 - place[0]
    accs = (acc_gate, acc_up, acc_hidden)
    for acc, value in zip(accs, (in_gate, in_up, in_hidden)):
        acc[...] = value[...]
    project_half(rows, gate, up, down, down_in, sems, side, accs, False)
    pre_gate, pre_up, hidden = acc_gate[...], acc_up[...], acc_hidden[...]
    sigma = jax.nn.sigmoid(pre_gate)
    grad_gate[...] = (hidden * pre_up * sigma * (1.0 + pre_gate * (1.0 - sigma))).astype(BF16)
    grad_up[...] = (hidden * pre_gate * sigma).astype(BF16)
    back_rows(place, side, grad_gate, grad_up, gate, up, theirs)


def expert(place, rows, weights, accs):
    height = rows.shape[0]
    acc = accs[0].shape
    grad = jax.ShapeDtypeStruct(acc, BF16)
    resident = pl.BlockSpec(memory_space=pltpu.VMEM)
    return pl.pallas_call(
        expert_kernel,
        out_shape=(jax.ShapeDtypeStruct((height, weights[0].shape[0] // 4), BF16), grad, grad),
        grid_spec=grid_of(
            (1,),
            [resident] * 3 + [pl.BlockSpec(memory_space=pl.ANY)] + [resident] * 3,
            (resident,) * 3,
            [pltpu.VMEM(acc, F32)] * 3 + down_scratch(rows.shape[1], acc[1]),
        ),
        compiler_params=params(24),
        name="expert",
    )(place, rows, *weights, *accs)


def mine_kernel(place, grad_gate, grad_up, gate, up, mine):
    back_rows(place, place[0], grad_gate, grad_up, gate, up, mine)


def mine_rows(place, grads, weights):
    gate, up, _ = weights
    resident = pl.BlockSpec(memory_space=pltpu.VMEM)
    return pl.pallas_call(
        mine_kernel,
        out_shape=jax.ShapeDtypeStruct((2 * grads[0].shape[0], gate.shape[0] // 4), BF16),
        grid_spec=grid_of((1,), [resident] * 4, resident),
        compiler_params=params(16),
        name="mine_rows",
    )(place, *grads, gate, up)


def merge_kernel(mine, other, out):
    out[...] = (mine[...].astype(F32) + other[...].astype(F32)).astype(BF16)


def merge(mine, other):
    rows, columns = mine.shape
    spec = pl.BlockSpec((rows // 4, columns), lambda i: (i, 0))
    return pl.pallas_call(
        merge_kernel,
        out_shape=jax.ShapeDtypeStruct((rows, columns), BF16),
        grid=(4,),
        in_specs=[spec, spec],
        out_specs=spec,
        compiler_params=params(12),
        name="merge",
    )(mine, other)


def combine_kernel(place, gather, rows, kept, sent):
    count = kept.shape[0]
    total = jnp.dot(gather[...], rows[...], preferred_element_type=F32)
    low, high = total[:count], total[count:]
    flip = place[1] == 1
    kept[...] = jnp.where(flip, high, low)
    sent[...] = jnp.where(flip, low, high).astype(BF16)


def combine(place, gather, rows):
    count = gather.shape[0] // 2
    height, columns = rows.shape
    steps = 2
    part = columns // steps
    block = pl.BlockSpec((count, part), lambda i, place: (0, i))
    return pl.pallas_call(
        combine_kernel,
        out_shape=(jax.ShapeDtypeStruct((count, columns), F32), jax.ShapeDtypeStruct((count, columns), BF16)),
        grid_spec=grid_of(
            (steps,),
            [whole(gather.shape), pl.BlockSpec((height, part), lambda i, place: (0, i))],
            (block, block),
        ),
        compiler_params=params(16),
        name="combine",
    )(place, gather, rows)


def product_kernel(place, kept, sent, own_tokens, other_tokens, own_gain, other_gain, product):
    part = kept[...] * (own_tokens[...].astype(F32) * own_gain[...])
    part = part + sent[...].astype(F32) * (other_tokens[...].astype(F32) * other_gain[...])
    product[...] = jnp.broadcast_to(jnp.sum(part, axis=1, keepdims=True), product.shape)


def row_products(place, kept, sent, tokens, gain):
    count, columns = kept.shape

    def quarter(size, other):
        def index(i, place):
            high = 1 - place[1] if other else place[1]
            return (0, 2 * high + place[0])

        return pl.BlockSpec((size, columns), index)

    return pl.pallas_call(
        product_kernel,
        out_shape=jax.ShapeDtypeStruct((count, LANES), F32),
        grid_spec=grid_of(
            (1,),
            [whole(kept.shape), whole(sent.shape)]
            + [quarter(count, False), quarter(count, True), quarter(1, False), quarter(1, True)],
            whole((count, LANES)),
        ),
        compiler_params=params(16),
        name="row_products",
    )(place, kept, sent, tokens, tokens, gain, gain)


def final_kernel(width, place, kept, arrived, own_product, other_product, tokens, cotangent, gain, inverse, out):
    scale = inverse[...]
    row_product = own_product[:, :1] + other_product[:, :1]
    grad = kept[...] + arrived[...].astype(F32)
    value = cotangent[...].astype(F32) + scale * gain[...] * grad
    out[...] = (value - tokens[...].astype(F32) * (scale * scale * scale * row_product / width)).astype(BF16)


def final(place, kept, arrived, own_product, other_product, tokens, cotangent, gain, inverse):
    count, width = tokens.shape
    columns = width // 4
    quarter = lambda height: pl.BlockSpec((height, columns), lambda i, place: (0, place[2]))
    return pl.pallas_call(
        functools.partial(final_kernel, width),
        out_shape=jax.ShapeDtypeStruct((count, columns), BF16),
        grid_spec=grid_of(
            (1,),
            [whole(array.shape) for array in (kept, arrived, own_product, other_product)]
            + [quarter(count), quarter(count), quarter(1), whole(inverse.shape)],
            whole((count, columns)),
        ),
        compiler_params=params(16),
        name="final",
    )(place, kept, arrived, own_product, other_product, tokens, cotangent, gain, inverse)


def body(tokens, cotangent, norm_gain, expert_ids, gate_weights, w_gate, w_up, w_down):
    experts = lax.axis_size("expert")
    token_count, width = tokens.shape
    top_count = expert_ids.shape[1]
    capacity = token_count * top_count * 3 // (2 * experts)
    pipe = lax.axis_index("pipe")
    place = jnp.stack([lax.rem(pipe, 2), pipe // 2, pipe]).astype(jnp.int32)
    weights = (w_gate[0], w_up[0], in_hbm(w_down[0]))
    ids = in_hbm(expert_ids.T)
    gain = norm_gain.reshape(1, width)

    rows, inverse = make_message(
        place,
        in_hbm(tokens),
        in_hbm(cotangent),
        in_hbm(gain),
        ids,
        in_hbm(gate_weights.T),
        capacity,
        experts,
    )
    rows, ids = lax.optimization_barrier((exchange(rows), ids))
    accs = project(place, rows, weights)
    theirs, *grads = expert(place, core_swap(rows), weights, accs)
    back = merge(mine_rows(place, grads, weights), core_swap(theirs))
    back, gather = lax.optimization_barrier((back, gather_matrix(ids, capacity, experts)))
    kept, sent = combine(place, gather, exchange(back))
    product = row_products(place, kept, sent, tokens, gain)
    product = product + core_swap(product)
    return final(
        place, kept, high_swap(sent), product, high_swap(product), tokens, cotangent, gain, inverse
    )


def solution(mesh):
    in_specs = (
        P("expert", None),
        P("expert", None),
        P(),
        P("expert", None),
        P("expert", None),
        P("expert", None, "pipe"),
        P("expert", None, "pipe"),
        P("expert", "pipe", None),
    )
    out_specs = P("expert", "pipe")
    return jax.shard_map(body, mesh=mesh, in_specs=in_specs, out_specs=out_specs, check_vma=False)
```

```python
import functools

import jax
import jax.numpy as jnp
from jax import lax
from jax.experimental import pallas as pl
from jax.experimental.pallas import tpu as pltpu
from jax.sharding import PartitionSpec as P

EPSILON = 1e-06
BF16 = jnp.bfloat16
F32 = jnp.float32
MIB = 1024 * 1024
FILL = 896
DEPTH = 1792
BACK = 896
LANES = 128
LAST = (((1,), (1,)), ((), ()))
CORE_SWAP = [(0, 1), (1, 0), (2, 3), (3, 2)]
HIGH_SWAP = [(0, 2), (2, 0), (1, 3), (3, 1)]


def params(mebibytes):
    return pltpu.CompilerParams(vmem_limit_bytes=mebibytes * MIB)


def in_hbm(array):
    return pltpu.with_memory_space_constraint(array, pltpu.HBM)


def whole(shape):
    return pl.BlockSpec(shape, lambda *_: (0,) * len(shape))


def grid_of(grid, in_specs, out_specs, scratch=()):
    return pltpu.PrefetchScalarGridSpec(
        num_scalar_prefetch=1, grid=grid, in_specs=in_specs, out_specs=out_specs, scratch_shapes=scratch
    )


def core_swap(array):
    return lax.ppermute(array, "pipe", CORE_SWAP)


def high_swap(array):
    return lax.ppermute(array, "pipe", HIGH_SWAP)


def exchange(rows):
    experts = lax.axis_size("expert")
    shaped = rows.reshape(experts, rows.shape[0] // experts, rows.shape[1])
    return lax.all_to_all(shaped, "expert", split_axis=0, concat_axis=0, tiled=True).reshape(rows.shape)


def message_kernel(capacity, place, tokens, cotangent, gain, ids, weights, rows, inverse, tokens_in, cotangent_in, select, factors, sems):
    top, count = ids.shape
    half = rows.shape[1]
    start = place[0] * half
    own_half = pl.ds(pl.multiple_of(start, half), half)
    copies = (
        pltpu.make_async_copy(tokens, tokens_in, sems.at[0]),
        pltpu.make_async_copy(cotangent.at[:, own_half], cotangent_in, sems.at[1]),
    )
    for copy in copies:
        copy.start()
    height = select.shape[0]
    experts = height // (2 * capacity)
    expert_of = lax.broadcasted_iota(jnp.int32, (experts, count), 0)
    earlier_of = lax.broadcasted_iota(jnp.int32, (count, count), 0)
    later_of = lax.broadcasted_iota(jnp.int32, (count, count), 1)
    before = (earlier_of < later_of).astype(F32).astype(BF16)
    row = lax.broadcasted_iota(jnp.int32, (height, count), 0)
    taken = jnp.zeros((experts, 1), F32)
    normed_part = jnp.zeros(row.shape, F32)
    routed_part = jnp.zeros(row.shape, F32)
    factor = jnp.zeros(row.shape, F32)
    for k in range(top):
        expert = ids[k : k + 1, :]
        named = (expert_of == expert).astype(F32)
        earlier = jnp.dot(named.astype(BF16), before, preferred_element_type=F32) + taken
        rank = jnp.sum(earlier * named, axis=0, keepdims=True).astype(jnp.int32)
        taken = taken + jnp.sum(named, axis=1, keepdims=True)
        at = expert * (2 * capacity) + rank
        hit = row == at
        hit_routed = row == at + capacity
        normed_part = jnp.where(hit, 1.0, normed_part)
        routed_part = jnp.where(hit_routed, 1.0, routed_part)
        factor = jnp.where(hit, 1.0, jnp.where(hit_routed, weights[k : k + 1, :], factor))
    select[:, :count] = normed_part.astype(BF16)
    select[:, count:] = routed_part.astype(BF16)
    factors[...] = jnp.broadcast_to(jnp.sum(factor, axis=1, keepdims=True), factors.shape)
    copies[0].wait()
    values = tokens_in[...].astype(F32)
    scale = lax.rsqrt(jnp.mean(values * values, axis=1, keepdims=True) + EPSILON)
    inverse[...] = scale
    copies[1].wait()
    for at in range(0, half, FILL):
        own = pl.ds(pl.multiple_of(start + at, LANES), FILL)
        normed = (tokens_in[:, own].astype(F32) * scale * gain[:, own]).astype(BF16)
        both = jnp.concatenate([normed, cotangent_in[:, at : at + FILL]], axis=0)
        picked = jnp.dot(select[...], both, preferred_element_type=F32)
        rows[:, at : at + FILL] = (picked * factors[:, :1]).astype(BF16)


def make_message(place, tokens, cotangent, gain, ids, weights, capacity, experts):
    count, width = tokens.shape
    half = width // 2
    height = experts * 2 * capacity
    any_space = pl.BlockSpec(memory_space=pl.ANY)
    resident = pl.BlockSpec(memory_space=pltpu.VMEM)
    return pl.pallas_call(
        functools.partial(message_kernel, capacity),
        out_shape=(jax.ShapeDtypeStruct((height, half), BF16), jax.ShapeDtypeStruct((count, 1), F32)),
        grid_spec=grid_of(
            (1,),
            [any_space, any_space, whole(gain.shape), whole(ids.shape), whole(weights.shape)],
            (resident, whole((count, 1))),
            [
                pltpu.VMEM((count, width), BF16),
                pltpu.VMEM((count, half), BF16),
                pltpu.VMEM((height, 2 * count), BF16),
                pltpu.VMEM((height, LANES), F32),
                pltpu.SemaphoreType.DMA((2,)),
            ],
        ),
        compiler_params=params(24),
        name="message",
    )(place, tokens, cotangent, gain, ids, weights)


def gather_kernel(capacity, ids, out):
    top, count = ids.shape
    rows = out.shape[1]
    experts = rows // (2 * capacity)
    expert_of = lax.broadcasted_iota(jnp.int32, (experts, count), 0)
    earlier_of = lax.broadcasted_iota(jnp.int32, (count, count), 0)
    later_of = lax.broadcasted_iota(jnp.int32, (count, count), 1)
    before = (earlier_of < later_of).astype(F32).astype(BF16)
    row = lax.broadcasted_iota(jnp.int32, (count, rows), 1).astype(F32)
    taken = jnp.zeros((experts, 1), F32)
    first = jnp.zeros(row.shape, F32)
    second = jnp.zeros(row.shape, F32)
    for k in range(top):
        expert = ids[k : k + 1, :]
        named = (expert_of == expert).astype(F32)
        earlier = jnp.dot(named.astype(BF16), before, preferred_element_type=F32) + taken
        rank = jnp.sum(earlier * named, axis=0, keepdims=True)
        taken = taken + jnp.sum(named, axis=1, keepdims=True)
        at = expert.astype(F32) * (2 * capacity) + rank
        at = jnp.sum(jnp.where(earlier_of == later_of, at, 0.0), axis=1, keepdims=True)
        first = first + (row == at).astype(F32)
        second = second + (row == at + capacity).astype(F32)
    out[:count, :] = first.astype(BF16)
    out[count:, :] = second.astype(BF16)


def gather_matrix(ids, capacity, experts):
    count = ids.shape[1]
    return pl.pallas_call(
        functools.partial(gather_kernel, capacity),
        out_shape=jax.ShapeDtypeStruct((2 * count, experts * 2 * capacity), BF16),
        compiler_params=params(8),
        name="gather_matrix",
    )(ids)


def tiles(x, group):
    return x.reshape(x.shape[0] // (8 * group), group, 8, x.shape[1])


def upper(shape):
    return lax.broadcasted_iota(jnp.int32, shape, 1) < 4


def split_rows(x):
    rows, columns = x.shape
    x = x.astype(F32)
    a, b = tiles(x, 6), tiles(pltpu.roll(x, 4, 0), 6)
    top = upper((rows // 48, 8, columns))
    first = [a[:, 0], jnp.where(top, a[:, 1], b[:, 3]), b[:, 4]]
    second = [b[:, 2], jnp.where(top, b[:, 3], a[:, 4]), a[:, 5]]
    return [
        jnp.concatenate([p[:, None] for p in parts], axis=1).reshape(rows // 2, columns).astype(BF16)
        for parts in (first, second)
    ]


def interleave(x, y):
    rows, columns = x.shape
    x0, x1, x2 = tiles(x, 3), tiles(pltpu.roll(x, 4, 0), 3), tiles(pltpu.roll(x, rows - 4, 0), 3)
    y0, y1 = tiles(y, 3), tiles(pltpu.roll(y, 4, 0), 3)
    shape = (rows // 24, 8, columns)
    parts = [
        x0[:, 0],
        jnp.where(upper(shape), x0[:, 1], y1[:, 0]),
        y1[:, 1],
        x1[:, 2],
        jnp.where(upper(shape), x2[:, 2], y0[:, 1]),
        y0[:, 2],
    ]
    return jnp.concatenate([p[:, None] for p in parts], axis=1).reshape(2 * rows, columns)


def project_half(rows, gate, up, down, down_in, sems, side, accs, bases):
    half = rows.shape[1]
    copies = []
    for i in range(half // DEPTH):
        at = pl.ds(pl.multiple_of(side * half + i * DEPTH, DEPTH), DEPTH)
        to = pl.ds(i * DEPTH, DEPTH)
        copies.append(pltpu.make_async_copy(down.at[:, at], down_in.at[:, to], sems.at[i]))
        copies[i].start()
    for i in range(half // DEPTH):
        at = pl.ds(pl.multiple_of(side * half + i * DEPTH, DEPTH), DEPTH)
        to = slice(i * DEPTH, (i + 1) * DEPTH)
        normed, routed = split_rows(rows[:, to])
        to_gate = jnp.dot(normed, gate[at, :], preferred_element_type=F32)
        to_up = jnp.dot(normed, up[at, :], preferred_element_type=F32)
        copies[i].wait()
        to_hidden = lax.dot_general(routed, down_in[:, to], LAST, preferred_element_type=F32)
        for number, add in enumerate((to_gate, to_up, to_hidden)):
            base = (bases if i == 0 else accs)[number]
            accs[number][...] = add if base is None else base[...] + add


def back_rows(place, side, grad_gate, grad_up, gate, up, out):
    columns = out.shape[1]

    def one(start):
        at = pl.ds(pl.multiple_of(start, LANES), BACK)
        total = lax.dot_general(grad_gate[...], gate[at, :], LAST, preferred_element_type=F32)
        return total + lax.dot_general(grad_up[...], up[at, :], LAST, preferred_element_type=F32)

    for at in range(0, columns, BACK):
        rows = interleave(one(side * columns + at), one((2 + side) * columns + at))
        out[:, at : at + BACK] = rows.astype(BF16)


def down_scratch(half, hidden):
    return [pltpu.VMEM((hidden, half), BF16), pltpu.SemaphoreType.DMA((half // DEPTH,))]


def project_kernel(place, rows, gate, up, down, acc_gate, acc_up, acc_hidden, down_in, sems):
    project_half(rows, gate, up, down, down_in, sems, place[0], (acc_gate, acc_up, acc_hidden), (None,) * 3)


def project(place, rows, weights):
    acc = jax.ShapeDtypeStruct((rows.shape[0] // 2, weights[0].shape[1]), F32)
    resident = pl.BlockSpec(memory_space=pltpu.VMEM)
    return pl.pallas_call(
        project_kernel,
        out_shape=(acc,) * 3,
        grid_spec=grid_of(
            (1,),
            [resident] * 3 + [pl.BlockSpec(memory_space=pl.ANY)],
            (resident,) * 3,
            down_scratch(rows.shape[1], acc.shape[1]),
        ),
        compiler_params=params(20),
        name="project",
    )(place, rows, *weights)


def expert_kernel(place, rows, gate, up, down, in_gate, in_up, in_hidden, theirs, grad_gate, grad_up, acc_gate, acc_up, acc_hidden, down_in, sems):
    side = 1 - place[0]
    accs = (acc_gate, acc_up, acc_hidden)
    project_half(rows, gate, up, down, down_in, sems, side, accs, (in_gate, in_up, in_hidden))
    pre_gate, pre_up, hidden = acc_gate[...], acc_up[...], acc_hidden[...]
    sigma = jax.nn.sigmoid(pre_gate)
    grad_gate[...] = (hidden * pre_up * sigma * (1.0 + pre_gate * (1.0 - sigma))).astype(BF16)
    grad_up[...] = (hidden * pre_gate * sigma).astype(BF16)
    back_rows(place, side, grad_gate, grad_up, gate, up, theirs)


def expert(place, rows, weights, accs):
    height = rows.shape[0]
    acc = accs[0].shape
    grad = jax.ShapeDtypeStruct(acc, BF16)
    resident = pl.BlockSpec(memory_space=pltpu.VMEM)
    return pl.pallas_call(
        expert_kernel,
        out_shape=(jax.ShapeDtypeStruct((height, weights[0].shape[0] // 4), BF16), grad, grad),
        grid_spec=grid_of(
            (1,),
            [resident] * 3 + [pl.BlockSpec(memory_space=pl.ANY)] + [resident] * 3,
            (resident,) * 3,
            [pltpu.VMEM(acc, F32)] * 3 + down_scratch(rows.shape[1], acc[1]),
        ),
        compiler_params=params(24),
        name="expert",
    )(place, rows, *weights, *accs)


def mine_kernel(place, grad_gate, grad_up, gate, up, mine):
    back_rows(place, place[0], grad_gate, grad_up, gate, up, mine)


def mine_rows(place, grads, weights):
    gate, up, _ = weights
    resident = pl.BlockSpec(memory_space=pltpu.VMEM)
    return pl.pallas_call(
        mine_kernel,
        out_shape=jax.ShapeDtypeStruct((2 * grads[0].shape[0], gate.shape[0] // 4), BF16),
        grid_spec=grid_of((1,), [resident] * 4, resident),
        compiler_params=params(16),
        name="mine_rows",
    )(place, *grads, gate, up)


def merge_kernel(mine, other, out):
    out[...] = (mine[...].astype(F32) + other[...].astype(F32)).astype(BF16)


def merge(mine, other):
    rows, columns = mine.shape
    spec = pl.BlockSpec((rows // 4, columns), lambda i: (i, 0))
    return pl.pallas_call(
        merge_kernel,
        out_shape=jax.ShapeDtypeStruct((rows, columns), BF16),
        grid=(4,),
        in_specs=[spec, spec],
        out_specs=spec,
        compiler_params=params(12),
        name="merge",
    )(mine, other)


def sums_kernel(place, gather, rows, out):
    out[...] = jnp.dot(gather[...], rows[...], preferred_element_type=F32).astype(out.dtype)


def token_sums(place, gather, rows, other, kind):
    count = gather.shape[0] // 2
    height, columns = rows.shape
    resident = pl.BlockSpec(memory_space=pltpu.VMEM)
    mine = pl.BlockSpec((count, height), lambda i, place: (1 - place[1] if other else place[1], 0))
    return pl.pallas_call(
        sums_kernel,
        out_shape=jax.ShapeDtypeStruct((count, columns), kind),
        grid_spec=grid_of((1,), [mine, resident], resident),
        compiler_params=params(16),
        name="token_sums",
    )(place, gather, rows)


def product_kernel(place, kept, sent, own_tokens, other_tokens, own_gain, other_gain, product):
    part = kept[...] * (own_tokens[...].astype(F32) * own_gain[...])
    part = part + sent[...].astype(F32) * (other_tokens[...].astype(F32) * other_gain[...])
    product[...] = jnp.broadcast_to(jnp.sum(part, axis=1, keepdims=True), product.shape)


def row_products(place, kept, sent, tokens, gain):
    count, columns = kept.shape

    def quarter(size, other):
        def index(i, place):
            high = 1 - place[1] if other else place[1]
            return (0, 2 * high + place[0])

        return pl.BlockSpec((size, columns), index)

    return pl.pallas_call(
        product_kernel,
        out_shape=jax.ShapeDtypeStruct((count, LANES), F32),
        grid_spec=grid_of(
            (1,),
            [whole(kept.shape), whole(sent.shape)]
            + [quarter(count, False), quarter(count, True), quarter(1, False), quarter(1, True)],
            whole((count, LANES)),
        ),
        compiler_params=params(16),
        name="row_products",
    )(place, kept, sent, tokens, tokens, gain, gain)


def final_kernel(width, place, kept, arrived, own_product, other_product, tokens, cotangent, gain, inverse, out):
    scale = inverse[...]
    row_product = own_product[:, :1] + other_product[:, :1]
    grad = kept[...] + arrived[...].astype(F32)
    value = cotangent[...].astype(F32) + scale * gain[...] * grad
    out[...] = (value - tokens[...].astype(F32) * (scale * scale * scale * row_product / width)).astype(BF16)


def final(place, kept, arrived, own_product, other_product, tokens, cotangent, gain, inverse):
    count, width = tokens.shape
    columns = width // 4
    quarter = lambda height: pl.BlockSpec((height, columns), lambda i, place: (0, place[2]))
    return pl.pallas_call(
        functools.partial(final_kernel, width),
        out_shape=jax.ShapeDtypeStruct((count, columns), BF16),
        grid_spec=grid_of(
            (1,),
            [whole(array.shape) for array in (kept, arrived, own_product, other_product)]
            + [quarter(count), quarter(count), quarter(1), whole(inverse.shape)],
            whole((count, columns)),
        ),
        compiler_params=params(16),
        name="final",
    )(place, kept, arrived, own_product, other_product, tokens, cotangent, gain, inverse)


def body(tokens, cotangent, norm_gain, expert_ids, gate_weights, w_gate, w_up, w_down):
    experts = lax.axis_size("expert")
    token_count, width = tokens.shape
    top_count = expert_ids.shape[1]
    capacity = token_count * top_count * 3 // (2 * experts)
    pipe = lax.axis_index("pipe")
    place = jnp.stack([lax.rem(pipe, 2), pipe // 2, pipe]).astype(jnp.int32)
    weights = (w_gate[0], w_up[0], in_hbm(w_down[0]))
    ids = in_hbm(expert_ids.T)
    gain = norm_gain.reshape(1, width)

    rows, inverse = make_message(
        place,
        in_hbm(tokens),
        in_hbm(cotangent),
        in_hbm(gain),
        ids,
        in_hbm(gate_weights.T),
        capacity,
        experts,
    )
    rows, ids = lax.optimization_barrier((exchange(rows), ids))
    accs = project(place, rows, weights)
    theirs, *grads = expert(place, core_swap(rows), weights, accs)
    back = merge(mine_rows(place, grads, weights), core_swap(theirs))
    back, gather = lax.optimization_barrier((back, gather_matrix(ids, capacity, experts)))
    back = exchange(back)
    sent = token_sums(place, gather, back, True, BF16)
    kept = token_sums(place, gather, back, False, F32)
    product = row_products(place, kept, sent, tokens, gain)
    product = product + core_swap(product)
    return final(
        place, kept, high_swap(sent), product, high_swap(product), tokens, cotangent, gain, inverse
    )


def solution(mesh):
    in_specs = (
        P("expert", None),
        P("expert", None),
        P(),
        P("expert", None),
        P("expert", None),
        P("expert", None, "pipe"),
        P("expert", None, "pipe"),
        P("expert", "pipe", None),
    )
    out_specs = P("expert", "pipe")
    return jax.shard_map(body, mesh=mesh, in_specs=in_specs, out_specs=out_specs, check_vma=False)
```

```python
import functools

import jax
import jax.numpy as jnp
from jax import lax
from jax.experimental import pallas as pl
from jax.experimental.pallas import tpu as pltpu
from jax.sharding import PartitionSpec as P

EPSILON = 1e-06
BF16 = jnp.bfloat16
F32 = jnp.float32
MIB = 1024 * 1024
FILL = 896
DEPTH = 1792
BACK = 896
LANES = 128
LAST = (((1,), (1,)), ((), ()))
CORE_SWAP = [(0, 1), (1, 0), (2, 3), (3, 2)]
HIGH_SWAP = [(0, 2), (2, 0), (1, 3), (3, 1)]


def params(mebibytes):
    return pltpu.CompilerParams(vmem_limit_bytes=mebibytes * MIB)


def in_hbm(array):
    return pltpu.with_memory_space_constraint(array, pltpu.HBM)


def whole(shape):
    return pl.BlockSpec(shape, lambda *_: (0,) * len(shape))


def grid_of(grid, in_specs, out_specs, scratch=()):
    return pltpu.PrefetchScalarGridSpec(
        num_scalar_prefetch=1, grid=grid, in_specs=in_specs, out_specs=out_specs, scratch_shapes=scratch
    )


def core_swap(array):
    return lax.ppermute(array, "pipe", CORE_SWAP)


def high_swap(array):
    return lax.ppermute(array, "pipe", HIGH_SWAP)


def exchange(rows):
    experts = lax.axis_size("expert")
    shaped = rows.reshape(experts, rows.shape[0] // experts, rows.shape[1])
    return lax.all_to_all(shaped, "expert", split_axis=0, concat_axis=0, tiled=True).reshape(rows.shape)


def message_kernel(capacity, place, tokens, cotangent, gain, ids, weights, rows, inverse, tokens_in, cotangent_in, select, factors, sems):
    top, count = ids.shape
    half = rows.shape[1]
    start = place[0] * half
    own_half = pl.ds(pl.multiple_of(start, half), half)
    copies = (
        pltpu.make_async_copy(tokens, tokens_in, sems.at[0]),
        pltpu.make_async_copy(cotangent.at[:, own_half], cotangent_in, sems.at[1]),
    )
    for copy in copies:
        copy.start()
    height = select.shape[0]
    experts = height // (2 * capacity)
    expert_of = lax.broadcasted_iota(jnp.int32, (experts, count), 0)
    earlier_of = lax.broadcasted_iota(jnp.int32, (count, count), 0)
    later_of = lax.broadcasted_iota(jnp.int32, (count, count), 1)
    before = (earlier_of < later_of).astype(F32).astype(BF16)
    row = lax.broadcasted_iota(jnp.int32, (height, count), 0)
    taken = jnp.zeros((experts, 1), F32)
    normed_part = jnp.zeros(row.shape, F32)
    routed_part = jnp.zeros(row.shape, F32)
    factor = jnp.zeros(row.shape, F32)
    for k in range(top):
        expert = ids[k : k + 1, :]
        named = (expert_of == expert).astype(F32)
        earlier = jnp.dot(named.astype(BF16), before, preferred_element_type=F32) + taken
        rank = jnp.sum(earlier * named, axis=0, keepdims=True).astype(jnp.int32)
        taken = taken + jnp.sum(named, axis=1, keepdims=True)
        at = expert * (2 * capacity) + rank
        hit = row == at
        hit_routed = row == at + capacity
        normed_part = jnp.where(hit, 1.0, normed_part)
        routed_part = jnp.where(hit_routed, 1.0, routed_part)
        factor = jnp.where(hit, 1.0, jnp.where(hit_routed, weights[k : k + 1, :], factor))
    select[:, :count] = normed_part.astype(BF16)
    select[:, count:] = routed_part.astype(BF16)
    factors[...] = jnp.broadcast_to(jnp.sum(factor, axis=1, keepdims=True), factors.shape)
    copies[0].wait()
    values = tokens_in[...].astype(F32)
    scale = lax.rsqrt(jnp.mean(values * values, axis=1, keepdims=True) + EPSILON)
    inverse[...] = scale
    copies[1].wait()
    for at in range(0, half, FILL):
        own = pl.ds(pl.multiple_of(start + at, LANES), FILL)
        normed = (tokens_in[:, own].astype(F32) * scale * gain[:, own]).astype(BF16)
        both = jnp.concatenate([normed, cotangent_in[:, at : at + FILL]], axis=0)
        picked = jnp.dot(select[...], both, preferred_element_type=F32)
        rows[:, at : at + FILL] = (picked * factors[:, :1]).astype(BF16)


def make_message(place, tokens, cotangent, gain, ids, weights, capacity, experts):
    count, width = tokens.shape
    half = width // 2
    height = experts * 2 * capacity
    any_space = pl.BlockSpec(memory_space=pl.ANY)
    resident = pl.BlockSpec(memory_space=pltpu.VMEM)
    return pl.pallas_call(
        functools.partial(message_kernel, capacity),
        out_shape=(jax.ShapeDtypeStruct((height, half), BF16), jax.ShapeDtypeStruct((count, 1), F32)),
        grid_spec=grid_of(
            (1,),
            [any_space, any_space, whole(gain.shape), whole(ids.shape), whole(weights.shape)],
            (resident, whole((count, 1))),
            [
                pltpu.VMEM((count, width), BF16),
                pltpu.VMEM((count, half), BF16),
                pltpu.VMEM((height, 2 * count), BF16),
                pltpu.VMEM((height, LANES), F32),
                pltpu.SemaphoreType.DMA((2,)),
            ],
        ),
        compiler_params=params(24),
        name="message",
    )(place, tokens, cotangent, gain, ids, weights)


def gather_kernel(capacity, ids, out):
    top, count = ids.shape
    rows = out.shape[1]
    experts = rows // (2 * capacity)
    expert_of = lax.broadcasted_iota(jnp.int32, (experts, count), 0)
    earlier_of = lax.broadcasted_iota(jnp.int32, (count, count), 0)
    later_of = lax.broadcasted_iota(jnp.int32, (count, count), 1)
    before = (earlier_of < later_of).astype(F32).astype(BF16)
    row = lax.broadcasted_iota(jnp.int32, (count, rows), 1).astype(F32)
    taken = jnp.zeros((experts, 1), F32)
    first = jnp.zeros(row.shape, F32)
    second = jnp.zeros(row.shape, F32)
    for k in range(top):
        expert = ids[k : k + 1, :]
        named = (expert_of == expert).astype(F32)
        earlier = jnp.dot(named.astype(BF16), before, preferred_element_type=F32) + taken
        rank = jnp.sum(earlier * named, axis=0, keepdims=True)
        taken = taken + jnp.sum(named, axis=1, keepdims=True)
        at = expert.astype(F32) * (2 * capacity) + rank
        at = jnp.sum(jnp.where(earlier_of == later_of, at, 0.0), axis=1, keepdims=True)
        first = first + (row == at).astype(F32)
        second = second + (row == at + capacity).astype(F32)
    out[:count, :] = first.astype(BF16)
    out[count:, :] = second.astype(BF16)


def gather_matrix(ids, capacity, experts):
    count = ids.shape[1]
    return pl.pallas_call(
        functools.partial(gather_kernel, capacity),
        out_shape=jax.ShapeDtypeStruct((2 * count, experts * 2 * capacity), BF16),
        compiler_params=params(8),
        name="gather_matrix",
    )(ids)


def tiles(x, group):
    return x.reshape(x.shape[0] // (8 * group), group, 8, x.shape[1])


def upper(shape):
    return lax.broadcasted_iota(jnp.int32, shape, 1) < 4


def split_rows(x):
    rows, columns = x.shape
    x = x.astype(F32)
    a, b = tiles(x, 6), tiles(pltpu.roll(x, 4, 0), 6)
    top = upper((rows // 48, 8, columns))
    first = [a[:, 0], jnp.where(top, a[:, 1], b[:, 3]), b[:, 4]]
    second = [b[:, 2], jnp.where(top, b[:, 3], a[:, 4]), a[:, 5]]
    return [
        jnp.concatenate([p[:, None] for p in parts], axis=1).reshape(rows // 2, columns).astype(BF16)
        for parts in (first, second)
    ]


def interleave(x, y):
    rows, columns = x.shape
    x0, x1, x2 = tiles(x, 3), tiles(pltpu.roll(x, 4, 0), 3), tiles(pltpu.roll(x, rows - 4, 0), 3)
    y0, y1 = tiles(y, 3), tiles(pltpu.roll(y, 4, 0), 3)
    shape = (rows // 24, 8, columns)
    parts = [
        x0[:, 0],
        jnp.where(upper(shape), x0[:, 1], y1[:, 0]),
        y1[:, 1],
        x1[:, 2],
        jnp.where(upper(shape), x2[:, 2], y0[:, 1]),
        y0[:, 2],
    ]
    return jnp.concatenate([p[:, None] for p in parts], axis=1).reshape(2 * rows, columns)


def project_half(rows, gate, up, down, down_in, sems, side, accs, bases):
    half = rows.shape[1]
    copies = []
    for i in range(half // DEPTH):
        at = pl.ds(pl.multiple_of(side * half + i * DEPTH, DEPTH), DEPTH)
        to = pl.ds(i * DEPTH, DEPTH)
        copies.append(pltpu.make_async_copy(down.at[:, at], down_in.at[:, to], sems.at[i]))
        copies[i].start()
    for i in range(half // DEPTH):
        at = pl.ds(pl.multiple_of(side * half + i * DEPTH, DEPTH), DEPTH)
        to = slice(i * DEPTH, (i + 1) * DEPTH)
        normed, routed = split_rows(rows[:, to])
        to_gate = jnp.dot(normed, gate[at, :], preferred_element_type=F32)
        to_up = jnp.dot(normed, up[at, :], preferred_element_type=F32)
        copies[i].wait()
        to_hidden = lax.dot_general(routed, down_in[:, to], LAST, preferred_element_type=F32)
        for number, add in enumerate((to_gate, to_up, to_hidden)):
            base = (bases if i == 0 else accs)[number]
            accs[number][...] = add if base is None else base[...] + add


def back_rows(place, side, grad_gate, grad_up, gate, up, out):
    columns = out.shape[1]

    def one(start):
        at = pl.ds(pl.multiple_of(start, LANES), BACK)
        total = lax.dot_general(grad_gate[...], gate[at, :], LAST, preferred_element_type=F32)
        return total + lax.dot_general(grad_up[...], up[at, :], LAST, preferred_element_type=F32)

    for at in range(0, columns, BACK):
        rows = interleave(one(side * columns + at), one((2 + side) * columns + at))
        out[:, at : at + BACK] = rows.astype(BF16)


def down_scratch(half, hidden):
    return [pltpu.VMEM((hidden, half), BF16), pltpu.SemaphoreType.DMA((half // DEPTH,))]


def project_kernel(place, rows, gate, up, down, acc_gate, acc_up, acc_hidden, down_in, sems):
    project_half(rows, gate, up, down, down_in, sems, place[0], (acc_gate, acc_up, acc_hidden), (None,) * 3)


def project(place, rows, weights):
    acc = jax.ShapeDtypeStruct((rows.shape[0] // 2, weights[0].shape[1]), F32)
    resident = pl.BlockSpec(memory_space=pltpu.VMEM)
    return pl.pallas_call(
        project_kernel,
        out_shape=(acc,) * 3,
        grid_spec=grid_of(
            (1,),
            [resident] * 3 + [pl.BlockSpec(memory_space=pl.ANY)],
            (resident,) * 3,
            down_scratch(rows.shape[1], acc.shape[1]),
        ),
        compiler_params=params(20),
        name="project",
    )(place, rows, *weights)


def expert_kernel(place, rows, gate, up, down, in_gate, in_up, in_hidden, theirs, grad_gate, grad_up, acc_gate, acc_up, acc_hidden, down_in, sems):
    side = 1 - place[0]
    accs = (acc_gate, acc_up, acc_hidden)
    project_half(rows, gate, up, down, down_in, sems, side, accs, (in_gate, in_up, in_hidden))
    pre_gate, pre_up, hidden = acc_gate[...], acc_up[...], acc_hidden[...]
    sigma = jax.nn.sigmoid(pre_gate)
    grad_gate[...] = (hidden * pre_up * sigma * (1.0 + pre_gate * (1.0 - sigma))).astype(BF16)
    grad_up[...] = (hidden * pre_gate * sigma).astype(BF16)
    back_rows(place, side, grad_gate, grad_up, gate, up, theirs)


def expert(place, rows, weights, accs):
    height = rows.shape[0]
    acc = accs[0].shape
    grad = jax.ShapeDtypeStruct(acc, BF16)
    resident = pl.BlockSpec(memory_space=pltpu.VMEM)
    return pl.pallas_call(
        expert_kernel,
        out_shape=(jax.ShapeDtypeStruct((height, weights[0].shape[0] // 4), BF16), grad, grad),
        grid_spec=grid_of(
            (1,),
            [resident] * 3 + [pl.BlockSpec(memory_space=pl.ANY)] + [resident] * 3,
            (resident,) * 3,
            [pltpu.VMEM(acc, F32)] * 3 + down_scratch(rows.shape[1], acc[1]),
        ),
        compiler_params=params(24),
        name="expert",
    )(place, rows, *weights, *accs)


def mine_kernel(place, grad_gate, grad_up, gate, up, mine):
    back_rows(place, place[0], grad_gate, grad_up, gate, up, mine)


def mine_rows(place, grads, weights):
    gate, up, _ = weights
    resident = pl.BlockSpec(memory_space=pltpu.VMEM)
    return pl.pallas_call(
        mine_kernel,
        out_shape=jax.ShapeDtypeStruct((2 * grads[0].shape[0], gate.shape[0] // 4), BF16),
        grid_spec=grid_of((1,), [resident] * 4, resident),
        compiler_params=params(16),
        name="mine_rows",
    )(place, *grads, gate, up)


def merge_kernel(mine, other, out):
    out[...] = (mine[...].astype(F32) + other[...].astype(F32)).astype(BF16)


def merge(mine, other):
    rows, columns = mine.shape
    spec = pl.BlockSpec((rows // 4, columns), lambda i: (i, 0))
    return pl.pallas_call(
        merge_kernel,
        out_shape=jax.ShapeDtypeStruct((rows, columns), BF16),
        grid=(4,),
        in_specs=[spec, spec],
        out_specs=spec,
        compiler_params=params(12),
        name="merge",
    )(mine, other)


def sums_kernel(place, gather, rows, out):
    out[...] = jnp.dot(gather[...], rows[...], preferred_element_type=F32).astype(out.dtype)


def token_sums(place, gather, rows, other, kind):
    count = gather.shape[0] // 2
    height, columns = rows.shape
    resident = pl.BlockSpec(memory_space=pltpu.VMEM)
    mine = pl.BlockSpec((count, height), lambda i, place: (1 - place[1] if other else place[1], 0))
    return pl.pallas_call(
        sums_kernel,
        out_shape=jax.ShapeDtypeStruct((count, columns), kind),
        grid_spec=grid_of((1,), [mine, resident], resident),
        compiler_params=params(16),
        name="token_sums",
    )(place, gather, rows)


def diagonal(count):
    shape = (count, count)
    return lax.broadcasted_iota(jnp.int32, shape, 0) == lax.broadcasted_iota(jnp.int32, shape, 1)


def product_kernel(place, kept, sent, own_tokens, other_tokens, own_gain, other_gain, product):
    part = kept[...] * (own_tokens[...].astype(F32) * own_gain[...])
    part = part + sent[...].astype(F32) * (other_tokens[...].astype(F32) * other_gain[...])
    column = jnp.sum(part, axis=1, keepdims=True)
    row = jnp.sum(jnp.where(diagonal(part.shape[0]), column, 0.0), axis=0, keepdims=True)
    product[...] = jnp.broadcast_to(row, product.shape)


def row_products(place, kept, sent, tokens, gain):
    count, columns = kept.shape

    def quarter(size, other):
        def index(i, place):
            high = 1 - place[1] if other else place[1]
            return (0, 2 * high + place[0])

        return pl.BlockSpec((size, columns), index)

    return pl.pallas_call(
        product_kernel,
        out_shape=jax.ShapeDtypeStruct((8, count), F32),
        grid_spec=grid_of(
            (1,),
            [whole(kept.shape), whole(sent.shape)]
            + [quarter(count, False), quarter(count, True), quarter(1, False), quarter(1, True)],
            whole((8, count)),
        ),
        compiler_params=params(16),
        name="row_products",
    )(place, kept, sent, tokens, tokens, gain, gain)


def final_kernel(width, place, kept, arrived, own_product, other_product, tokens, cotangent, gain, inverse, out):
    scale = inverse[...]
    row = own_product[:1, :] + other_product[:1, :]
    row_product = jnp.sum(jnp.where(diagonal(out.shape[0]), row, 0.0), axis=1, keepdims=True)
    grad = kept[...] + arrived[...].astype(F32)
    value = cotangent[...].astype(F32) + scale * gain[...] * grad
    out[...] = (value - tokens[...].astype(F32) * (scale * scale * scale * row_product / width)).astype(BF16)


def final(place, kept, arrived, own_product, other_product, tokens, cotangent, gain, inverse):
    count, width = tokens.shape
    columns = width // 4
    quarter = lambda height: pl.BlockSpec((height, columns), lambda i, place: (0, place[2]))
    return pl.pallas_call(
        functools.partial(final_kernel, width),
        out_shape=jax.ShapeDtypeStruct((count, columns), BF16),
        grid_spec=grid_of(
            (1,),
            [whole(array.shape) for array in (kept, arrived, own_product, other_product)]
            + [quarter(count), quarter(count), quarter(1), whole(inverse.shape)],
            whole((count, columns)),
        ),
        compiler_params=params(16),
        name="final",
    )(place, kept, arrived, own_product, other_product, tokens, cotangent, gain, inverse)


def body(tokens, cotangent, norm_gain, expert_ids, gate_weights, w_gate, w_up, w_down):
    experts = lax.axis_size("expert")
    token_count, width = tokens.shape
    top_count = expert_ids.shape[1]
    capacity = token_count * top_count * 3 // (2 * experts)
    pipe = lax.axis_index("pipe")
    place = jnp.stack([lax.rem(pipe, 2), pipe // 2, pipe]).astype(jnp.int32)
    weights = (w_gate[0], w_up[0], in_hbm(w_down[0]))
    ids = in_hbm(expert_ids.T)
    gain = norm_gain.reshape(1, width)

    rows, inverse = make_message(
        place,
        in_hbm(tokens),
        in_hbm(cotangent),
        in_hbm(gain),
        ids,
        in_hbm(gate_weights.T),
        capacity,
        experts,
    )
    rows, ids = lax.optimization_barrier((exchange(rows), ids))
    accs = project(place, rows, weights)
    swapped, gather = lax.optimization_barrier((core_swap(rows), gather_matrix(ids, capacity, experts)))
    theirs, *grads = expert(place, swapped, weights, accs)
    back = merge(mine_rows(place, grads, weights), core_swap(theirs))
    back = exchange(back)
    sent = token_sums(place, gather, back, True, BF16)
    kept = token_sums(place, gather, back, False, F32)
    product = row_products(place, kept, sent, tokens, gain)
    product = product + core_swap(product)
    return final(
        place, kept, high_swap(sent), product, high_swap(product), tokens, cotangent, gain, inverse
    )


def solution(mesh):
    in_specs = (
        P("expert", None),
        P("expert", None),
        P(),
        P("expert", None),
        P("expert", None),
        P("expert", None, "pipe"),
        P("expert", None, "pipe"),
        P("expert", "pipe", None),
    )
    out_specs = P("expert", "pipe")
    return jax.shard_map(body, mesh=mesh, in_specs=in_specs, out_specs=out_specs, check_vma=False)
```

```python
import functools

import jax
import jax.numpy as jnp
from jax import lax
from jax.experimental import pallas as pl
from jax.experimental.pallas import tpu as pltpu
from jax.sharding import PartitionSpec as P

EPSILON = 1e-06
BF16 = jnp.bfloat16
F32 = jnp.float32
MIB = 1024 * 1024
FILL = 896
DEPTH = 1792
BACK = 896
LANES = 128
LAST = (((1,), (1,)), ((), ()))
CORE_SWAP = [(0, 1), (1, 0), (2, 3), (3, 2)]
HIGH_SWAP = [(0, 2), (2, 0), (1, 3), (3, 1)]


def params(mebibytes):
    return pltpu.CompilerParams(vmem_limit_bytes=mebibytes * MIB)


def in_hbm(array):
    return pltpu.with_memory_space_constraint(array, pltpu.HBM)


def whole(shape):
    return pl.BlockSpec(shape, lambda *_: (0,) * len(shape))


def grid_of(grid, in_specs, out_specs, scratch=()):
    return pltpu.PrefetchScalarGridSpec(
        num_scalar_prefetch=1, grid=grid, in_specs=in_specs, out_specs=out_specs, scratch_shapes=scratch
    )


def core_swap(array):
    return lax.ppermute(array, "pipe", CORE_SWAP)


def high_swap(array):
    return lax.ppermute(array, "pipe", HIGH_SWAP)


def exchange(rows):
    experts = lax.axis_size("expert")
    shaped = rows.reshape(experts, rows.shape[0] // experts, rows.shape[1])
    return lax.all_to_all(shaped, "expert", split_axis=0, concat_axis=0, tiled=True).reshape(rows.shape)


def message_kernel(capacity, place, tokens, cotangent, all_gain, all_ids, all_weights, rows, inverse, tokens_in, cotangent_in, gain, ids, weights, select, factors, sems):
    top, count = ids.shape
    half = rows.shape[1]
    start = place[0] * half
    own_half = pl.ds(pl.multiple_of(start, half), half)
    small = (
        pltpu.make_async_copy(all_ids, ids, sems.at[2]),
        pltpu.make_async_copy(all_weights, weights, sems.at[3]),
        pltpu.make_async_copy(all_gain, gain, sems.at[4]),
    )
    copies = (
        pltpu.make_async_copy(tokens, tokens_in, sems.at[0]),
        pltpu.make_async_copy(cotangent.at[:, own_half], cotangent_in, sems.at[1]),
    )
    for copy in small + copies:
        copy.start()
    for copy in small:
        copy.wait()
    height = select.shape[0]
    experts = height // (2 * capacity)
    expert_of = lax.broadcasted_iota(jnp.int32, (experts, count), 0)
    earlier_of = lax.broadcasted_iota(jnp.int32, (count, count), 0)
    later_of = lax.broadcasted_iota(jnp.int32, (count, count), 1)
    before = (earlier_of < later_of).astype(F32).astype(BF16)
    row = lax.broadcasted_iota(jnp.int32, (height, count), 0)
    taken = jnp.zeros((experts, 1), F32)
    normed_part = jnp.zeros(row.shape, F32)
    routed_part = jnp.zeros(row.shape, F32)
    factor = jnp.zeros(row.shape, F32)
    for k in range(top):
        expert = ids[k : k + 1, :]
        named = (expert_of == expert).astype(F32)
        earlier = jnp.dot(named.astype(BF16), before, preferred_element_type=F32) + taken
        rank = jnp.sum(earlier * named, axis=0, keepdims=True).astype(jnp.int32)
        taken = taken + jnp.sum(named, axis=1, keepdims=True)
        at = expert * (2 * capacity) + rank
        hit = row == at
        hit_routed = row == at + capacity
        normed_part = jnp.where(hit, 1.0, normed_part)
        routed_part = jnp.where(hit_routed, 1.0, routed_part)
        factor = jnp.where(hit, 1.0, jnp.where(hit_routed, weights[k : k + 1, :], factor))
    select[:, :count] = normed_part.astype(BF16)
    select[:, count:] = routed_part.astype(BF16)
    factors[...] = jnp.broadcast_to(jnp.sum(factor, axis=1, keepdims=True), factors.shape)
    copies[0].wait()
    values = tokens_in[...].astype(F32)
    scale = lax.rsqrt(jnp.mean(values * values, axis=1, keepdims=True) + EPSILON)
    inverse[...] = scale
    copies[1].wait()
    for at in range(0, half, FILL):
        own = pl.ds(pl.multiple_of(start + at, LANES), FILL)
        normed = (tokens_in[:, own].astype(F32) * scale * gain[:, own]).astype(BF16)
        both = jnp.concatenate([normed, cotangent_in[:, at : at + FILL]], axis=0)
        picked = jnp.dot(select[...], both, preferred_element_type=F32)
        rows[:, at : at + FILL] = (picked * factors[:, :1]).astype(BF16)


def make_message(place, tokens, cotangent, gain, ids, weights, capacity, experts):
    count, width = tokens.shape
    half = width // 2
    height = experts * 2 * capacity
    any_space = pl.BlockSpec(memory_space=pl.ANY)
    resident = pl.BlockSpec(memory_space=pltpu.VMEM)
    return pl.pallas_call(
        functools.partial(message_kernel, capacity),
        out_shape=(jax.ShapeDtypeStruct((height, half), BF16), jax.ShapeDtypeStruct((count, 1), F32)),
        grid_spec=grid_of(
            (1,),
            [any_space] * 5,
            (resident, resident),
            [
                pltpu.VMEM((count, width), BF16),
                pltpu.VMEM((count, half), BF16),
                pltpu.VMEM(gain.shape, F32),
                pltpu.VMEM(ids.shape, jnp.int32),
                pltpu.VMEM(weights.shape, F32),
                pltpu.VMEM((height, 2 * count), BF16),
                pltpu.VMEM((height, LANES), F32),
                pltpu.SemaphoreType.DMA((5,)),
            ],
        ),
        compiler_params=params(24),
        name="message",
    )(place, tokens, cotangent, gain, ids, weights)


def gather_kernel(capacity, ids, out):
    top, count = ids.shape
    rows = out.shape[1]
    experts = rows // (2 * capacity)
    expert_of = lax.broadcasted_iota(jnp.int32, (experts, count), 0)
    earlier_of = lax.broadcasted_iota(jnp.int32, (count, count), 0)
    later_of = lax.broadcasted_iota(jnp.int32, (count, count), 1)
    before = (earlier_of < later_of).astype(F32).astype(BF16)
    row = lax.broadcasted_iota(jnp.int32, (count, rows), 1).astype(F32)
    taken = jnp.zeros((experts, 1), F32)
    first = jnp.zeros(row.shape, F32)
    second = jnp.zeros(row.shape, F32)
    for k in range(top):
        expert = ids[k : k + 1, :]
        named = (expert_of == expert).astype(F32)
        earlier = jnp.dot(named.astype(BF16), before, preferred_element_type=F32) + taken
        rank = jnp.sum(earlier * named, axis=0, keepdims=True)
        taken = taken + jnp.sum(named, axis=1, keepdims=True)
        at = expert.astype(F32) * (2 * capacity) + rank
        at = jnp.sum(jnp.where(earlier_of == later_of, at, 0.0), axis=1, keepdims=True)
        first = first + (row == at).astype(F32)
        second = second + (row == at + capacity).astype(F32)
    out[:count, :] = first.astype(BF16)
    out[count:, :] = second.astype(BF16)


def gather_matrix(ids, capacity, experts):
    count = ids.shape[1]
    return pl.pallas_call(
        functools.partial(gather_kernel, capacity),
        out_shape=jax.ShapeDtypeStruct((2 * count, experts * 2 * capacity), BF16),
        compiler_params=params(8),
        name="gather_matrix",
    )(ids)


def tiles(x, group):
    return x.reshape(x.shape[0] // (8 * group), group, 8, x.shape[1])


def upper(shape):
    return lax.broadcasted_iota(jnp.int32, shape, 1) < 4


def split_rows(x):
    rows, columns = x.shape
    x = x.astype(F32)
    a, b = tiles(x, 6), tiles(pltpu.roll(x, 4, 0), 6)
    top = upper((rows // 48, 8, columns))
    first = [a[:, 0], jnp.where(top, a[:, 1], b[:, 3]), b[:, 4]]
    second = [b[:, 2], jnp.where(top, b[:, 3], a[:, 4]), a[:, 5]]
    return [
        jnp.concatenate([p[:, None] for p in parts], axis=1).reshape(rows // 2, columns).astype(BF16)
        for parts in (first, second)
    ]


def interleave(x, y):
    rows, columns = x.shape
    x0, x1, x2 = tiles(x, 3), tiles(pltpu.roll(x, 4, 0), 3), tiles(pltpu.roll(x, rows - 4, 0), 3)
    y0, y1 = tiles(y, 3), tiles(pltpu.roll(y, 4, 0), 3)
    shape = (rows // 24, 8, columns)
    parts = [
        x0[:, 0],
        jnp.where(upper(shape), x0[:, 1], y1[:, 0]),
        y1[:, 1],
        x1[:, 2],
        jnp.where(upper(shape), x2[:, 2], y0[:, 1]),
        y0[:, 2],
    ]
    return jnp.concatenate([p[:, None] for p in parts], axis=1).reshape(2 * rows, columns)


def project_half(rows, gate, up, down, down_in, sems, side, accs, bases):
    half = rows.shape[1]
    copies = []
    for i in range(half // DEPTH):
        at = pl.ds(pl.multiple_of(side * half + i * DEPTH, DEPTH), DEPTH)
        to = pl.ds(i * DEPTH, DEPTH)
        copies.append(pltpu.make_async_copy(down.at[:, at], down_in.at[:, to], sems.at[i]))
        copies[i].start()
    for i in range(half // DEPTH):
        at = pl.ds(pl.multiple_of(side * half + i * DEPTH, DEPTH), DEPTH)
        to = slice(i * DEPTH, (i + 1) * DEPTH)
        normed, routed = split_rows(rows[:, to])
        to_gate = jnp.dot(normed, gate[at, :], preferred_element_type=F32)
        to_up = jnp.dot(normed, up[at, :], preferred_element_type=F32)
        copies[i].wait()
        to_hidden = lax.dot_general(routed, down_in[:, to], LAST, preferred_element_type=F32)
        for number, add in enumerate((to_gate, to_up, to_hidden)):
            base = (bases if i == 0 else accs)[number]
            accs[number][...] = add if base is None else base[...] + add


def back_rows(place, side, grad_gate, grad_up, gate, up, out):
    columns = out.shape[1]

    def one(start):
        at = pl.ds(pl.multiple_of(start, LANES), BACK)
        total = lax.dot_general(grad_gate[...], gate[at, :], LAST, preferred_element_type=F32)
        return total + lax.dot_general(grad_up[...], up[at, :], LAST, preferred_element_type=F32)

    for at in range(0, columns, BACK):
        rows = interleave(one(side * columns + at), one((2 + side) * columns + at))
        out[:, at : at + BACK] = rows.astype(BF16)


def down_scratch(half, hidden):
    return [pltpu.VMEM((hidden, half), BF16), pltpu.SemaphoreType.DMA((half // DEPTH,))]


def project_kernel(place, rows, gate, up, down, acc_gate, acc_up, acc_hidden, down_in, sems):
    project_half(rows, gate, up, down, down_in, sems, place[0], (acc_gate, acc_up, acc_hidden), (None,) * 3)


def project(place, rows, weights):
    acc = jax.ShapeDtypeStruct((rows.shape[0] // 2, weights[0].shape[1]), F32)
    resident = pl.BlockSpec(memory_space=pltpu.VMEM)
    return pl.pallas_call(
        project_kernel,
        out_shape=(acc,) * 3,
        grid_spec=grid_of(
            (1,),
            [resident] * 3 + [pl.BlockSpec(memory_space=pl.ANY)],
            (resident,) * 3,
            down_scratch(rows.shape[1], acc.shape[1]),
        ),
        compiler_params=params(20),
        name="project",
    )(place, rows, *weights)


def expert_kernel(place, rows, gate, up, down, in_gate, in_up, in_hidden, theirs, grad_gate, grad_up, acc_gate, acc_up, acc_hidden, down_in, sems):
    side = 1 - place[0]
    accs = (acc_gate, acc_up, acc_hidden)
    project_half(rows, gate, up, down, down_in, sems, side, accs, (in_gate, in_up, in_hidden))
    pre_gate, pre_up, hidden = acc_gate[...], acc_up[...], acc_hidden[...]
    sigma = jax.nn.sigmoid(pre_gate)
    grad_gate[...] = (hidden * pre_up * sigma * (1.0 + pre_gate * (1.0 - sigma))).astype(BF16)
    grad_up[...] = (hidden * pre_gate * sigma).astype(BF16)
    back_rows(place, side, grad_gate, grad_up, gate, up, theirs)


def expert(place, rows, weights, accs):
    height = rows.shape[0]
    acc = accs[0].shape
    grad = jax.ShapeDtypeStruct(acc, BF16)
    resident = pl.BlockSpec(memory_space=pltpu.VMEM)
    return pl.pallas_call(
        expert_kernel,
        out_shape=(jax.ShapeDtypeStruct((height, weights[0].shape[0] // 4), BF16), grad, grad),
        grid_spec=grid_of(
            (1,),
            [resident] * 3 + [pl.BlockSpec(memory_space=pl.ANY)] + [resident] * 3,
            (resident,) * 3,
            [pltpu.VMEM(acc, F32)] * 3 + down_scratch(rows.shape[1], acc[1]),
        ),
        compiler_params=params(24),
        name="expert",
    )(place, rows, *weights, *accs)


def mine_kernel(place, grad_gate, grad_up, gate, up, mine):
    back_rows(place, place[0], grad_gate, grad_up, gate, up, mine)


def mine_rows(place, grads, weights):
    gate, up, _ = weights
    resident = pl.BlockSpec(memory_space=pltpu.VMEM)
    return pl.pallas_call(
        mine_kernel,
        out_shape=jax.ShapeDtypeStruct((2 * grads[0].shape[0], gate.shape[0] // 4), BF16),
        grid_spec=grid_of((1,), [resident] * 4, resident),
        compiler_params=params(16),
        name="mine_rows",
    )(place, *grads, gate, up)


def merge_kernel(mine, other, out):
    out[...] = (mine[...].astype(F32) + other[...].astype(F32)).astype(BF16)


def merge(mine, other):
    rows, columns = mine.shape
    spec = pl.BlockSpec((rows // 4, columns), lambda i: (i, 0))
    return pl.pallas_call(
        merge_kernel,
        out_shape=jax.ShapeDtypeStruct((rows, columns), BF16),
        grid=(4,),
        in_specs=[spec, spec],
        out_specs=spec,
        compiler_params=params(12),
        name="merge",
    )(mine, other)


def sums_kernel(other, place, gather, rows, out):
    count = out.shape[0]
    high = 1 - place[1] if other else place[1]
    mine = pl.ds(pl.multiple_of(high * count, count), count)
    out[...] = jnp.dot(gather[mine, :], rows[...], preferred_element_type=F32).astype(out.dtype)


def token_sums(place, gather, rows, other, kind):
    count = gather.shape[0] // 2
    columns = rows.shape[1]
    resident = pl.BlockSpec(memory_space=pltpu.VMEM)
    return pl.pallas_call(
        functools.partial(sums_kernel, other),
        out_shape=jax.ShapeDtypeStruct((count, columns), kind),
        grid_spec=grid_of((1,), [resident, resident], resident),
        compiler_params=params(16),
        name="token_sums",
    )(place, gather, rows)


def diagonal(count):
    shape = (count, count)
    return lax.broadcasted_iota(jnp.int32, shape, 0) == lax.broadcasted_iota(jnp.int32, shape, 1)


def product_kernel(place, kept, sent, own_tokens, other_tokens, own_gain, other_gain, product):
    part = kept[...] * (own_tokens[...].astype(F32) * own_gain[...])
    part = part + sent[...].astype(F32) * (other_tokens[...].astype(F32) * other_gain[...])
    column = jnp.sum(part, axis=1, keepdims=True)
    row = jnp.sum(jnp.where(diagonal(part.shape[0]), column, 0.0), axis=0, keepdims=True)
    product[...] = jnp.broadcast_to(row, product.shape)


def row_products(place, kept, sent, tokens, gain):
    count, columns = kept.shape

    def quarter(size, other):
        def index(i, place):
            high = 1 - place[1] if other else place[1]
            return (0, 2 * high + place[0])

        return pl.BlockSpec((size, columns), index)

    return pl.pallas_call(
        product_kernel,
        out_shape=jax.ShapeDtypeStruct((8, count), F32),
        grid_spec=grid_of(
            (1,),
            [whole(kept.shape), whole(sent.shape)]
            + [quarter(count, False), quarter(count, True), quarter(1, False), quarter(1, True)],
            whole((8, count)),
        ),
        compiler_params=params(16),
        name="row_products",
    )(place, kept, sent, tokens, tokens, gain, gain)


def final_kernel(place, kept, arrived, own_product, other_product, tokens, cotangent, gain, inverse, out):
    count, columns = out.shape
    own = pl.ds(pl.multiple_of(place[2] * columns, LANES), columns)
    scale = inverse[...]
    row = own_product[:1, :] + other_product[:1, :]
    row_product = jnp.sum(jnp.where(diagonal(count), row, 0.0), axis=1, keepdims=True)
    grad = kept[...] + arrived[...].astype(F32)
    value = cotangent[:, own].astype(F32) + scale * gain[:, own] * grad
    share = scale * scale * scale * row_product / tokens.shape[1]
    out[...] = (value - tokens[:, own].astype(F32) * share).astype(BF16)


def final(place, *arrays):
    count, columns = arrays[0].shape
    resident = pl.BlockSpec(memory_space=pltpu.VMEM)
    return pl.pallas_call(
        final_kernel,
        out_shape=jax.ShapeDtypeStruct((count, columns), BF16),
        grid_spec=grid_of((1,), [resident] * len(arrays), whole((count, columns))),
        compiler_params=params(16),
        name="final",
    )(place, *arrays)


def body(tokens, cotangent, norm_gain, expert_ids, gate_weights, w_gate, w_up, w_down):
    experts = lax.axis_size("expert")
    token_count, width = tokens.shape
    top_count = expert_ids.shape[1]
    capacity = token_count * top_count * 3 // (2 * experts)
    pipe = lax.axis_index("pipe")
    place = jnp.stack([lax.rem(pipe, 2), pipe // 2, pipe]).astype(jnp.int32)
    weights = (w_gate[0], w_up[0], in_hbm(w_down[0]))
    ids = in_hbm(expert_ids.T)
    gain = norm_gain.reshape(1, width)

    rows, inverse = make_message(
        place,
        in_hbm(tokens),
        in_hbm(cotangent),
        in_hbm(gain),
        ids,
        in_hbm(gate_weights.T),
        capacity,
        experts,
    )
    rows, ids = lax.optimization_barrier((exchange(rows), ids))
    accs = project(place, rows, weights)
    swapped, gather = lax.optimization_barrier((core_swap(rows), gather_matrix(ids, capacity, experts)))
    theirs, *grads = expert(place, swapped, weights, accs)
    back = merge(mine_rows(place, grads, weights), core_swap(theirs))
    back = exchange(back)
    sent = token_sums(place, gather, back, True, BF16)
    kept = token_sums(place, gather, back, False, F32)
    product = row_products(place, kept, sent, tokens, gain)
    product = product + core_swap(product)
    return final(
        place, kept, high_swap(sent), product, high_swap(product), tokens, cotangent, gain, inverse
    )


def solution(mesh):
    in_specs = (
        P("expert", None),
        P("expert", None),
        P(),
        P("expert", None),
        P("expert", None),
        P("expert", None, "pipe"),
        P("expert", None, "pipe"),
        P("expert", "pipe", None),
    )
    out_specs = P("expert", "pipe")
    return jax.shard_map(body, mesh=mesh, in_specs=in_specs, out_specs=out_specs, check_vma=False)
```

```python
import functools

import jax
import jax.numpy as jnp
from jax import lax
from jax.experimental import pallas as pl
from jax.experimental.pallas import tpu as pltpu
from jax.sharding import PartitionSpec as P

EPSILON = 1e-06
BF16 = jnp.bfloat16
F32 = jnp.float32
MIB = 1024 * 1024
FILL = 896
DEPTH = 1792
BACK = 896
LANES = 128
LAST = (((1,), (1,)), ((), ()))
CORE_SWAP = [(0, 1), (1, 0), (2, 3), (3, 2)]
HIGH_SWAP = [(0, 2), (2, 0), (1, 3), (3, 1)]


def params(mebibytes):
    return pltpu.CompilerParams(vmem_limit_bytes=mebibytes * MIB)


def in_hbm(array):
    return pltpu.with_memory_space_constraint(array, pltpu.HBM)


def whole(shape):
    return pl.BlockSpec(shape, lambda *_: (0,) * len(shape))


def grid_of(grid, in_specs, out_specs, scratch=()):
    return pltpu.PrefetchScalarGridSpec(
        num_scalar_prefetch=1, grid=grid, in_specs=in_specs, out_specs=out_specs, scratch_shapes=scratch
    )


def core_swap(array):
    return lax.ppermute(array, "pipe", CORE_SWAP)


def high_swap(array):
    return lax.ppermute(array, "pipe", HIGH_SWAP)


def exchange(rows):
    experts = lax.axis_size("expert")
    shaped = rows.reshape(experts, rows.shape[0] // experts, rows.shape[1])
    return lax.all_to_all(shaped, "expert", split_axis=0, concat_axis=0, tiled=True).reshape(rows.shape)


def message_kernel(capacity, place, tokens, cotangent, all_gain, all_ids, all_weights, rows, inverse, tokens_in, cotangent_in, gain, ids, weights, select, factors, sems):
    top, count = ids.shape
    half = rows.shape[1]
    start = place[0] * half
    own_half = pl.ds(pl.multiple_of(start, half), half)
    small = (
        pltpu.make_async_copy(all_ids, ids, sems.at[2]),
        pltpu.make_async_copy(all_weights, weights, sems.at[3]),
        pltpu.make_async_copy(all_gain, gain, sems.at[4]),
    )
    copies = (
        pltpu.make_async_copy(tokens, tokens_in, sems.at[0]),
        pltpu.make_async_copy(cotangent.at[:, own_half], cotangent_in, sems.at[1]),
    )
    for copy in small + copies:
        copy.start()
    for copy in small:
        copy.wait()
    height = select.shape[0]
    experts = height // (2 * capacity)
    expert_of = lax.broadcasted_iota(jnp.int32, (experts, count), 0)
    earlier_of = lax.broadcasted_iota(jnp.int32, (count, count), 0)
    later_of = lax.broadcasted_iota(jnp.int32, (count, count), 1)
    before = (earlier_of < later_of).astype(F32).astype(BF16)
    row = lax.broadcasted_iota(jnp.int32, (height, count), 0)
    taken = jnp.zeros((experts, 1), F32)
    normed_part = jnp.zeros(row.shape, F32)
    routed_part = jnp.zeros(row.shape, F32)
    factor = jnp.zeros(row.shape, F32)
    for k in range(top):
        expert = ids[k : k + 1, :]
        named = (expert_of == expert).astype(F32)
        earlier = jnp.dot(named.astype(BF16), before, preferred_element_type=F32) + taken
        rank = jnp.sum(earlier * named, axis=0, keepdims=True).astype(jnp.int32)
        taken = taken + jnp.sum(named, axis=1, keepdims=True)
        at = expert * (2 * capacity) + rank
        hit = row == at
        hit_routed = row == at + capacity
        normed_part = jnp.where(hit, 1.0, normed_part)
        routed_part = jnp.where(hit_routed, 1.0, routed_part)
        factor = jnp.where(hit, 1.0, jnp.where(hit_routed, weights[k : k + 1, :], factor))
    select[:, :count] = normed_part.astype(BF16)
    select[:, count:] = routed_part.astype(BF16)
    factors[...] = jnp.broadcast_to(jnp.sum(factor, axis=1, keepdims=True), factors.shape)
    copies[0].wait()
    values = tokens_in[...].astype(F32)
    scale = lax.rsqrt(jnp.mean(values * values, axis=1, keepdims=True) + EPSILON)
    inverse[...] = scale
    copies[1].wait()
    for at in range(0, half, FILL):
        own = pl.ds(pl.multiple_of(start + at, LANES), FILL)
        normed = (tokens_in[:, own].astype(F32) * scale * gain[:, own]).astype(BF16)
        both = jnp.concatenate([normed, cotangent_in[:, at : at + FILL]], axis=0)
        picked = jnp.dot(select[...], both, preferred_element_type=F32)
        rows[:, at : at + FILL] = (picked * factors[:, :1]).astype(BF16)


def make_message(place, tokens, cotangent, gain, ids, weights, capacity, experts):
    count, width = tokens.shape
    half = width // 2
    height = experts * 2 * capacity
    any_space = pl.BlockSpec(memory_space=pl.ANY)
    resident = pl.BlockSpec(memory_space=pltpu.VMEM)
    return pl.pallas_call(
        functools.partial(message_kernel, capacity),
        out_shape=(jax.ShapeDtypeStruct((height, half), BF16), jax.ShapeDtypeStruct((count, 1), F32)),
        grid_spec=grid_of(
            (1,),
            [any_space] * 5,
            (resident, resident),
            [
                pltpu.VMEM((count, width), BF16),
                pltpu.VMEM((count, half), BF16),
                pltpu.VMEM(gain.shape, F32),
                pltpu.VMEM(ids.shape, jnp.int32),
                pltpu.VMEM(weights.shape, F32),
                pltpu.VMEM((height, 2 * count), BF16),
                pltpu.VMEM((height, LANES), F32),
                pltpu.SemaphoreType.DMA((5,)),
            ],
        ),
        compiler_params=params(24),
        name="message",
    )(place, tokens, cotangent, gain, ids, weights)


def gather_kernel(capacity, ids, out):
    top, count = ids.shape
    rows = out.shape[1]
    experts = rows // (2 * capacity)
    expert_of = lax.broadcasted_iota(jnp.int32, (experts, count), 0)
    earlier_of = lax.broadcasted_iota(jnp.int32, (count, count), 0)
    later_of = lax.broadcasted_iota(jnp.int32, (count, count), 1)
    before = (earlier_of < later_of).astype(F32).astype(BF16)
    row = lax.broadcasted_iota(jnp.int32, (count, rows), 1).astype(F32)
    taken = jnp.zeros((experts, 1), F32)
    first = jnp.zeros(row.shape, F32)
    second = jnp.zeros(row.shape, F32)
    for k in range(top):
        expert = ids[k : k + 1, :]
        named = (expert_of == expert).astype(F32)
        earlier = jnp.dot(named.astype(BF16), before, preferred_element_type=F32) + taken
        rank = jnp.sum(earlier * named, axis=0, keepdims=True)
        taken = taken + jnp.sum(named, axis=1, keepdims=True)
        at = expert.astype(F32) * (2 * capacity) + rank
        at = jnp.sum(jnp.where(earlier_of == later_of, at, 0.0), axis=1, keepdims=True)
        first = first + (row == at).astype(F32)
        second = second + (row == at + capacity).astype(F32)
    out[:count, :] = first.astype(BF16)
    out[count:, :] = second.astype(BF16)


def gather_matrix(ids, capacity, experts):
    count = ids.shape[1]
    return pl.pallas_call(
        functools.partial(gather_kernel, capacity),
        out_shape=jax.ShapeDtypeStruct((2 * count, experts * 2 * capacity), BF16),
        compiler_params=params(8),
        name="gather_matrix",
    )(ids)


def tiles(x, group):
    return x.reshape(x.shape[0] // (8 * group), group, 8, x.shape[1])


def upper(shape):
    return lax.broadcasted_iota(jnp.int32, shape, 1) < 4


def split_rows(x):
    rows, columns = x.shape
    x = x.astype(F32)
    a, b = tiles(x, 6), tiles(pltpu.roll(x, 4, 0), 6)
    top = upper((rows // 48, 8, columns))
    first = [a[:, 0], jnp.where(top, a[:, 1], b[:, 3]), b[:, 4]]
    second = [b[:, 2], jnp.where(top, b[:, 3], a[:, 4]), a[:, 5]]
    return [
        jnp.concatenate([p[:, None] for p in parts], axis=1).reshape(rows // 2, columns).astype(BF16)
        for parts in (first, second)
    ]


def interleave(x, y):
    rows, columns = x.shape
    x0, x1, x2 = tiles(x, 3), tiles(pltpu.roll(x, 4, 0), 3), tiles(pltpu.roll(x, rows - 4, 0), 3)
    y0, y1 = tiles(y, 3), tiles(pltpu.roll(y, 4, 0), 3)
    shape = (rows // 24, 8, columns)
    parts = [
        x0[:, 0],
        jnp.where(upper(shape), x0[:, 1], y1[:, 0]),
        y1[:, 1],
        x1[:, 2],
        jnp.where(upper(shape), x2[:, 2], y0[:, 1]),
        y0[:, 2],
    ]
    return jnp.concatenate([p[:, None] for p in parts], axis=1).reshape(2 * rows, columns)


def project_half(rows, gate, up, down, down_in, sems, side, accs, bases):
    half = rows.shape[1]
    copies = []
    for i in range(half // DEPTH):
        at = pl.ds(pl.multiple_of(side * half + i * DEPTH, DEPTH), DEPTH)
        to = pl.ds(i * DEPTH, DEPTH)
        copies.append(pltpu.make_async_copy(down.at[:, at], down_in.at[:, to], sems.at[i]))
        copies[i].start()
    for i in range(half // DEPTH):
        at = pl.ds(pl.multiple_of(side * half + i * DEPTH, DEPTH), DEPTH)
        to = slice(i * DEPTH, (i + 1) * DEPTH)
        normed, routed = split_rows(rows[:, to])
        to_gate = jnp.dot(normed, gate[at, :], preferred_element_type=F32)
        to_up = jnp.dot(normed, up[at, :], preferred_element_type=F32)
        copies[i].wait()
        to_hidden = lax.dot_general(routed, down_in[:, to], LAST, preferred_element_type=F32)
        for number, add in enumerate((to_gate, to_up, to_hidden)):
            base = (bases if i == 0 else accs)[number]
            accs[number][...] = add if base is None else base[...] + add


def back_rows(place, side, grad_gate, grad_up, gate, up, out):
    columns = out.shape[1]

    def one(start):
        at = pl.ds(pl.multiple_of(start, LANES), BACK)
        total = lax.dot_general(grad_gate[...], gate[at, :], LAST, preferred_element_type=F32)
        return total + lax.dot_general(grad_up[...], up[at, :], LAST, preferred_element_type=F32)

    for at in range(0, columns, BACK):
        rows = interleave(one(side * columns + at), one((2 + side) * columns + at))
        out[:, at : at + BACK] = rows.astype(BF16)


def down_scratch(half, hidden):
    return [pltpu.VMEM((hidden, half), BF16), pltpu.SemaphoreType.DMA((half // DEPTH,))]


def project_kernel(place, rows, gate, up, down, acc_gate, acc_up, acc_hidden, down_in, sems):
    project_half(rows, gate, up, down, down_in, sems, place[0], (acc_gate, acc_up, acc_hidden), (None,) * 3)


def project(place, rows, weights):
    acc = jax.ShapeDtypeStruct((rows.shape[0] // 2, weights[0].shape[1]), F32)
    resident = pl.BlockSpec(memory_space=pltpu.VMEM)
    return pl.pallas_call(
        project_kernel,
        out_shape=(acc,) * 3,
        grid_spec=grid_of(
            (1,),
            [resident] * 3 + [pl.BlockSpec(memory_space=pl.ANY)],
            (resident,) * 3,
            down_scratch(rows.shape[1], acc.shape[1]),
        ),
        compiler_params=params(20),
        name="project",
    )(place, rows, *weights)


def expert_kernel(place, rows, gate, up, down, in_gate, in_up, in_hidden, theirs, grad_gate, grad_up, acc_gate, acc_up, acc_hidden, down_in, sems):
    side = 1 - place[0]
    accs = (acc_gate, acc_up, acc_hidden)
    project_half(rows, gate, up, down, down_in, sems, side, accs, (in_gate, in_up, in_hidden))
    pre_gate, pre_up, hidden = acc_gate[...], acc_up[...], acc_hidden[...]
    sigma = jax.nn.sigmoid(pre_gate)
    grad_gate[...] = (hidden * pre_up * sigma * (1.0 + pre_gate * (1.0 - sigma))).astype(BF16)
    grad_up[...] = (hidden * pre_gate * sigma).astype(BF16)
    back_rows(place, side, grad_gate, grad_up, gate, up, theirs)


def expert(place, rows, weights, accs):
    height = rows.shape[0]
    acc = accs[0].shape
    grad = jax.ShapeDtypeStruct(acc, BF16)
    resident = pl.BlockSpec(memory_space=pltpu.VMEM)
    return pl.pallas_call(
        expert_kernel,
        out_shape=(jax.ShapeDtypeStruct((height, weights[0].shape[0] // 4), BF16), grad, grad),
        grid_spec=grid_of(
            (1,),
            [resident] * 3 + [pl.BlockSpec(memory_space=pl.ANY)] + [resident] * 3,
            (resident,) * 3,
            [pltpu.VMEM(acc, F32)] * 3 + down_scratch(rows.shape[1], acc[1]),
        ),
        compiler_params=params(24),
        name="expert",
    )(place, rows, *weights, *accs)


def mine_kernel(place, grad_gate, grad_up, gate, up, mine):
    back_rows(place, place[0], grad_gate, grad_up, gate, up, mine)


def mine_rows(place, grads, weights):
    gate, up, _ = weights
    resident = pl.BlockSpec(memory_space=pltpu.VMEM)
    return pl.pallas_call(
        mine_kernel,
        out_shape=jax.ShapeDtypeStruct((2 * grads[0].shape[0], gate.shape[0] // 4), BF16),
        grid_spec=grid_of((1,), [resident] * 4, resident),
        compiler_params=params(16),
        name="mine_rows",
    )(place, *grads, gate, up)


def merge_kernel(mine, other, out):
    out[...] = (mine[...].astype(F32) + other[...].astype(F32)).astype(BF16)


def merge(mine, other):
    resident = pl.BlockSpec(memory_space=pltpu.VMEM)
    return pl.pallas_call(
        merge_kernel,
        out_shape=jax.ShapeDtypeStruct(mine.shape, BF16),
        in_specs=[resident, resident],
        out_specs=resident,
        compiler_params=params(12),
        name="merge",
    )(mine, other)


def sums_kernel(other, place, gather, rows, out):
    count = out.shape[0]
    high = 1 - place[1] if other else place[1]
    mine = pl.ds(pl.multiple_of(high * count, count), count)
    out[...] = jnp.dot(gather[mine, :], rows[...], preferred_element_type=F32).astype(out.dtype)


def token_sums(place, gather, rows, other, kind):
    count = gather.shape[0] // 2
    columns = rows.shape[1]
    resident = pl.BlockSpec(memory_space=pltpu.VMEM)
    return pl.pallas_call(
        functools.partial(sums_kernel, other),
        out_shape=jax.ShapeDtypeStruct((count, columns), kind),
        grid_spec=grid_of((1,), [resident, resident], resident),
        compiler_params=params(16),
        name="token_sums",
    )(place, gather, rows)


def diagonal(count):
    shape = (count, count)
    return lax.broadcasted_iota(jnp.int32, shape, 0) == lax.broadcasted_iota(jnp.int32, shape, 1)


def product_kernel(place, kept, sent, own_tokens, other_tokens, own_gain, other_gain, product):
    part = kept[...] * (own_tokens[...].astype(F32) * own_gain[...])
    part = part + sent[...].astype(F32) * (other_tokens[...].astype(F32) * other_gain[...])
    column = jnp.sum(part, axis=1, keepdims=True)
    row = jnp.sum(jnp.where(diagonal(part.shape[0]), column, 0.0), axis=0, keepdims=True)
    product[...] = jnp.broadcast_to(row, product.shape)


def row_products(place, kept, sent, tokens, gain):
    count, columns = kept.shape

    def quarter(size, other):
        def index(i, place):
            high = 1 - place[1] if other else place[1]
            return (0, 2 * high + place[0])

        return pl.BlockSpec((size, columns), index)

    return pl.pallas_call(
        product_kernel,
        out_shape=jax.ShapeDtypeStruct((8, count), F32),
        grid_spec=grid_of(
            (1,),
            [whole(kept.shape), whole(sent.shape)]
            + [quarter(count, False), quarter(count, True), quarter(1, False), quarter(1, True)],
            whole((8, count)),
        ),
        compiler_params=params(16),
        name="row_products",
    )(place, kept, sent, tokens, tokens, gain, gain)


def final_kernel(place, kept, arrived, own_product, other_product, tokens, cotangent, gain, inverse, out, result, sems):
    count, columns = out.shape
    half = columns // 2
    scale = inverse[...]
    row = own_product[:1, :] + other_product[:1, :]
    row_product = jnp.sum(jnp.where(diagonal(count), row, 0.0), axis=1, keepdims=True)
    share = scale * scale * scale * row_product / tokens.shape[1]
    copies = []
    for number in range(2):
        part = slice(number * half, (number + 1) * half)
        own = pl.ds(pl.multiple_of(place[2] * columns + number * half, LANES), half)
        grad = kept[:, part] + arrived[:, part].astype(F32)
        value = cotangent[:, own].astype(F32) + scale * gain[:, own] * grad
        result[:, part] = (value - tokens[:, own].astype(F32) * share).astype(BF16)
        copies.append(pltpu.make_async_copy(result.at[:, part], out.at[:, part], sems.at[number]))
        copies[number].start()
    for copy in copies:
        copy.wait()


def final(place, *arrays):
    count, columns = arrays[0].shape
    resident = pl.BlockSpec(memory_space=pltpu.VMEM)
    return pl.pallas_call(
        final_kernel,
        out_shape=jax.ShapeDtypeStruct((count, columns), BF16),
        grid_spec=grid_of(
            (1,),
            [resident] * len(arrays),
            pl.BlockSpec(memory_space=pl.ANY),
            [pltpu.VMEM((count, columns), BF16), pltpu.SemaphoreType.DMA((2,))],
        ),
        compiler_params=params(16),
        name="final",
    )(place, *arrays)


def body(tokens, cotangent, norm_gain, expert_ids, gate_weights, w_gate, w_up, w_down):
    experts = lax.axis_size("expert")
    token_count, width = tokens.shape
    top_count = expert_ids.shape[1]
    capacity = token_count * top_count * 3 // (2 * experts)
    pipe = lax.axis_index("pipe")
    place = jnp.stack([lax.rem(pipe, 2), pipe // 2, pipe]).astype(jnp.int32)
    weights = (w_gate[0], w_up[0], in_hbm(w_down[0]))
    ids = in_hbm(expert_ids.T)
    gain = norm_gain.reshape(1, width)

    rows, inverse = make_message(
        place,
        in_hbm(tokens),
        in_hbm(cotangent),
        in_hbm(gain),
        ids,
        in_hbm(gate_weights.T),
        capacity,
        experts,
    )
    rows, ids = lax.optimization_barrier((exchange(rows), ids))
    accs = project(place, rows, weights)
    swapped, gather = lax.optimization_barrier((core_swap(rows), gather_matrix(ids, capacity, experts)))
    theirs, *grads = expert(place, swapped, weights, accs)
    back = merge(mine_rows(place, grads, weights), core_swap(theirs))
    back = exchange(back)
    sent = token_sums(place, gather, back, True, BF16)
    kept = token_sums(place, gather, back, False, F32)
    product = row_products(place, kept, sent, tokens, gain)
    product = product + core_swap(product)
    return final(
        place, kept, high_swap(sent), product, high_swap(product), tokens, cotangent, gain, inverse
    )


def solution(mesh):
    in_specs = (
        P("expert", None),
        P("expert", None),
        P(),
        P("expert", None),
        P("expert", None),
        P("expert", None, "pipe"),
        P("expert", None, "pipe"),
        P("expert", "pipe", None),
    )
    out_specs = P("expert", "pipe")
    return jax.shard_map(body, mesh=mesh, in_specs=in_specs, out_specs=out_specs, check_vma=False)
```
